32 devices in a mesh: dp: 4 (over x, core), row: 2 (over y), col: 4 (over z).
Axes of the slice: x: 2, y: 2, z: 4, core: 2. Of those that a mesh axis runs over, the one named last changes fastest.
Arguments:
- tokens: bfloat16 [8192, 1024], P(('dp', 'col'), 'row'), may hold values from -6 to 6
- segments: int32 [8192], P('dp'), may hold values from 0 to 17, as said below
- triple_weight: bfloat16 [1024, 3, 1024], P('row', None, 'col'), may hold values from -0.25 to 0.25
- pair_bias: bfloat16 [2, 1024], P(None, 'col'), may hold values from -3 to 3
- merge_weight: bfloat16 [1024, 1024], P('col', 'row'), may hold values from -1.5 to 1.5
- merge_bias: bfloat16 [1024], P('row'), may hold values from -2 to 2
- first_gain: bfloat16 [1024], P('row'), may hold values from 0.5 to 1.5
- first_shift: bfloat16 [1024], P('row'), may hold values from -3 to 3
- expand_weight: bfloat16 [1024, 4096], P('row', 'col'), may hold values from -0.1875 to 0.1875
- expand_bias: bfloat16 [4096], P('col'), may hold values from -3 to 3
- shrink_weight: bfloat16 [4096, 1024], P('col', 'row'), may hold values from -0.09375 to 0.09375
- shrink_bias: bfloat16 [1024], P('row'), may hold values from -2 to 2
- second_gain: bfloat16 [1024], P('row'), may hold values from 0.5 to 1.5
- second_shift: bfloat16 [1024], P('row'), may hold values from -3 to 3
- cotangent: bfloat16 [8192, 1024], P(('dp', 'col'), 'row'), may hold values from -6 to 6
Outputs:
- layer_out: bfloat16 [8192, 1024], P(('dp', 'col'), 'row')
- grad_tokens: float32 [8192, 1024], P(('dp', 'col'), 'row')
- grad_triple: float32 [1024, 3, 1024], P('row', None, 'col')
- grad_pair: float32 [2, 1024], P(None, 'col')
- grad_merge: float32 [1024, 1024], P('col', 'row')
- grad_merge_bias: float32 [1024], P('row')
- grad_first_gain: float32 [1024], P('row')
- grad_first_shift: float32 [1024], P('row')
- grad_expand: float32 [1024, 4096], P('row', 'col')
- grad_expand_bias: float32 [4096], P('col')
- grad_shrink: float32 [4096, 1024], P('col', 'row')
- grad_shrink_bias: float32 [1024], P('row')
- grad_second_gain: float32 [1024], P('row')
- grad_second_shift: float32 [1024], P('row')
The draws below stay inside these ranges and needn't reach their ends.
Inputs may be any that keep to these rules, and one draw needn't show every extreme that they name: `segments`: within each sequence of 1024 consecutive tokens the numbers are 1, 2, 3, ... over whole documents of 60 to 800 tokens, followed by 0 on a trailing pad of fewer than 800 tokens; some document holds exactly 800 tokens.
All inputs are finite; a program needn't handle non-finite values.
Results may differ from the reference program's by a relative error of at most 0.017.
The reference program's roundings to bfloat16 on the way count: a program that leaves them out, or rounds other values in their place, can miss the bound.
Values may be sent and summed in bfloat16 or wider, within the bound.
No kernel may reach another device: no remote copies, remote signals or barrier semaphores. Data moves between devices by JAX's collectives and lax.ppermute only.
A program may use at most 192 MiB of HBM per device.

```python
import jax
import jax.numpy as jnp
from jax import lax

D = 1024
HEADS = 16
HEAD = 64
FF = 4096
LEN = 1024
DOC_MIN = 60
DOC_MAX = 800
TOKENS = 8192


def draw_segments(key, part):
    key = jax.random.fold_in(key, 11)
    seq_count = TOKENS // LEN
    slot_count = LEN // DOC_MIN + 1
    doc_sizes = jax.random.randint(jax.random.fold_in(key, 1), (seq_count, slot_count), DOC_MIN, DOC_MAX + 1)
    chosen = jax.random.randint(jax.random.fold_in(key, 2), (), 0, seq_count)
    packed = (chosen + 1) % seq_count
    is_chosen = jnp.arange(seq_count) == chosen
    is_packed = jnp.arange(seq_count) == packed
    slots = jnp.arange(slot_count)
    packed_sizes = jnp.where(slots == (LEN - 1) // DOC_MIN, DOC_MAX, DOC_MIN)
    doc_sizes = jnp.where(is_packed[:, None], packed_sizes[None, :], doc_sizes)
    doc_sizes = doc_sizes.at[:, 0].set(jnp.where(is_chosen, DOC_MAX, doc_sizes[:, 0]))
    doc_ends = jnp.cumsum(doc_sizes, axis=1)
    positions = jnp.arange(LEN)
    doc_index = jnp.sum((doc_ends[:, None, :] <= positions[None, :, None]).astype(jnp.int32), axis=-1)
    doc_stop = jnp.take_along_axis(doc_ends, doc_index, axis=1)
    segment = jnp.where(doc_stop <= LEN, doc_index + 1, 0)
    return segment.reshape(-1).astype(jnp.int32)


def block_levels(own_key, dims, pieces, low, top_value):
    def one(position, blocks):
        steps = jax.random.uniform(jax.random.fold_in(jax.random.fold_in(own_key, 6), position), (blocks,), jnp.float32, low / len(pieces), top_value / len(pieces))
        return jnp.repeat(jnp.exp(steps), dims[position] // blocks).reshape((-1,) + (1,) * (len(dims) - position - 1))

    loudness = one(*pieces[0])
    for cut in pieces[1:]:
        loudness = loudness * one(*cut)
    return loudness


def gaussian(rng, extent, spread, bound, shards=(), kind=jnp.bfloat16):
    gain = block_levels(rng, extent, shards, -0.22, 0.18) if shards else 1.0
    values = jax.random.normal(rng, extent, jnp.float32) * spread * gain
    return jnp.minimum(jnp.maximum(values, -bound), bound).astype(kind)


def setup_inputs(seed: int = 0) -> dict:
    arg_keys = jax.random.split(jax.random.key(seed), 16)
    tokens = gaussian(arg_keys[0], (TOKENS, D), 1.0, 6.0, ((0, 16), (1, 2)))
    segments = draw_segments(jax.random.fold_in(arg_keys[15], 71), 0)
    triple_weight = gaussian(arg_keys[2], (D, 3, D), (D // 2) ** -0.5, 0.25, ((0, 2), (2, 4)))
    pair_bias = gaussian(arg_keys[3], (2, D), 0.5, 3.0, ((1, 4),))
    merge_weight = gaussian(arg_keys[4], (D, D), (D // 64) ** -0.5, 1.5, ((0, 4), (1, 2)))
    merge_bias = gaussian(arg_keys[5], (D,), 0.3, 2.0, ((0, 2),))
    first_gain = jnp.clip(1.0 + 0.1 * jax.random.normal(arg_keys[6], (D,), jnp.float32), 0.5, 1.5).astype(jnp.bfloat16)
    first_shift = gaussian(arg_keys[7], (D,), 0.5, 3.0, ((0, 2),))
    expand_weight = gaussian(arg_keys[8], (D, FF), D ** -0.5, 0.1875, ((0, 2), (1, 4)))
    expand_bias = gaussian(arg_keys[9], (FF,), 0.5, 3.0, ((0, 4),))
    shrink_weight = gaussian(arg_keys[10], (FF, D), FF ** -0.5, 0.09375, ((0, 4), (1, 2)))
    shrink_bias = gaussian(arg_keys[11], (D,), 0.3, 2.0, ((0, 2),))
    second_gain = jnp.clip(1.0 + 0.1 * jax.random.normal(arg_keys[12], (D,), jnp.float32), 0.5, 1.5).astype(jnp.bfloat16)
    second_shift = gaussian(arg_keys[13], (D,), 0.5, 3.0, ((0, 2),))
    cotangent = gaussian(arg_keys[14], (TOKENS, D), 1.0, 6.0, ((0, 16), (1, 2)))
    return dict(tokens=tokens, segments=segments, triple_weight=triple_weight, pair_bias=pair_bias, merge_weight=merge_weight, merge_bias=merge_bias, first_gain=first_gain, first_shift=first_shift, expand_weight=expand_weight, expand_bias=expand_bias, shrink_weight=shrink_weight, shrink_bias=shrink_bias, second_gain=second_gain, second_shift=second_shift, cotangent=cotangent)


@jax.custom_vjp
def low(v):
    return lax.optimization_barrier(v.astype(jnp.bfloat16)).astype(jnp.float32)

@jax.custom_vjp
def low_back(v):
    return v

def low_keep(v):
    return (low(v), None)

def low_pass(kept, grad):
    return (grad,)

def back_keep(v):
    return (v, None)

def back_low(kept, grad):
    return (low(grad),)
low.defvjp(low_keep, low_pass)
low_back.defvjp(back_keep, back_low)
epsilon = 1e-05
masked_score = -1e+30
highest = lax.Precision.HIGHEST

def layer_norm(values, gain_row, shift_row):
    center = lax.optimization_barrier(jnp.mean(values, axis=-1, keepdims=True))
    square = lax.optimization_barrier(jnp.mean(values * values, axis=-1, keepdims=True))
    scaled = (values - center) * lax.rsqrt(square - center * center + epsilon)
    return scaled * gain_row + shift_row

def attend(queries, key_rows, value_rows, segment):
    scores = jnp.einsum('qhd,khd->hqk', queries, key_rows, precision=highest) * HEAD ** (-0.5)
    scores = low_back(scores)
    same_doc = segment[:, None] == segment[None, :]
    scores = jnp.where(same_doc[None], scores, masked_score)
    weights = jax.nn.softmax(scores, axis=-1)
    return jnp.einsum('hqk,khd->qhd', low(weights), value_rows, precision=highest)

def forward(params, rows_in, segment):
    triple, pair_vec, merge_matrix, merge_vec, gain_one, shift_one, expand_matrix, expand_vec, shrink_matrix, shrink_vec, gain_two, shift_two = params
    projected = jnp.dot(rows_in, triple.reshape(D, 3 * D), precision=highest).reshape(LEN, 3, D)
    queries = low_back(low(projected[:, 0] + pair_vec[0]))
    key_rows = low_back(low(projected[:, 1]))
    value_rows = low_back(low(projected[:, 2] + pair_vec[1]))
    head_shape = (LEN, HEADS, HEAD)
    attended = attend(queries.reshape(head_shape), key_rows.reshape(head_shape), value_rows.reshape(head_shape), segment).reshape(LEN, D)
    attended = low_back(low(attended))
    branch = low_back(jnp.dot(attended, merge_matrix, precision=highest) + merge_vec)
    normed_one = layer_norm(rows_in + branch, gain_one, shift_one)
    pre_gelu = low_back(jnp.dot(low(normed_one), expand_matrix, precision=highest) + expand_vec)
    hidden = low(jax.nn.gelu(pre_gelu, approximate=False))
    shrunk = low_back(jnp.dot(hidden, shrink_matrix, precision=highest) + shrink_vec)
    return layer_norm(normed_one + shrunk, gain_two, shift_two)

def reference(tokens, segments, triple_weight, pair_bias, merge_weight, merge_bias, first_gain, first_shift, expand_weight, expand_bias, shrink_weight, shrink_bias, second_gain, second_shift, cotangent):
    params = tuple((member.astype(jnp.float32) for member in (triple_weight, pair_bias, merge_weight, merge_bias, first_gain, first_shift, expand_weight, expand_bias, shrink_weight, shrink_bias, second_gain, second_shift)))
    seq_count = tokens.shape[0] // LEN
    stacked = (tokens.astype(jnp.float32).reshape(seq_count, LEN, D), segments.reshape(seq_count, LEN), cotangent.astype(jnp.float32).reshape(seq_count, LEN, D))

    def advance(totals, member):
        rows_in, segment, upstream = member

        def run_block(weights, inputs):
            return forward(weights, inputs, segment)
        result, pullback = jax.vjp(run_block, params, rows_in)
        live_mask = (segment != 0).astype(result.dtype)[:, None]
        weight_grads, grad_rows = pullback(upstream * live_mask)
        return (jax.tree.map(jnp.add, totals, weight_grads), (result.astype(jnp.bfloat16), grad_rows))
    initial = jax.tree.map(jnp.zeros_like, params)
    totals, (outputs, grad_rows) = lax.scan(advance, initial, stacked)
    return (outputs.reshape(-1, D), grad_rows.reshape(-1, D), totals[0], totals[1], totals[2], totals[3], totals[4], totals[5], totals[6], totals[7], totals[8], totals[9], totals[10], totals[11])
```

```python
import jax
import jax.numpy as jnp
from jax import lax
from jax.sharding import Mesh, PartitionSpec as P

D = 1024
HEAD = 64
LEN = 1024
epsilon = 1e-05
masked_score = -1e30
bf16 = jnp.bfloat16
f32 = jnp.float32


def size(axis):
    return lax.axis_size(axis)


def place(axis):
    return lax.axis_index(axis)


def pair(values, axis):
    return lax.ppermute(values, axis, [(0, 1), (1, 0)])


def by_place(bit, own, other, axis):
    return jnp.where(
        bit == 0,
        jnp.concatenate((own, other), axis),
        jnp.concatenate((other, own), axis),
    )


def nt(left, right, kind=f32):
    return lax.dot_general(
        left, right, (((1,), (1,)), ((), ())), preferred_element_type=f32
    ).astype(kind)


def nn(left, right, kind=f32):
    return lax.dot_general(
        left, right, (((1,), (0,)), ((), ())), preferred_element_type=f32
    ).astype(kind)


def tn(left, right, kind=f32):
    return lax.dot_general(
        left, right, (((0,), (0,)), ((), ())), preferred_element_type=f32
    ).astype(kind)


def swap_sequences(values):
    count = size("col")
    perm = []
    for core in range(2):
        for col in range(count):
            half, other = col % 2, col - col % 2
            target = (half, other + core)
            perm.append((core * count + col, target[0] * count + target[1]))
    return lax.ppermute(values, ("core", "col"), perm)


def own_first(values):
    if size("row") != 2:
        return values
    half = values.shape[0] // 2
    return jnp.where(place("row") == 0, values, jnp.roll(values, half, axis=0))


def own_part(values):
    share = values.shape[0] // size("row")
    if size("row") == 2:
        return values[:share]
    return lax.dynamic_slice_in_dim(values, place("row") * share, share)


def gather_features(values):
    if size("row") == 2:
        full = by_place(place("row"), values, pair(values, "row"), 1)
        return own_first(full)
    return lax.all_gather(values, "row", axis=1, tiled=True)


def gather_tokens(values):
    if size("row") == 2:
        return jnp.concatenate((values, pair(values, "row")), 0)
    return lax.all_gather(values, "row", axis=0, tiled=True)


def sum_tokens(partial):
    if size("row") == 2:
        share = partial.shape[0] // 2
        return partial[:share] + pair(partial[share:].astype(bf16), "row").astype(f32)
    return lax.psum_scatter(partial, "row", scatter_dimension=0, tiled=True)


def to_own_tokens(values):
    if size("row") == 2:
        bit = place("row")
        ordered = own_first(values)
        share = values.shape[0] // 2
        return by_place(bit, ordered[:share], pair(ordered[share:], "row"), 1)
    return lax.all_to_all(values, "row", 0, 1, tiled=True)


def to_own_features(values):
    if size("row") == 2:
        bit = place("row")
        half = values.shape[1] // 2
        low, high = values[:, :half], values[:, half:]
        own = jnp.where(bit == 0, low, high)
        other = pair(jnp.where(bit == 0, high, low), "row")
        return by_place(bit, own, other, 0)
    return lax.all_to_all(values, "row", 1, 0, tiled=True)


def three_groups(triple, merge, expand, shrink):
    depth = triple.shape[0]
    heads = triple.transpose(1, 2, 0).reshape(3, 2, 2, 1, HEAD, depth)
    out = merge.reshape(1, 2, 2, 1, HEAD, depth)
    keys_values = jnp.concatenate((heads[1], heads[2]), 3 - 1)
    queries_merge = jnp.concatenate((heads[0], out[0]), 3 - 1)
    attend = jnp.stack((keys_values, queries_merge), 2).reshape(2, 2, 2, 2 * HEAD, depth)
    widen = expand.T.reshape(2, 2, 2, -1, depth)
    narrow = shrink.reshape(2, 2, 2, -1, depth)
    return attend, widen, narrow


def my_quarter(group):
    some = lax.dynamic_index_in_dim(group, place("outer"), 1, keepdims=False)
    return lax.dynamic_index_in_dim(some, place("core"), 1, keepdims=False)


def exchange_rows(quarter):
    bit = place("row")
    mine = jnp.where(bit == 0, quarter[0], quarter[1])
    other = pair(jnp.where(bit == 0, quarter[1], quarter[0]), "row")
    return by_place(bit, mine, other, 1)


def spread(quarter):
    count = size("col")
    parts = [quarter] + [
        lax.ppermute(quarter, "col", [(i, (i + step) % count) for i in range(count)])
        for step in range(1, count)
    ]
    four = jnp.stack(parts)
    eight = jnp.stack((four, pair(four, "outer")))
    return jnp.stack((eight, pair(eight, "core")))


def collect(own, other):
    count = size("col")
    bit = place("row")
    total = own + pair(other.astype(bf16), "core").astype(f32)
    total = total[0] + pair(total[1].astype(bf16), "outer").astype(f32)
    last = total[0]
    for step in range(1, count):
        last = last + lax.ppermute(
            total[step].astype(bf16), "col", [(i, (i - step) % count) for i in range(count)]
        ).astype(f32)
    half = last.shape[1] // 2
    low, high = last[:, :half].astype(bf16), last[:, half:].astype(bf16)
    mine = jnp.where(bit == 0, low, high)
    got = pair(jnp.where(bit == 0, high, low), "row")
    block = jnp.stack((jnp.where(bit == 0, mine, got), jnp.where(bit == 0, got, mine)))
    block = by_place(place("core"), block[:, None], pair(block, "core")[:, None], 1)
    block = by_place(place("outer"), block[:, None], pair(block, "outer")[:, None], 1)
    return block.astype(f32)


def ungroup(attend, widen, narrow):
    depth = attend.shape[-1]
    heads = attend.reshape(4, 2, 2, HEAD, depth)
    keys, values = heads[:, 0, 0], heads[:, 0, 1]
    queries, merge = heads[:, 1, 0], heads[:, 1, 1]
    triple = jnp.stack((queries, keys, values)).reshape(3, 4 * HEAD, depth).transpose(2, 0, 1)
    return (
        triple,
        merge.reshape(4 * HEAD, depth),
        widen.reshape(-1, depth).T,
        narrow.reshape(-1, depth),
    )


def local_order(full, units):
    count = size("col")
    rows = full.reshape(count, 2, 2, 2, units)
    rows = lax.dynamic_index_in_dim(rows, place("row"), 1, keepdims=False)
    rows = jnp.where(place("outer") == 0, rows, rows[:, ::-1])
    rows = jnp.where(place("core") == 0, rows, rows[:, :, ::-1])
    steps = [
        lax.dynamic_index_in_dim(rows, (place("col") - step) % count, 0, keepdims=False)
        for step in range(count)
    ]
    return jnp.stack(steps).transpose(2, 1, 0, 3)


def global_order(local, units):
    count = size("col")
    rows = local.reshape(2, 2, count, units).transpose(2, 1, 0, 3)
    rows = jnp.where(place("core") == 0, rows, rows[:, :, ::-1])
    rows = jnp.where(place("outer") == 0, rows, rows[:, ::-1])
    full = jnp.zeros((count, 2, 2, 2, units), local.dtype)
    for step in range(count):
        full = lax.dynamic_update_slice(
            full,
            rows[step][None, None],
            ((place("col") - step) % count, place("row"), 0, 0, 0),
        )
    return full.reshape(-1)


def masked(scores, query_segment, key_segment):
    same = query_segment[:, None] == key_segment[None, :]
    return jnp.where(same[None], scores, masked_score)


def attention_forward(queries, keys, values, query_segment, key_segment):
    scores = jnp.einsum("qhd,khd->hqk", queries, keys, preferred_element_type=f32)
    scores = masked(scores * HEAD**-0.5, query_segment, key_segment)
    top = jnp.max(scores, axis=-1, keepdims=True)
    weights = jnp.exp(scores - top)
    total = jnp.sum(weights, axis=-1, keepdims=True)
    low = (weights / total).astype(bf16)
    attended = jnp.einsum("hqk,khd->qhd", low, values, preferred_element_type=f32)
    return attended.astype(bf16), top + jnp.log(total)


def attention_backward(queries, keys, values, query_segment, key_segment, lse, grad):
    scores = jnp.einsum("qhd,khd->hqk", queries, keys, preferred_element_type=f32)
    scores = masked(scores * HEAD**-0.5, query_segment, key_segment)
    weights = jnp.exp(scores - lse)
    grad_weights = jnp.einsum("qhd,khd->hqk", grad, values, preferred_element_type=f32)
    inner = jnp.sum(weights * grad_weights, axis=-1, keepdims=True)
    grad_scores = (weights * (grad_weights - inner)).astype(bf16)
    scale = HEAD**-0.5
    grad_queries = jnp.einsum("hqk,khd->qhd", grad_scores, keys, preferred_element_type=f32) * scale
    grad_keys = jnp.einsum("hqk,qhd->khd", grad_scores, queries, preferred_element_type=f32) * scale
    grad_values = jnp.einsum(
        "hqk,qhd->khd", weights.astype(bf16), grad, preferred_element_type=f32
    )
    return grad_queries.astype(bf16), grad_keys, grad_values


def norm_forward(values, gain, shift):
    center = jnp.mean(values, axis=1, keepdims=True)
    inverse = lax.rsqrt(
        jnp.mean(values * values, axis=1, keepdims=True) - center * center + epsilon
    )
    scaled = (values - center) * inverse
    return scaled, inverse, scaled * gain + shift


def norm_backward(upstream, scaled, inverse, gain):
    through = upstream * gain
    grad = inverse * (
        through
        - jnp.mean(through, axis=1, keepdims=True)
        - scaled * jnp.mean(through * scaled, axis=1, keepdims=True)
    )
    return grad, jnp.sum(upstream * scaled, axis=0), jnp.sum(upstream, axis=0)


def exact_gelu(values):
    return jax.nn.gelu(values, approximate=False)


def shards(
    tokens,
    segments,
    triple_weight,
    pair_bias,
    merge_weight,
    merge_bias,
    first_gain,
    first_shift,
    expand_weight,
    expand_bias,
    shrink_weight,
    shrink_bias,
    second_gain,
    second_shift,
    cotangent,
):
    rows, cols = size("row"), size("col")
    count = tokens.shape[0]
    span = LEN // count
    special = rows == 2 and span == 2
    own = count // rows
    heads = D // HEAD // rows
    row, col, core = place("row"), place("col"), place("core")

    packed = jnp.concatenate(
        (
            pair_bias.reshape(-1),
            expand_bias,
            merge_bias,
            first_gain,
            first_shift,
            shrink_bias,
            second_gain,
            second_shift,
        )
    )
    everyone = lax.all_gather(packed, ("row", "col"), axis=0).reshape(rows, cols, -1)
    pair_size, hidden_size, row_size = pair_bias.shape[1], expand_bias.shape[0], merge_bias.shape[0]
    begin = 2 * pair_size + hidden_size
    pair_full = everyone[0, :, : 2 * pair_size].reshape(cols, 2, pair_size)
    query_bias, value_bias = pair_full[:, 0].reshape(-1), pair_full[:, 1].reshape(-1)
    hidden_bias = everyone[0, :, 2 * pair_size : begin].reshape(-1)
    vectors = everyone[:, 0, begin:].reshape(rows, 6, row_size).transpose(1, 0, 2).reshape(6, D)
    vectors = vectors.astype(f32)

    if special:
        half = col % 2
        other = pair(segments.astype(f32), "core").astype(jnp.int32)
        mine = jnp.where(half == core, segments, other)
        sequence = lax.dynamic_slice_in_dim(mine, (col // 2) * LEN, LEN).reshape(2, count)
        query_segment = lax.dynamic_index_in_dim(sequence, core, 0, keepdims=False)
        far_segment = lax.dynamic_index_in_dim(sequence, 1 - core, 0, keepdims=False)
        query_segment = own_first(query_segment)
        key_segment = jnp.concatenate((query_segment, own_first(far_segment)))
        tokens, cotangent = swap_sequences(tokens), swap_sequences(cotangent)
    else:
        query_segment = lax.dynamic_slice_in_dim(segments, col * count, count)
        key_segment = query_segment

    if special:
        groups = [
            spread(exchange_rows(my_quarter(group)))
            for group in three_groups(triple_weight, merge_weight, expand_weight, shrink_weight)
        ]
        attend_group = groups[0]
        first = jnp.where(core == 0, attend_group[0], attend_group[1])
        second = jnp.where(core == 0, attend_group[1], attend_group[0])
        first = first.reshape(heads, 2, HEAD, D)
        second = second.reshape(heads, 2, HEAD, D)
        weight_keys, weight_values = first[:, 0].reshape(-1, D), first[:, 1].reshape(-1, D)
        weight_queries, weight_merge = second[:, 0].reshape(-1, D), second[:, 1].reshape(-1, D)
        weight_expand, weight_shrink = groups[1].reshape(-1, D), groups[2].reshape(-1, D)
        bias_hidden = local_order(hidden_bias, hidden_size // 8).reshape(-1).astype(f32)

        def heads_order(vector):
            blocks = vector.reshape(cols, 2, 2, HEAD)
            blocks = lax.dynamic_index_in_dim(blocks, row, 1, keepdims=False)
            blocks = jnp.where(place("outer") == 0, blocks, blocks[:, ::-1])
            steps = [
                lax.dynamic_index_in_dim(blocks, (col - step) % cols, 0, keepdims=False)
                for step in range(cols)
            ]
            return jnp.stack(steps).transpose(1, 0, 2).reshape(-1)

        bias_queries, bias_values = heads_order(query_bias), heads_order(value_bias)
    else:
        triple = lax.all_gather(triple_weight, "col", axis=2, tiled=True)
        triple = lax.all_gather(triple, "row", axis=0, tiled=True).transpose(1, 2, 0)
        merge = lax.all_gather(merge_weight, "col", axis=0, tiled=True)
        merge = lax.all_gather(merge, "row", axis=1, tiled=True)
        expand = lax.all_gather(expand_weight, "col", axis=1, tiled=True)
        expand = lax.all_gather(expand, "row", axis=0, tiled=True).T
        shrink = lax.all_gather(shrink_weight, "col", axis=0, tiled=True)
        shrink = lax.all_gather(shrink, "row", axis=1, tiled=True)

        def mine_of(full):
            return lax.dynamic_slice_in_dim(full, row * (full.shape[0] // rows), full.shape[0] // rows)

        weight_queries, weight_keys, weight_values = (mine_of(triple[j]) for j in range(3))
        weight_merge, weight_expand, weight_shrink = mine_of(merge), mine_of(expand), mine_of(shrink)
        bias_hidden = mine_of(hidden_bias).astype(f32)
        bias_queries, bias_values = mine_of(query_bias), mine_of(value_bias)

    inputs = gather_features(tokens)
    head_shape = (-1, heads, HEAD)
    queries = (nt(inputs, weight_queries) + bias_queries.astype(f32)).astype(bf16)
    keys = nt(inputs, weight_keys).astype(bf16)
    values = (nt(inputs, weight_values) + bias_values.astype(f32)).astype(bf16)
    if special:
        keys_values = jnp.concatenate((keys, values), 1)
        all_keys_values = jnp.concatenate((keys_values, pair(keys_values, "core")), 0)
        all_keys = all_keys_values[:, : heads * HEAD]
        all_values = all_keys_values[:, heads * HEAD :]
    else:
        all_keys, all_values = keys, values
    queries_heads = queries.reshape(head_shape)
    keys_heads, values_heads = all_keys.reshape(head_shape), all_values.reshape(head_shape)
    attended, lse = attention_forward(
        queries_heads, keys_heads, values_heads, query_segment, key_segment
    )
    attended = attended.reshape(count, -1)
    branch = sum_tokens(nn(attended, weight_merge))
    residual = own_part(inputs).astype(f32) + (branch + vectors[0])
    scaled_one, inverse_one, normed_one = norm_forward(residual, vectors[1], vectors[2])
    normed_low = gather_tokens(normed_one.astype(bf16))
    pre_gelu = nt(normed_low, weight_expand) + bias_hidden
    hidden = exact_gelu(pre_gelu).astype(bf16)
    shrunk = sum_tokens(nn(hidden, weight_shrink))
    scaled_two, inverse_two, final = norm_forward(
        normed_one + (shrunk + vectors[3]), vectors[4], vectors[5]
    )
    layer_out = to_own_features(final.astype(bf16))

    live = (own_part(query_segment) != 0).astype(f32)[:, None]
    upstream = to_own_tokens(cotangent).astype(f32) * live
    grad_sum_two, grad_gain_two, grad_shift_two = norm_backward(
        upstream, scaled_two, inverse_two, vectors[4]
    )
    grad_shrunk_own = grad_sum_two.astype(bf16)
    grad_shrunk = gather_tokens(grad_shrunk_own)
    grad_hidden = nt(grad_shrunk, weight_shrink)
    grad_pre = jax.vjp(exact_gelu, pre_gelu)[1](grad_hidden)[0].astype(bf16)
    grad_normed = grad_sum_two + sum_tokens(nn(grad_pre, weight_expand))
    grad_res, grad_gain_one, grad_shift_one = norm_backward(
        grad_normed, scaled_one, inverse_one, vectors[1]
    )
    grad_branch_own = grad_res.astype(bf16)
    grad_branch = gather_tokens(grad_branch_own)
    grad_attended = nt(grad_branch, weight_merge).astype(bf16)
    grad_queries, grad_keys, grad_values = attention_backward(
        queries_heads,
        keys_heads,
        values_heads,
        query_segment,
        key_segment,
        lse,
        grad_attended.reshape(head_shape),
    )
    grad_queries = grad_queries.reshape(count, -1)
    grad_keys_values = jnp.concatenate(
        (grad_keys.reshape(-1, heads * HEAD), grad_values.reshape(-1, heads * HEAD)), 1
    )
    if special:
        grad_keys_values = grad_keys_values[:count] + pair(grad_keys_values[count:], "core")
    grad_keys_values = grad_keys_values.astype(bf16)
    grad_keys, grad_values = (
        grad_keys_values[:, : heads * HEAD],
        grad_keys_values[:, heads * HEAD :],
    )
    grad_entry = sum_tokens(
        nn(grad_queries, weight_queries)
        + nn(grad_keys, weight_keys)
        + nn(grad_values, weight_values)
    )
    grad_tokens = to_own_features(grad_res + grad_entry)
    if special:
        layer_out, grad_tokens = swap_sequences(layer_out), swap_sequences(grad_tokens)

    if special:
        half = hidden.shape[1] // 2
        units = hidden_size // 8
        narrow = collect(
            tn(hidden[:, :half], grad_shrunk).reshape(2, cols, units, D),
            tn(hidden[:, half:], grad_shrunk).reshape(2, cols, units, D),
        )
        widen = collect(
            tn(grad_pre[:, :half], normed_low).reshape(2, cols, units, D),
            tn(grad_pre[:, half:], normed_low).reshape(2, cols, units, D),
        )
        parts = (heads, HEAD, D)
        first = jnp.stack(
            (tn(grad_keys, inputs).reshape(parts), tn(grad_values, inputs).reshape(parts)), 1
        )
        second = jnp.stack(
            (tn(grad_queries, inputs).reshape(parts), tn(attended, grad_branch).reshape(parts)), 1
        )
        shape = (2, cols, 2 * HEAD, D)
        attend = collect(
            jnp.where(core == 0, first, second).reshape(shape),
            jnp.where(core == 0, second, first).reshape(shape),
        )
        grad_triple, grad_merge, grad_expand, grad_shrink = ungroup(attend, widen, narrow)
    else:

        def assemble(local, row_axis, col_axis):
            full = jnp.zeros((local.shape[0], local.shape[1] * rows, D), bf16)
            full = lax.dynamic_update_slice(
                full, local.astype(bf16), (0, row * local.shape[1], 0)
            )
            full = lax.psum_scatter(full, "row", scatter_dimension=2, tiled=True)
            full = lax.psum_scatter(full, "col", scatter_dimension=1, tiled=True)
            return lax.psum(full, ("outer", "core")).astype(f32)

        grad_triple = assemble(
            jnp.stack(
                (tn(grad_queries, inputs), tn(grad_keys, inputs), tn(grad_values, inputs))
            ),
            0,
            2,
        ).transpose(2, 0, 1)
        grad_merge = assemble(tn(attended, grad_branch)[None], 1, 0)[0]
        grad_expand = assemble(tn(grad_pre, normed_low)[None], 0, 1)[0].T
        grad_shrink = assemble(tn(hidden, grad_shrunk)[None], 1, 0)[0]

    def column_sums(values):
        return jnp.sum(values, axis=0, dtype=f32)

    sum_hidden = column_sums(grad_pre)
    sum_queries, sum_values = column_sums(grad_queries), column_sums(grad_values)
    if special:
        sum_hidden = global_order(sum_hidden, hidden_size // 8)

        def heads_back(local):
            blocks = local.reshape(2, cols, HEAD).transpose(1, 0, 2)
            blocks = jnp.where(place("outer") == 0, blocks, blocks[:, ::-1])
            full = jnp.zeros((cols, 2, 2, HEAD), f32)
            for step in range(cols):
                full = lax.dynamic_update_slice(
                    full, blocks[step][None, None], ((col - step) % cols, row, 0, 0)
                )
            return full.reshape(-1)

        sum_queries, sum_values = heads_back(sum_queries), heads_back(sum_values)
    else:

        def whole(local):
            full = jnp.zeros(local.shape[0] * rows, f32)
            return lax.dynamic_update_slice(full, local, (row * local.shape[0],))

        sum_hidden, sum_queries, sum_values = (
            whole(sum_hidden),
            whole(sum_queries),
            whole(sum_values),
        )
    sums = lax.psum(
        jnp.concatenate(
            (
                column_sums(grad_branch_own),
                grad_gain_one,
                grad_shift_one,
                column_sums(grad_shrunk_own),
                grad_gain_two,
                grad_shift_two,
                sum_queries,
                sum_values,
                sum_hidden,
            )
        ),
        ("outer", "core", "row", "col"),
    )

    def row_share(index):
        return lax.dynamic_slice_in_dim(sums, index * D + row * row_size, row_size)

    grad_pair = jnp.stack(
        [
            lax.dynamic_slice_in_dim(sums, index * D + col * pair_size, pair_size)
            for index in (6, 7)
        ]
    )
    grad_expand_bias = lax.dynamic_slice_in_dim(sums, 8 * D + col * hidden_size, hidden_size)
    return (
        layer_out,
        grad_tokens,
        grad_triple,
        grad_pair,
        grad_merge,
        row_share(0),
        row_share(1),
        row_share(2),
        grad_expand,
        grad_expand_bias,
        grad_shrink,
        row_share(3),
        row_share(4),
        row_share(5),
    )


def solution(mesh):
    sizes = mesh.shape
    axes = ("outer", "core", "row", "col")
    split = Mesh(
        mesh.devices.reshape(sizes["dp"] // 2, 2, sizes["row"], sizes["col"]), axes
    )
    dp = ("outer", "core")
    activations = P(("outer", "core", "col"), "row")
    return jax.shard_map(
        shards,
        mesh=split,
        in_specs=(
            activations,
            P(dp),
            P("row", None, "col"),
            P(None, "col"),
            P("col", "row"),
            P("row"),
            P("row"),
            P("row"),
            P("row", "col"),
            P("col"),
            P("col", "row"),
            P("row"),
            P("row"),
            P("row"),
            activations,
        ),
        out_specs=(
            activations,
            activations,
            P("row", None, "col"),
            P(None, "col"),
            P("col", "row"),
            P("row"),
            P("row"),
            P("row"),
            P("row", "col"),
            P("col"),
            P("col", "row"),
            P("row"),
            P("row"),
            P("row"),
        ),
        check_vma=False,
    )
```

```python
import functools

import jax
import jax.numpy as jnp
from jax import lax
from jax.experimental import pallas as pl
from jax.experimental.pallas import tpu as pltpu
from jax.sharding import Mesh, PartitionSpec as P

D = 1024
HEAD = 64
LEN = 1024
epsilon = 1e-05
masked_score = -1e30
bf16 = jnp.bfloat16
f32 = jnp.float32


def size(axis):
    return lax.axis_size(axis)


def place(axis):
    return lax.axis_index(axis)


def pair(values, axis):
    return lax.ppermute(values, axis, [(0, 1), (1, 0)])


def after(values, *others):
    return lax.optimization_barrier((values,) + others)[0]


def shift(values, step):
    count = size("col")
    return lax.ppermute(values, "col", [(i, (i + step) % count) for i in range(count)])


def by_place(bit, own, other, axis):
    return jnp.where(
        bit == 0,
        jnp.concatenate((own, other), axis),
        jnp.concatenate((other, own), axis),
    )


def nt(left, right, kind=f32):
    return lax.dot_general(
        left, right, (((1,), (1,)), ((), ())), preferred_element_type=f32
    ).astype(kind)


def nn(left, right, kind=f32):
    return lax.dot_general(
        left, right, (((1,), (0,)), ((), ())), preferred_element_type=f32
    ).astype(kind)


def tn(left, right, kind=f32):
    return lax.dot_general(
        left, right, (((0,), (0,)), ((), ())), preferred_element_type=f32
    ).astype(kind)


def swap_sequences(values):
    count = size("col")
    perm = []
    for core in range(2):
        for col in range(count):
            half, other = col % 2, col - col % 2
            target = (half, other + core)
            perm.append((core * count + col, target[0] * count + target[1]))
    return lax.ppermute(values, ("core", "col"), perm)


def own_first(values):
    if size("row") != 2:
        return values
    half = values.shape[0] // 2
    return jnp.where(place("row") == 0, values, jnp.roll(values, half, axis=0))


def own_part(values):
    share = values.shape[0] // size("row")
    if size("row") == 2:
        return values[:share]
    return lax.dynamic_slice_in_dim(values, place("row") * share, share)


def gather_features(values):
    if size("row") == 2:
        full = by_place(place("row"), values, pair(values, "row"), 1)
        return own_first(full)
    return lax.all_gather(values, "row", axis=1, tiled=True)


def gather_tokens(values):
    if size("row") == 2:
        return jnp.concatenate((values, pair(values, "row")), 0)
    return lax.all_gather(values, "row", axis=0, tiled=True)


def sum_tokens(partial):
    if size("row") == 2:
        share = partial.shape[0] // 2
        return partial[:share] + pair(partial[share:].astype(bf16), "row").astype(f32)
    return lax.psum_scatter(partial, "row", scatter_dimension=0, tiled=True)


def to_own_tokens(values):
    if size("row") == 2:
        bit = place("row")
        ordered = own_first(values)
        share = values.shape[0] // 2
        return by_place(bit, ordered[:share], pair(ordered[share:], "row"), 1)
    return lax.all_to_all(values, "row", 0, 1, tiled=True)


def to_own_features(values):
    if size("row") == 2:
        bit = place("row")
        half = values.shape[1] // 2
        low, high = values[:, :half], values[:, half:]
        own = jnp.where(bit == 0, low, high)
        other = pair(jnp.where(bit == 0, high, low), "row")
        return by_place(bit, own, other, 0)
    return lax.all_to_all(values, "row", 1, 0, tiled=True)


def sum_features(partial, addend):
    if size("row") == 2:
        half = partial.shape[1] // 2
        low, high = partial[:, :half], partial[:, half:]
        bit = place("row")
        got = pair(jnp.where(bit == 0, high, low).astype(bf16), "row").astype(f32)
        got = jnp.roll(got, partial.shape[0] // 2, axis=0)
        return own_first(jnp.where(bit == 0, low, high) + got) + addend
    return lax.psum_scatter(partial, "row", scatter_dimension=1, tiled=True) + addend


def three_groups(triple, merge, expand, shrink):
    depth = triple.shape[0]
    heads = triple.transpose(1, 2, 0).reshape(3, 2, 2, 1, HEAD, depth)
    out = merge.reshape(1, 2, 2, 1, HEAD, depth)
    keys_values = jnp.concatenate((heads[1], heads[2]), 3 - 1)
    queries_merge = jnp.concatenate((heads[0], out[0]), 3 - 1)
    attend = jnp.stack((keys_values, queries_merge), 2).reshape(2, 2, 2, 2 * HEAD, depth)
    widen = expand.T.reshape(2, 2, 2, -1, depth)
    narrow = shrink.reshape(2, 2, 2, -1, depth)
    return attend, widen, narrow


def my_quarter(group):
    some = lax.dynamic_index_in_dim(group, place("outer"), 1, keepdims=False)
    return lax.dynamic_index_in_dim(some, place("core"), 1, keepdims=False)


def exchange_rows(quarter):
    bit = place("row")
    mine = jnp.where(bit == 0, quarter[0], quarter[1])
    other = pair(jnp.where(bit == 0, quarter[1], quarter[0]), "row")
    return by_place(bit, mine, other, 1)


STEPS = (1, 3, 2)


def own_core_half(parts, pairs):
    count = size("col")
    return jnp.stack(
        [jnp.stack([group[step] for step in range(count)]) for group in (parts, pairs)]
    )


def gather_attend(quarter):
    parts = {0: quarter}
    for step in STEPS:
        parts[step] = shift(quarter, step)
    pairs = {step: pair(parts[step], "outer") for step in (0,) + STEPS}
    return own_core_half(parts, pairs), parts[2], pairs[2]


BACK = (2, 1, 3)


def collect_outer(own, other):
    total = own + pair(other, "core").astype(f32)
    return total[0], total[1].astype(bf16)


def collect_send(mates):
    return {step: pair(mates[step], "outer") for step in BACK + (0,)}


def collect_add(own, got, step):
    return own[step] + got[step].astype(f32)


def collect_rest(sums):
    last = sums[0]
    for step in BACK:
        last = last + sums[step].astype(f32)
    return last


def collect_block(last):
    bit = place("row")
    half = last.shape[1] // 2
    low, high = last[:, :half].astype(bf16), last[:, half:].astype(bf16)
    mine = jnp.where(bit == 0, low, high)
    got = pair(jnp.where(bit == 0, high, low), "row")
    block = jnp.stack((jnp.where(bit == 0, mine, got), jnp.where(bit == 0, got, mine)))
    block = by_place(place("outer"), block[:, None], pair(block, "outer")[:, None], 1)
    block = by_place(place("core"), block[:, :, None], pair(block, "core")[:, :, None], 2)
    return block.astype(f32)


def ungroup(attend, widen, narrow):
    depth = attend.shape[-1]
    heads = attend.reshape(4, 2, 2, HEAD, depth)
    keys, values = heads[:, 0, 0], heads[:, 0, 1]
    queries, merge = heads[:, 1, 0], heads[:, 1, 1]
    triple = jnp.stack((queries, keys, values)).reshape(3, 4 * HEAD, depth).transpose(2, 0, 1)
    return (
        triple,
        merge.reshape(4 * HEAD, depth),
        widen.reshape(-1, depth).T,
        narrow.reshape(-1, depth),
    )


def flip(values, axis, bit):
    return jnp.where(bit == 0, values, jnp.flip(values, axis))


def dot(left, right, left_dim, right_dim):
    return lax.dot_general(
        left, right, (((left_dim,), (right_dim,)), ((), ())), preferred_element_type=f32
    )


def params():
    return pltpu.CompilerParams(vmem_limit_bytes=56 << 20)


def anywhere(arrays):
    return [pl.BlockSpec(memory_space=pl.ANY) for _ in arrays]


def attend_forward_kernel(q_ref, kv_ref, qs_ref, ks_ref, *rest):
    out_ref, lse_ref = rest[-2:]
    same = ks_ref[...] == qs_ref[...]
    for head in range(2):
        part = slice(head * HEAD, (head + 1) * HEAD)
        keys = kv_ref[:, 2 * head * HEAD : (2 * head + 1) * HEAD]
        values = kv_ref[:, (2 * head + 1) * HEAD : (2 * head + 2) * HEAD]
        queries = q_ref[:, part] * jnp.asarray(HEAD**-0.5, bf16)
        scores = jnp.where(same, dot(keys, queries, 1, 1), masked_score)
        top = jnp.max(scores, axis=0, keepdims=True)
        weights = jnp.exp(scores - top)
        total = jnp.sum(weights, axis=0, keepdims=True)
        low = (weights * (1.0 / total)).astype(bf16)
        out_ref[part] = dot(values, low, 0, 0).astype(bf16)
        lse_ref[0, head : head + 1] = top + jnp.log(total)


def attend_forward(queries, keys_values, query_segment, key_segment, begin, steps, *earlier):
    tokens = queries.shape[0]
    width = steps * 2 * HEAD
    keys = keys_values.shape[0]
    return pl.pallas_call(
        attend_forward_kernel,
        grid=(steps,),
        in_specs=[
            pl.BlockSpec((tokens, 2 * HEAD), lambda i: (0, begin + i)),
            pl.BlockSpec((keys, 4 * HEAD), lambda i: (0, begin + i)),
            pl.BlockSpec((1, tokens), lambda i: (0, 0)),
            pl.BlockSpec((keys, 1), lambda i: (0, 0)),
        ]
        + anywhere(earlier),
        out_specs=[
            pl.BlockSpec((2 * HEAD, tokens), lambda i: (i, 0)),
            pl.BlockSpec((1, 2, tokens), lambda i: (i, 0, 0)),
        ],
        out_shape=[
            jax.ShapeDtypeStruct((width, tokens), bf16),
            jax.ShapeDtypeStruct((steps, 2, tokens), f32),
        ],
        compiler_params=params(),
        cost_estimate=pl.CostEstimate(
            flops=4 * tokens * keys * width * 4,
            bytes_accessed=4 << 20,
            transcendentals=tokens * keys * width // HEAD,
        ),
    )(queries, keys_values, query_segment, key_segment, *earlier)


def attend_backward_kernel(
    q_ref, kv_ref, g_ref, qs_ref, ks_ref, lse_ref, *rest
):
    dq_ref, near_ref, far_ref = rest[-3:]
    same = ks_ref[...] == qs_ref[...]
    scale = HEAD**-0.5
    near = near_ref.shape[0]
    for head in range(2):
        part = slice(head * HEAD, (head + 1) * HEAD)
        key_part = slice(2 * head * HEAD, (2 * head + 1) * HEAD)
        value_part = slice((2 * head + 1) * HEAD, (2 * head + 2) * HEAD)
        keys, values = kv_ref[:, key_part], kv_ref[:, value_part]
        queries = q_ref[:, part] * jnp.asarray(scale, bf16)
        grad = g_ref[:, part]
        scores = jnp.where(same, dot(keys, queries, 1, 1), masked_score)
        weights = jnp.exp(scores - lse_ref[0, head : head + 1])
        grad_weights = dot(values, grad, 1, 1)
        inner = jnp.sum(weights * grad_weights, axis=0, keepdims=True)
        grad_scores = (weights * (grad_weights - inner)).astype(bf16)
        dq_ref[part] = (dot(keys, grad_scores, 0, 0) * scale).astype(bf16)
        grad_keys = dot(grad_scores, queries, 1, 0)
        grad_values = dot(weights.astype(bf16), grad, 1, 0)
        near_ref[:, key_part], far_ref[:, key_part] = grad_keys[:near], grad_keys[near:]
        near_ref[:, value_part], far_ref[:, value_part] = grad_values[:near], grad_values[near:]


def attend_backward(
    queries, keys_values, grad, query_segment, key_segment, lse, begin, steps, *earlier
):
    tokens = queries.shape[0]
    keys = keys_values.shape[0]
    key_block = pl.BlockSpec((tokens, 4 * HEAD), lambda i: (0, i))
    return pl.pallas_call(
        attend_backward_kernel,
        grid=(steps,),
        in_specs=[
            pl.BlockSpec((tokens, 2 * HEAD), lambda i: (0, begin + i)),
            pl.BlockSpec((keys, 4 * HEAD), lambda i: (0, begin + i)),
            pl.BlockSpec((tokens, 2 * HEAD), lambda i: (0, begin + i)),
            pl.BlockSpec((1, tokens), lambda i: (0, 0)),
            pl.BlockSpec((keys, 1), lambda i: (0, 0)),
            pl.BlockSpec((1, 2, tokens), lambda i: (i, 0, 0)),
        ]
        + anywhere(earlier),
        out_specs=[pl.BlockSpec((2 * HEAD, tokens), lambda i: (i, 0)), key_block, key_block],
        out_shape=[
            jax.ShapeDtypeStruct((2 * HEAD * steps, tokens), bf16),
            jax.ShapeDtypeStruct((tokens, 4 * HEAD * steps), f32),
            jax.ShapeDtypeStruct((tokens, 4 * HEAD * steps), f32),
        ],
        compiler_params=params(),
        cost_estimate=pl.CostEstimate(
            flops=10 * tokens * keys * steps * 2 * HEAD * 4,
            bytes_accessed=8 << 20,
            transcendentals=tokens * keys * steps * 2,
        ),
    )(queries, keys_values, grad, query_segment, key_segment, lse, *earlier)


def attend_weights_kernel(
    which_ref, dkv_ref, dq_ref, out_in_ref, x_ref, g_ref, *rest, added, cols
):
    add_ref = rest[0] if added else None
    out_refs = rest[-cols:]

    def put(rows, value):
        value = value.reshape(cols, -1, D)
        for step, out_ref in enumerate(out_refs):
            term = value[step]
            if added:
                term = term + add_ref[0, step, rows].astype(f32)
            out_ref[rows] = term.astype(out_ref.dtype)

    @pl.when(which_ref[0] == 0)
    def _():
        put(slice(0, 2 * HEAD), dot(dkv_ref[...], x_ref[...], 0, 0))

    @pl.when(which_ref[0] == 1)
    def _():
        put(slice(0, HEAD), dot(dq_ref[...], x_ref[...], 1, 0))
        put(slice(HEAD, 2 * HEAD), dot(out_in_ref[...], g_ref[...], 1, 0))


def attend_weights(which, dkv, dq, out_in, x, g, begin, cols, kind, add=None, earlier=()):
    tokens = x.shape[0]
    full = pl.BlockSpec((tokens, D), lambda i, w: (0, 0))
    rows = pl.BlockSpec((cols * HEAD, tokens), lambda i, w: (begin, 0))
    specs = [pl.BlockSpec((tokens, cols * 2 * HEAD), lambda i, w: (0, begin)), rows, rows, full, full]
    given = [dkv, dq, out_in, x, g]
    if add is not None:
        specs.append(pl.BlockSpec((1, cols, 2 * HEAD, D), lambda i, w: (begin, 0, 0, 0)))
        given.append(add)
    return pl.pallas_call(
        functools.partial(attend_weights_kernel, added=add is not None, cols=cols),
        grid_spec=pltpu.PrefetchScalarGridSpec(
            num_scalar_prefetch=1,
            grid=(1,),
            in_specs=specs + anywhere(earlier),
            out_specs=[pl.BlockSpec((2 * HEAD, D), lambda i, w: (0, 0))] * cols,
        ),
        out_shape=[jax.ShapeDtypeStruct((2 * HEAD, D), kind)] * cols,
        compiler_params=params(),
        cost_estimate=pl.CostEstimate(
            flops=4 * tokens * D * cols * HEAD, bytes_accessed=6 << 20, transcendentals=0
        ),
    )(which, *given, *earlier)


def attend_far_kernel(which_ref, dkv_ref, dq_ref, out_in_ref, x_ref, g_ref, *rest):
    out_ref = rest[-1]
    cols = out_ref.shape[1]

    @pl.when(which_ref[0] == 0)
    def _():
        value = dot(dkv_ref[...], x_ref[...], 0, 0)
        out_ref[0] = value.reshape(cols, 2 * HEAD, D).astype(out_ref.dtype)

    @pl.when(which_ref[0] == 1)
    def _():
        for part, value in enumerate(
            (dot(dq_ref[...], x_ref[...], 1, 0), dot(out_in_ref[...], g_ref[...], 1, 0))
        ):
            rows = slice(part * HEAD, (part + 1) * HEAD)
            out_ref[0, :, rows] = value.reshape(cols, HEAD, D).astype(out_ref.dtype)


def attend_far_weights(which, dkv, dq, out_in, x, g, cols, *earlier):
    tokens = x.shape[0]
    full = pl.BlockSpec((tokens, D), lambda i, w: (0, 0))
    rows = pl.BlockSpec((cols * HEAD, tokens), lambda i, w: (i, 0))
    return pl.pallas_call(
        attend_far_kernel,
        grid_spec=pltpu.PrefetchScalarGridSpec(
            num_scalar_prefetch=1,
            grid=(2,),
            in_specs=[
                pl.BlockSpec((tokens, cols * 2 * HEAD), lambda i, w: (0, i)), rows, rows, full, full
            ]
            + anywhere(earlier),
            out_specs=pl.BlockSpec((1, cols, 2 * HEAD, D), lambda i, w: (i, 0, 0, 0)),
        ),
        out_shape=jax.ShapeDtypeStruct((2, cols, 2 * HEAD, D), bf16),
        compiler_params=params(),
        cost_estimate=pl.CostEstimate(
            flops=8 * tokens * D * cols * HEAD, bytes_accessed=6 << 20, transcendentals=0
        ),
    )(which, dkv, dq, out_in, x, g, *earlier)


def hidden_forward_kernel(x_ref,own_ref,far_ref,bias_ref,hidden_ref,slope_ref,keep_ref,send_ref,total):
    step=pl.program_id(0)
    units=own_ref.shape[2]//2
    width=own_ref.shape[1]*units
    @pl.when(step==0)
    def _(): total[...]=jnp.zeros_like(total)
    for core,ref in enumerate((own_ref,far_ref)):
        expand=ref[0,:,:units].reshape(width,D)
        shrink=ref[0,:,units:].reshape(width,D)
        u=dot(x_ref[...],expand,1,1)+bias_ref[0,core:core+1]
        normal=0.5*(1.0+lax.erf(u*(0.5**0.5)))
        slope_ref[core]=normal+u*(jnp.exp(-0.5*u*u)*((0.5/jnp.pi)**0.5))
        hidden=(u*normal).astype(bf16)
        hidden_ref[core]=hidden
        total[...]+=dot(hidden,shrink,1,0)
    @pl.when(step==pl.num_programs(0)-1)
    def _():
        half=total.shape[0]//2
        keep_ref[...]=total[:half]
        send_ref[...]=total[half:].astype(bf16)


def hidden_forward(x,own,far,bias):
    tokens=x.shape[0]; outer,cols,two,_=own.shape; units=two//2; pairs=2
    steps=outer*cols//pairs; width=pairs*units; per=cols//pairs
    block=pl.BlockSpec((1,pairs,two,D),lambda i:(i//per,i%per,0,0))
    wide=pl.BlockSpec((2,tokens,width),lambda i:(0,0,i))
    half=pl.BlockSpec((tokens//2,D),lambda i:(0,0))
    return pl.pallas_call(hidden_forward_kernel,grid=(steps,),
      in_specs=[pl.BlockSpec((tokens,D),lambda i:(0,0)),block,block,pl.BlockSpec((1,2,width),lambda i:(i,0,0))],
      out_specs=[wide,wide,half,half],
      out_shape=[jax.ShapeDtypeStruct((2,tokens,steps*width),bf16),jax.ShapeDtypeStruct((2,tokens,steps*width),f32),
                 jax.ShapeDtypeStruct((tokens//2,D),f32),jax.ShapeDtypeStruct((tokens//2,D),bf16)],
      scratch_shapes=[pltpu.VMEM((tokens,D),f32)],compiler_params=params(),
      cost_estimate=pl.CostEstimate(flops=8*tokens*D*steps*width,bytes_accessed=20<<20,transcendentals=4*tokens*steps*width))(x,own,far,bias)


def hidden_backward_kernel(g_ref,own_ref,far_ref,slope_ref,grad_ref,sum_ref,keep_ref,send_ref,total):
    step=pl.program_id(0)
    units=own_ref.shape[2]//2
    width=own_ref.shape[1]*units
    @pl.when(step==0)
    def _(): total[...]=jnp.zeros_like(total)
    for core,ref in enumerate((own_ref,far_ref)):
        expand=ref[0,:,:units].reshape(width,D)
        shrink=ref[0,:,units:].reshape(width,D)
        grad=(dot(g_ref[...],shrink,1,1)*slope_ref[core]).astype(bf16)
        grad_ref[core]=grad
        sum_ref[0,core:core+1]=jnp.sum(grad.astype(f32),axis=0,keepdims=True)
        total[...]+=dot(grad,expand,1,0)
    @pl.when(step==pl.num_programs(0)-1)
    def _():
        half=total.shape[0]//2
        keep_ref[...]=total[:half]
        send_ref[...]=total[half:].astype(bf16)


def hidden_backward(g,own,far,slope):
    tokens=g.shape[0]; outer,cols,two,_=own.shape; units=two//2; pairs=2
    steps=outer*cols//pairs; width=pairs*units; per=cols//pairs
    block=pl.BlockSpec((1,pairs,two,D),lambda i:(i//per,i%per,0,0))
    wide=pl.BlockSpec((2,tokens,width),lambda i:(0,0,i))
    half=pl.BlockSpec((tokens//2,D),lambda i:(0,0))
    return pl.pallas_call(hidden_backward_kernel,grid=(steps,),
      in_specs=[pl.BlockSpec((tokens,D),lambda i:(0,0)),block,block,wide],
      out_specs=[wide,pl.BlockSpec((1,2,width),lambda i:(i,0,0)),half,half],
      out_shape=[jax.ShapeDtypeStruct((2,tokens,steps*width),bf16),jax.ShapeDtypeStruct((steps,2,width),f32),
                 jax.ShapeDtypeStruct((tokens//2,D),f32),jax.ShapeDtypeStruct((tokens//2,D),bf16)],
      scratch_shapes=[pltpu.VMEM((tokens,D),f32)],compiler_params=params(),
      cost_estimate=pl.CostEstimate(flops=8*tokens*D*steps*width,bytes_accessed=20<<20,transcendentals=0))(g,own,far,slope)


def hidden_weights_kernel(grad_ref,hidden_ref,x_ref,g_ref,*rest):
    out_ref=rest[-1]; add_ref=rest[0] if len(rest)>=2 else None
    cols,two,_=out_ref.shape[-3:]; units=two//2
    for part,(left,right) in enumerate(((grad_ref,x_ref),(hidden_ref,g_ref))):
        rows=slice(part*units,(part+1)*units)
        value=dot(left[0],right[...],0,0).reshape(cols,units,D)
        if add_ref is not None: value=value+add_ref[0,:,rows].astype(f32)
        out_ref[0,:,rows]=value.astype(out_ref.dtype)


def hidden_weights(grad,hidden,x,g,core,begin,count,cols,kind,add=None,earlier=()):
    tokens=x.shape[0]; width=grad.shape[2]//2; units=width//cols
    left=pl.BlockSpec((1,tokens,width),lambda i:(core,0,begin+i))
    full=pl.BlockSpec((tokens,D),lambda i:(0,0))
    specs=[left,left,full,full]; args=[grad,hidden,x,g]
    if add is not None:
        specs.append(pl.BlockSpec((1,cols,2*units,D),lambda i:(begin+i,0,0,0))); args.append(add)
    specs+=anywhere(earlier); args+=earlier
    return pl.pallas_call(hidden_weights_kernel,grid=(count,),in_specs=specs,
      out_specs=pl.BlockSpec((1,cols,2*units,D),lambda i:(i,0,0,0)),
      out_shape=jax.ShapeDtypeStruct((count,cols,2*units,D),kind),compiler_params=params(),
      cost_estimate=pl.CostEstimate(flops=4*tokens*D*width*count,bytes_accessed=8<<20,transcendentals=0))(*args)


def hidden_own_kernel(grad_ref, hidden_ref, x_ref, g_ref, add_ref, *rest, cols):
    out_refs = rest[-cols:]
    units = out_refs[0].shape[0] // 2
    for part, (left, right) in enumerate(((grad_ref, x_ref), (hidden_ref, g_ref))):
        rows = slice(part * units, (part + 1) * units)
        value = dot(left[0], right[...], 0, 0).reshape(cols, units, D)
        for step, out_ref in enumerate(out_refs):
            term = value[step] + add_ref[0, step, rows].astype(f32)
            out_ref[rows] = term.astype(out_ref.dtype)


def hidden_own_weights(grad, hidden, x, g, begin, cols, kind, add, *earlier):
    tokens = x.shape[0]
    width = grad.shape[2] // 2
    units = width // cols
    left = pl.BlockSpec((1, tokens, width), lambda i: (0, 0, begin))
    full = pl.BlockSpec((tokens, D), lambda i: (0, 0))
    return pl.pallas_call(
        functools.partial(hidden_own_kernel, cols=cols),
        grid=(1,),
        in_specs=[
            left, left, full, full, pl.BlockSpec((1, cols, 2 * units, D), lambda i: (begin, 0, 0, 0))
        ]
        + anywhere(earlier),
        out_specs=[pl.BlockSpec((2 * units, D), lambda i: (0, 0))] * cols,
        out_shape=[jax.ShapeDtypeStruct((2 * units, D), kind)] * cols,
        compiler_params=params(),
        cost_estimate=pl.CostEstimate(
            flops=4 * tokens * D * width, bytes_accessed=8 << 20, transcendentals=0
        ),
    )(grad, hidden, x, g, add, *earlier)


def layer(
    tokens, segments, triple_weight, pair_bias, merge_weight, merge_bias, first_gain, first_shift,
    expand_weight, expand_bias, shrink_weight, shrink_bias, second_gain, second_shift, cotangent,
):
    cols = size("col")
    count = tokens.shape[0]
    own = count // 2
    heads = D // HEAD // 2
    row, col, core, outer = place("row"), place("col"), place("core"), place("outer")
    row_size, pair_size, hidden_size = merge_bias.shape[0], pair_bias.shape[1], expand_bias.shape[0]

    tokens = swap_sequences(tokens)
    row_vectors = jnp.stack(
        (merge_bias, first_gain, first_shift, shrink_bias, second_gain, second_shift)
    )
    column = jnp.concatenate(
        [
            lax.dynamic_slice_in_dim(vector, row * (vector.shape[0] // 2), vector.shape[0] // 2)
            for vector in (pair_bias[0], pair_bias[1], expand_bias)
        ]
    )
    groups = [
        my_quarter(group)
        for group in three_groups(triple_weight, merge_weight, expand_weight, shrink_weight)
    ]
    quarter, row_vectors, column = lax.optimization_barrier(
        (exchange_rows(groups[0]), row_vectors, column)
    )
    parts = {0: quarter}
    for step in STEPS:
        parts[step] = shift(quarter, step)
    inputs = gather_features(tokens)
    other_quarter = exchange_rows(jnp.concatenate((groups[1], groups[2]), 1))

    half = col % 2
    other = pair(segments.astype(f32), "core").astype(jnp.int32)
    sequence = lax.dynamic_slice_in_dim(
        jnp.where(half == core, segments, other), (col // 2) * LEN, LEN
    ).reshape(2, count)
    query_segment = own_first(lax.dynamic_index_in_dim(sequence, core, 0, keepdims=False))
    far_segment = own_first(lax.dynamic_index_in_dim(sequence, 1 - core, 0, keepdims=False))
    key_segment = jnp.concatenate((query_segment, far_segment))
    segment_row, segment_column = query_segment[None], key_segment[:, None]
    segment_column = jnp.broadcast_to(segment_column, (2 * count, 1))

    vectors = by_place(row, row_vectors, pair(row_vectors, "row"), 1)
    column = jnp.stack([column] + [shift(column, step) for step in range(1, cols)])

    pairs = {step: pair(parts[step], "outer") for step in (0, 1, 3)}
    parts[2], other_quarter, vectors, column, inputs, segment_column, cotangent = (
        lax.optimization_barrier(
            (parts[2], other_quarter, vectors, column, inputs, segment_column, cotangent)
        )
    )
    pairs[2] = pair(parts[2], "outer")
    cotangent = swap_sequences(cotangent)
    other_parts = {0: other_quarter}
    for step in (1, 3):
        other_parts[step] = shift(other_quarter, step)
    attend_own = own_core_half(parts, pairs)
    attend_far = pair(attend_own, "core")
    other_pairs = {0: pair(other_quarter, "outer")}
    upstream = to_own_tokens(cotangent)

    vectors = vectors.astype(f32)
    short = pair_size // 2
    bias_pair = column[:, : 2 * short].reshape(cols, 2, 2, HEAD)
    bias_pair = flip(bias_pair, 2, outer).transpose(1, 2, 0, 3).reshape(2, heads, HEAD).astype(f32)
    bias_queries = bias_pair[0].reshape(-1)
    bias_keys_values = jnp.stack((jnp.zeros_like(bias_pair[1]), bias_pair[1]), 1).reshape(-1)
    bias_hidden = column[:, 2 * short :].reshape(cols, 2, 2, -1)
    bias_hidden = flip(flip(bias_hidden, 1, outer), 2, core).transpose(1, 0, 2, 3)
    bias_hidden = bias_hidden.reshape(2 * cols // 2, 2, 2, -1).transpose(0, 2, 1, 3)
    bias_hidden = bias_hidden.reshape(cols, 2, -1).astype(f32)

    weight_keys_values = jnp.where(core == 0, attend_own, attend_far).reshape(-1, D)
    second = jnp.where(core == 0, attend_far, attend_own).reshape(heads, 2, HEAD, D)
    weight_queries, weight_merge = second[:, 0].reshape(-1, D), second[:, 1].reshape(-1, D)

    cut = heads * HEAD // 2
    steps = heads // 4
    keys_values = (nt(inputs, weight_keys_values) + bias_keys_values).astype(bf16)
    far_keys_values = pair(keys_values, "core")
    queries = (nt(inputs, weight_queries) + bias_queries).astype(bf16)
    keys_values = jnp.concatenate((keys_values, far_keys_values), 0)
    queries, other_parts[1], other_parts[3], other_pairs[0] = lax.optimization_barrier(
        (queries, other_parts[1], other_parts[3], other_pairs[0])
    )
    other_parts[2], other_quarter = lax.optimization_barrier((other_quarter, other_parts[3]))
    other_parts[2] = shift(other_parts[2], 2)
    other_parts[3] = other_quarter
    for step in (1, 3):
        other_pairs[step] = pair(other_parts[step], "outer")
    attention = (queries, keys_values, segment_row, segment_column)
    attended_first, lse_first = attend_forward(*attention, 0, steps)
    attended_second, lse_second = attend_forward(
        *attention, steps, steps, lse_first, other_pairs[1]
    )
    attended_first, attended_second, upstream, other_pairs[3], other_parts[2] = (
        lax.optimization_barrier(
            (attended_first, attended_second, upstream, other_pairs[3], other_parts[2])
        )
    )
    other_pairs[2] = pair(other_parts[2], "outer")
    attended = jnp.concatenate((attended_first, attended_second), 0)
    branch = tn(attended, weight_merge)
    branch = sum_tokens(branch)
    residual = inputs[:own].astype(f32) + (branch + vectors[0])
    scaled_one, inverse_one, normed_one = norm_forward(residual, vectors[1], vectors[2])
    normed_low = gather_tokens(normed_one.astype(bf16))
    other_parts, other_pairs, normed_one = lax.optimization_barrier(
        (other_parts, other_pairs, normed_one)
    )

    other_own = own_core_half(other_parts, other_pairs)
    other_far = pair(other_own, "core")
    hidden, slope, keep, send = hidden_forward(normed_low, other_own, other_far, bias_hidden)
    shrunk = keep + pair(send, "row").astype(f32)
    scaled_two, inverse_two, final = norm_forward(
        normed_one + (shrunk + vectors[3]), vectors[4], vectors[5]
    )
    live = (query_segment[:own] != 0).astype(f32)[:, None]
    upstream = upstream.astype(f32) * live
    grad_sum_two, grad_gain_two, grad_shift_two = norm_backward(
        upstream, scaled_two, inverse_two, vectors[4]
    )
    grad_shrunk_own = grad_sum_two.astype(bf16)
    grad_shrunk = gather_tokens(grad_shrunk_own)
    grad_pre, sum_hidden, keep, send = hidden_backward(grad_shrunk, other_own, other_far, slope)
    got_normed = pair(send, "row")
    part = (grad_pre, hidden, normed_low, grad_shrunk)
    far = hidden_weights(*part, 1, 0, 2, cols, bf16)
    grad_normed = grad_sum_two + (keep + got_normed.astype(f32))
    grad_res, grad_gain_one, grad_shift_one = norm_backward(
        grad_normed, scaled_one, inverse_one, vectors[1]
    )
    grad_branch_own = grad_res.astype(bf16)
    grad_branch = gather_tokens(grad_branch_own)
    far, grad_branch_own = lax.optimization_barrier((far, grad_branch_own))
    far = pair(far, "core")
    mates = hidden_own_weights(*part, 1, cols, bf16, far)
    grad_branch, mates = lax.optimization_barrier((grad_branch, mates))
    hidden_got = collect_send(mates)

    grad_attended = nt(grad_branch, weight_merge, bf16)
    shared = (queries, keys_values, grad_attended, segment_row, segment_column)
    dq_first, near_first, far_first = attend_backward(*shared, lse_first, 0, steps)
    late_out, late_res, far_first = lax.optimization_barrier(
        (final.astype(bf16), grad_res, far_first)
    )
    far_first = pair(far_first, "core")
    hidden_got[2], dq_first = lax.optimization_barrier((hidden_got[2], dq_first))
    hidden_own = hidden_own_weights(*part, 0, cols, f32, far, dq_first)
    hidden_last = {2: collect_add(hidden_own, hidden_got, 2).astype(bf16)}
    dq_second, near_second, far_second = attend_backward(
        *shared, lse_second, steps, steps, hidden_last[2]
    )
    hidden_last[2] = shift(hidden_last[2], -2)
    far_second = pair(far_second, "core")
    layer_out, grad_res_columns = to_own_features(late_out), to_own_features(late_res)
    hidden_got[1], dq_second = lax.optimization_barrier((hidden_got[1], dq_second))
    hidden_last[1] = shift(collect_add(hidden_own, hidden_got, 1).astype(bf16), -1)
    grad_queries = jnp.concatenate((dq_first, dq_second), 0)
    grad_keys_values = jnp.concatenate(
        ((near_first + far_first).astype(bf16), (near_second + far_second).astype(bf16)), 1
    )

    part = (grad_keys_values, grad_queries, attended, inputs, grad_branch)
    far = attend_far_weights((1 - core).reshape(1), *part, cols, hidden_last[2])
    far_got = pair(far, "core")
    grad_entry = nn(grad_keys_values, weight_keys_values) + tn(grad_queries, weight_queries)
    grad_tokens = sum_features(grad_entry, grad_res_columns)
    hidden_got[3], far_got = lax.optimization_barrier((hidden_got[3], far_got))
    hidden_last[3] = shift(collect_add(hidden_own, hidden_got, 3).astype(bf16), -3)
    which = core.reshape(1)
    mates = attend_weights(which, *part, 1, cols, bf16, far_got, (hidden_last[1],))
    got = collect_send(mates)
    attend_own_sums = attend_weights(
        which, *part, 0, cols, f32, far_got, (hidden_got[0], hidden_last[3])
    )
    grad_tokens, layer_out = lax.optimization_barrier((grad_tokens, layer_out))
    layer_out, grad_tokens = swap_sequences(layer_out), swap_sequences(grad_tokens)
    sums = {2: collect_add(attend_own_sums, got, 2)}
    sums[2] = shift(sums[2].astype(bf16), -2)
    hidden_last[0] = collect_add(hidden_own, hidden_got, 0)
    hidden_rest = collect_rest(hidden_last)
    got[1], hidden_rest = lax.optimization_barrier((got[1], hidden_rest))
    for step in (1, 3, 0):
        sums[step] = collect_add(attend_own_sums, got, step)
    for step in (1, 3):
        sums[step] = shift(sums[step].astype(bf16), -step)
    units = hidden_size // 8
    both = collect_block(hidden_rest)
    widen, narrow = both[:, :, :, :units], both[:, :, :, units:]
    attend_rest = collect_rest(sums)
    attend = collect_block(attend_rest)
    grad_triple, grad_merge, grad_expand, grad_shrink = ungroup(attend, widen, narrow)

    sum_rows = jnp.stack(
        (
            jnp.sum(grad_branch_own, axis=0, dtype=f32),
            grad_gain_one,
            grad_shift_one,
            jnp.sum(grad_shrunk_own, axis=0, dtype=f32),
            grad_gain_two,
            grad_shift_two,
        )
    )
    sum_queries = jnp.sum(grad_queries, axis=1, dtype=f32)
    sum_values = jnp.sum(grad_keys_values, axis=0, dtype=f32).reshape(heads, 2, HEAD)[:, 1]
    sum_pair = jnp.stack((sum_queries, sum_values.reshape(-1))).reshape(2, 2, cols, HEAD)
    sum_pair = flip(sum_pair.transpose(2, 0, 1, 3), 2, outer).reshape(cols, -1)
    sum_hidden = sum_hidden.reshape(2, cols // 2, 2, 2, -1).transpose(1, 3, 0, 2, 4)
    sum_hidden = flip(flip(sum_hidden.reshape(cols, 2, 2, -1), 1, outer), 2, core).reshape(cols, -1)
    sum_columns = jnp.concatenate((sum_pair, sum_hidden), 1)
    length = sum_columns.shape[1]
    sum_columns = jnp.concatenate(
        [
            lax.dynamic_index_in_dim(sum_columns, (col - place_of) % cols, 0, keepdims=False)
            for place_of in range(cols)
        ]
    )
    total = jnp.concatenate((sum_columns, sum_rows.reshape(-1)))
    for bit in (1, 2):
        total = total + lax.ppermute(total, "col", [(i, i ^ bit) for i in range(cols)])
    total = total + pair(total, "core")
    total = total + pair(total, "outer")
    mine = lax.dynamic_slice_in_dim(total, col * length, length)
    sum_rows = total[cols * length :].reshape(6, 2, row_size)
    low, high = sum_rows[:, 0].reshape(-1), sum_rows[:, 1].reshape(-1)
    got = pair(jnp.concatenate((mine, jnp.where(row == 0, high, low))), "row")
    totals = (jnp.where(row == 0, low, high) + got[length:]).reshape(6, row_size)
    got = got[:length]
    short = 2 * HEAD
    grad_pair = by_place(
        row, mine[: 2 * short].reshape(2, short), got[: 2 * short].reshape(2, short), 1
    )
    grad_expand_bias = by_place(row, mine[2 * short :], got[2 * short :], 0)
    return (
        layer_out, grad_tokens, grad_triple, grad_pair, grad_merge, totals[0], totals[1], totals[2],
        grad_expand, grad_expand_bias, grad_shrink, totals[3], totals[4], totals[5],
    )


def masked(scores, query_segment, key_segment):
    same = query_segment[:, None] == key_segment[None, :]
    return jnp.where(same[None], scores, masked_score)


def attention_forward(queries, keys, values, query_segment, key_segment):
    scores = jnp.einsum("qhd,khd->hqk", queries, keys, preferred_element_type=f32)
    scores = masked(scores * HEAD**-0.5, query_segment, key_segment)
    top = jnp.max(scores, axis=-1, keepdims=True)
    weights = jnp.exp(scores - top)
    total = jnp.sum(weights, axis=-1, keepdims=True)
    low = (weights / total).astype(bf16)
    attended = jnp.einsum("hqk,khd->qhd", low, values, preferred_element_type=f32)
    return attended.astype(bf16), top + jnp.log(total)


def attention_backward(queries, keys, values, query_segment, key_segment, lse, grad):
    scores = jnp.einsum("qhd,khd->hqk", queries, keys, preferred_element_type=f32)
    scores = masked(scores * HEAD**-0.5, query_segment, key_segment)
    weights = jnp.exp(scores - lse)
    grad_weights = jnp.einsum("qhd,khd->hqk", grad, values, preferred_element_type=f32)
    inner = jnp.sum(weights * grad_weights, axis=-1, keepdims=True)
    grad_scores = (weights * (grad_weights - inner)).astype(bf16)
    scale = HEAD**-0.5
    grad_queries = jnp.einsum("hqk,khd->qhd", grad_scores, keys, preferred_element_type=f32) * scale
    grad_keys = jnp.einsum("hqk,qhd->khd", grad_scores, queries, preferred_element_type=f32) * scale
    grad_values = jnp.einsum(
        "hqk,qhd->khd", weights.astype(bf16), grad, preferred_element_type=f32
    )
    return grad_queries.astype(bf16), grad_keys, grad_values


def norm_forward(values, gain, shift):
    center = jnp.mean(values, axis=1, keepdims=True)
    inverse = lax.rsqrt(
        jnp.mean(values * values, axis=1, keepdims=True) - center * center + epsilon
    )
    scaled = (values - center) * inverse
    return scaled, inverse, scaled * gain + shift


def norm_backward(upstream, scaled, inverse, gain):
    through = upstream * gain
    grad = inverse * (
        through
        - jnp.mean(through, axis=1, keepdims=True)
        - scaled * jnp.mean(through * scaled, axis=1, keepdims=True)
    )
    return grad, jnp.sum(upstream * scaled, axis=0), jnp.sum(upstream, axis=0)


def exact_gelu(values):
    return jax.nn.gelu(values, approximate=False)


def layer_anywhere(
    tokens,
    segments,
    triple_weight,
    pair_bias,
    merge_weight,
    merge_bias,
    first_gain,
    first_shift,
    expand_weight,
    expand_bias,
    shrink_weight,
    shrink_bias,
    second_gain,
    second_shift,
    cotangent,
):
    rows, cols = size("row"), size("col")
    count = tokens.shape[0]
    own = count // rows
    heads = D // HEAD // rows
    row, col = place("row"), place("col")

    query_segment = lax.dynamic_slice_in_dim(segments, col * count, count)
    key_segment = query_segment

    row_size, pair_size, hidden_size = merge_bias.shape[0], pair_bias.shape[1], expand_bias.shape[0]
    row_vectors = jnp.stack(
        (merge_bias, first_gain, first_shift, shrink_bias, second_gain, second_shift)
    )
    vectors = lax.all_gather(row_vectors, "row", axis=1, tiled=True)

    def mine_of(full, axis=0):
        share = full.shape[axis] // rows
        return lax.dynamic_slice_in_dim(full, row * share, share, axis)

    bias_pair = mine_of(lax.all_gather(pair_bias, "col", axis=1, tiled=True), 1)
    bias_queries, bias_values = bias_pair[0], bias_pair[1]
    bias_hidden = mine_of(lax.all_gather(expand_bias, "col", axis=0, tiled=True)).astype(f32)
    vectors = vectors.astype(f32)

    triple = lax.all_gather(triple_weight, "col", axis=2, tiled=True)
    triple = lax.all_gather(triple, "row", axis=0, tiled=True).transpose(1, 2, 0)
    merge = lax.all_gather(merge_weight, "col", axis=0, tiled=True)
    merge = lax.all_gather(merge, "row", axis=1, tiled=True)
    expand = lax.all_gather(expand_weight, "col", axis=1, tiled=True)
    expand = lax.all_gather(expand, "row", axis=0, tiled=True).T
    shrink = lax.all_gather(shrink_weight, "col", axis=0, tiled=True)
    shrink = lax.all_gather(shrink, "row", axis=1, tiled=True)

    weight_queries, weight_keys, weight_values = (mine_of(triple[j]) for j in range(3))
    weight_merge, weight_expand, weight_shrink = mine_of(merge), mine_of(expand), mine_of(shrink)

    inputs = gather_features(tokens)
    head_shape = (-1, heads, HEAD)
    queries = (nt(inputs, weight_queries) + bias_queries.astype(f32)).astype(bf16)
    keys = nt(inputs, weight_keys).astype(bf16)
    values = (nt(inputs, weight_values) + bias_values.astype(f32)).astype(bf16)
    all_keys, all_values = keys, values
    queries_heads = queries.reshape(head_shape)
    keys_heads, values_heads = all_keys.reshape(head_shape), all_values.reshape(head_shape)
    attended, lse = attention_forward(
        queries_heads, keys_heads, values_heads, query_segment, key_segment
    )
    attended = attended.reshape(count, -1)
    branch = sum_tokens(nn(attended, weight_merge))
    residual = own_part(inputs).astype(f32) + (branch + vectors[0])
    scaled_one, inverse_one, normed_one = norm_forward(residual, vectors[1], vectors[2])
    normed_low = gather_tokens(normed_one.astype(bf16))
    pre_gelu = nt(normed_low, weight_expand) + bias_hidden
    hidden = exact_gelu(pre_gelu).astype(bf16)
    shrunk = sum_tokens(nn(hidden, weight_shrink))
    scaled_two, inverse_two, final = norm_forward(
        normed_one + (shrunk + vectors[3]), vectors[4], vectors[5]
    )

    live = (own_part(query_segment) != 0).astype(f32)[:, None]
    upstream = to_own_tokens(cotangent).astype(f32) * live
    grad_sum_two, grad_gain_two, grad_shift_two = norm_backward(
        upstream, scaled_two, inverse_two, vectors[4]
    )
    grad_shrunk_own = grad_sum_two.astype(bf16)
    grad_shrunk = gather_tokens(grad_shrunk_own)
    grad_hidden = nt(grad_shrunk, weight_shrink)
    grad_pre = jax.vjp(exact_gelu, pre_gelu)[1](grad_hidden)[0].astype(bf16)
    grad_normed = grad_sum_two + sum_tokens(nn(grad_pre, weight_expand))
    grad_res, grad_gain_one, grad_shift_one = norm_backward(
        grad_normed, scaled_one, inverse_one, vectors[1]
    )
    grad_branch_own = grad_res.astype(bf16)
    grad_branch = gather_tokens(grad_branch_own)
    grad_attended = nt(grad_branch, weight_merge).astype(bf16)
    late_out, late_res, grad_attended = lax.optimization_barrier(
        (final.astype(bf16), grad_res, grad_attended)
    )
    layer_out, grad_res_columns = to_own_features(late_out), to_own_features(late_res)
    grad_queries, grad_keys, grad_values = attention_backward(
        queries_heads,
        keys_heads,
        values_heads,
        query_segment,
        key_segment,
        lse,
        grad_attended.reshape(head_shape),
    )
    grad_queries = grad_queries.reshape(count, -1)
    grad_keys_values = jnp.concatenate(
        (grad_keys.reshape(-1, heads * HEAD), grad_values.reshape(-1, heads * HEAD)), 1
    )
    grad_keys_values = grad_keys_values.astype(bf16)
    grad_keys, grad_values = (
        grad_keys_values[:, : heads * HEAD],
        grad_keys_values[:, heads * HEAD :],
    )
    grad_entry = (
        nn(grad_queries, weight_queries)
        + nn(grad_keys, weight_keys)
        + nn(grad_values, weight_values)
    )
    grad_tokens = sum_features(grad_entry, grad_res_columns)

    def assemble(local, row_axis, col_axis):
        full = jnp.zeros((local.shape[0], local.shape[1] * rows, D), bf16)
        full = lax.dynamic_update_slice(
            full, local.astype(bf16), (0, row * local.shape[1], 0)
        )
        full = lax.psum_scatter(full, "row", scatter_dimension=2, tiled=True)
        full = lax.psum_scatter(full, "col", scatter_dimension=1, tiled=True)
        return lax.psum(full, ("outer", "core")).astype(f32)

    grad_triple = assemble(
        jnp.stack(
            (tn(grad_queries, inputs), tn(grad_keys, inputs), tn(grad_values, inputs))
        ),
        0,
        2,
    ).transpose(2, 0, 1)
    grad_merge = assemble(tn(attended, grad_branch)[None], 1, 0)[0]
    grad_expand = assemble(tn(grad_pre, normed_low)[None], 0, 1)[0].T
    grad_shrink = assemble(tn(hidden, grad_shrunk)[None], 1, 0)[0]

    def column_sums(values):
        return jnp.sum(values, axis=0, dtype=f32)

    sum_hidden = column_sums(grad_pre)
    sum_queries, sum_values = column_sums(grad_queries), column_sums(grad_values)
    sum_rows = jnp.stack(
        (
            column_sums(grad_branch_own),
            grad_gain_one,
            grad_shift_one,
            column_sums(grad_shrunk_own),
            grad_gain_two,
            grad_shift_two,
        )
    )
    everywhere = ("outer", "core", "col")
    row_totals = lax.psum_scatter(sum_rows, "row", scatter_dimension=1, tiled=True)
    row_totals = lax.psum(row_totals, everywhere)

    def whole(local):
        full = jnp.zeros(local.shape[:-1] + (local.shape[-1] * rows,), f32)
        full = lax.dynamic_update_slice_in_dim(full, local, row * local.shape[-1], -1)
        full = lax.psum(full, everywhere + ("row",))
        share = full.shape[-1] // cols
        return lax.dynamic_slice_in_dim(full, col * share, share, -1)

    grad_pair = whole(jnp.stack((sum_queries, sum_values)))
    grad_expand_bias = whole(sum_hidden)

    return (
        layer_out,
        grad_tokens,
        grad_triple,
        grad_pair,
        grad_merge,
        row_totals[0],
        row_totals[1],
        row_totals[2],
        grad_expand,
        grad_expand_bias,
        grad_shrink,
        row_totals[3],
        row_totals[4],
        row_totals[5],
    )


def shards(tokens, *others):
    sizes = [size(axis) for axis in ("outer", "core", "row", "col")]
    if sizes == [2, 2, 2, 4] and 2 * tokens.shape[0] == LEN:
        return layer(tokens, *others)
    return layer_anywhere(tokens, *others)


def solution(mesh):
    sizes = mesh.shape
    axes = ("outer", "core", "row", "col")
    split = Mesh(
        mesh.devices.reshape(sizes["dp"] // 2, 2, sizes["row"], sizes["col"]), axes
    )
    dp = ("outer", "core")
    activations = P(("outer", "core", "col"), "row")
    return jax.shard_map(
        shards,
        mesh=split,
        in_specs=(
            activations,
            P(dp),
            P("row", None, "col"),
            P(None, "col"),
            P("col", "row"),
            P("row"),
            P("row"),
            P("row"),
            P("row", "col"),
            P("col"),
            P("col", "row"),
            P("row"),
            P("row"),
            P("row"),
            activations,
        ),
        out_specs=(
            activations,
            activations,
            P("row", None, "col"),
            P(None, "col"),
            P("col", "row"),
            P("row"),
            P("row"),
            P("row"),
            P("row", "col"),
            P("col"),
            P("col", "row"),
            P("row"),
            P("row"),
            P("row"),
        ),
        check_vma=False,
    )
```

```python
import functools

import jax
import jax.numpy as jnp
from jax import lax
from jax.experimental import pallas as pl
from jax.experimental.pallas import tpu as pltpu
from jax.sharding import Mesh, PartitionSpec as P

D = 1024
HEAD = 64
LEN = 1024
epsilon = 1e-05
masked_score = -1e30
bf16 = jnp.bfloat16
f32 = jnp.float32


def size(axis):
    return lax.axis_size(axis)


def place(axis):
    return lax.axis_index(axis)


def pair(values, axis):
    return lax.ppermute(values, axis, [(0, 1), (1, 0)])


def after(values, *others):
    return lax.optimization_barrier((values,) + others)[0]


def together(*arrays):
    return lax.optimization_barrier(arrays)


def shift(values, step):
    count = size("col")
    return lax.ppermute(values, "col", [(i, (i + step) % count) for i in range(count)])


def across(values, bits):
    return lax.ppermute(values, "col", [(i, i ^ bits) for i in range(size("col"))])


def by_place(bit, own, other, axis):
    return jnp.where(
        bit == 0,
        jnp.concatenate((own, other), axis),
        jnp.concatenate((other, own), axis),
    )


def nt(left, right, kind=f32):
    return lax.dot_general(
        left, right, (((1,), (1,)), ((), ())), preferred_element_type=f32
    ).astype(kind)


def nn(left, right, kind=f32):
    return lax.dot_general(
        left, right, (((1,), (0,)), ((), ())), preferred_element_type=f32
    ).astype(kind)


def tn(left, right, kind=f32):
    return lax.dot_general(
        left, right, (((0,), (0,)), ((), ())), preferred_element_type=f32
    ).astype(kind)


def swap_sequences(values):
    count = size("col")
    perm = []
    for core in range(2):
        for col in range(count):
            half, other = col % 2, col - col % 2
            target = (half, other + core)
            perm.append((core * count + col, target[0] * count + target[1]))
    return lax.ppermute(values, ("core", "col"), perm)


def own_first(values):
    if size("row") != 2:
        return values
    half = values.shape[0] // 2
    return jnp.where(place("row") == 0, values, jnp.roll(values, half, axis=0))


def own_part(values):
    share = values.shape[0] // size("row")
    if size("row") == 2:
        return values[:share]
    return lax.dynamic_slice_in_dim(values, place("row") * share, share)


def gather_features(values):
    if size("row") == 2:
        full = by_place(place("row"), values, pair(values, "row"), 1)
        return own_first(full)
    return lax.all_gather(values, "row", axis=1, tiled=True)


def gather_tokens(values):
    if size("row") == 2:
        return jnp.concatenate((values, pair(values, "row")), 0)
    return lax.all_gather(values, "row", axis=0, tiled=True)


def sum_tokens(partial):
    if size("row") == 2:
        share = partial.shape[0] // 2
        return partial[:share] + pair(partial[share:].astype(bf16), "row").astype(f32)
    return lax.psum_scatter(partial, "row", scatter_dimension=0, tiled=True)


def to_own_tokens(values):
    if size("row") == 2:
        bit = place("row")
        ordered = own_first(values)
        share = values.shape[0] // 2
        return by_place(bit, ordered[:share], pair(ordered[share:], "row"), 1)
    return lax.all_to_all(values, "row", 0, 1, tiled=True)


def to_own_features(values):
    if size("row") == 2:
        bit = place("row")
        half = values.shape[1] // 2
        low, high = values[:, :half], values[:, half:]
        own = jnp.where(bit == 0, low, high)
        other = pair(jnp.where(bit == 0, high, low), "row")
        return by_place(bit, own, other, 0)
    return lax.all_to_all(values, "row", 1, 0, tiled=True)


def sum_features(partial, addend):
    if size("row") == 2:
        half = partial.shape[1] // 2
        low, high = partial[:, :half], partial[:, half:]
        bit = place("row")
        got = pair(jnp.where(bit == 0, high, low).astype(bf16), "row").astype(f32)
        got = jnp.roll(got, partial.shape[0] // 2, axis=0)
        return own_first(jnp.where(bit == 0, low, high) + got) + addend
    return lax.psum_scatter(partial, "row", scatter_dimension=1, tiled=True) + addend


def halves(values):
    middle = values.shape[0] // 2
    return values[:middle], values[middle:]


def three_groups(triple, merge, expand, shrink):
    depth = triple.shape[0]
    heads = triple.transpose(1, 2, 0).reshape(3, 2, 2, 1, HEAD, depth)
    out = merge.reshape(1, 2, 2, 1, HEAD, depth)
    keys_values = jnp.concatenate((heads[1], heads[2]), 3 - 1)
    queries_merge = jnp.concatenate((heads[0], out[0]), 3 - 1)
    attend = jnp.stack((keys_values, queries_merge), 2).reshape(2, 2, 2, 2 * HEAD, depth)
    widen = expand.T.reshape(2, 2, 2, -1, depth)
    narrow = shrink.reshape(2, 2, 2, -1, depth)
    return attend, widen, narrow


def my_quarter(group):
    some = lax.dynamic_index_in_dim(group, place("outer"), 1, keepdims=False)
    return lax.dynamic_index_in_dim(some, place("core"), 1, keepdims=False)


def exchange_rows(quarter):
    bit = place("row")
    mine = jnp.where(bit == 0, quarter[0], quarter[1])
    other = pair(jnp.where(bit == 0, quarter[1], quarter[0]), "row")
    return by_place(bit, mine, other, 1)


STEPS = (1, 3, 2)
BACK = (2, 1, 3)


def own_core_half(parts, pairs):
    count = size("col")
    return jnp.stack(
        [jnp.stack([group[step] for step in range(count)]) for group in (parts, pairs)]
    )


def gather_attend(quarter):
    parts = {0: quarter}
    for step in STEPS:
        parts[step] = shift(quarter, step)
    pairs = {step: pair(parts[step], "outer") for step in (0,) + STEPS}
    return own_core_half(parts, pairs), parts[2], pairs[2]


def collect_row(last):
    bit = place("row")
    half = last.shape[1] // 2
    low, high = last[:, :half].astype(bf16), last[:, half:].astype(bf16)
    mine = jnp.where(bit == 0, low, high)
    got = pair(jnp.where(bit == 0, high, low), "row")
    return jnp.stack((jnp.where(bit == 0, mine, got), jnp.where(bit == 0, got, mine)))


def ungroup(attend):
    depth = attend.shape[-1]
    heads = attend.reshape(4, 2, 2, HEAD, depth)
    keys, values = heads[:, 0, 0], heads[:, 0, 1]
    queries, merge = heads[:, 1, 0], heads[:, 1, 1]
    triple = jnp.stack((queries, keys, values)).reshape(3, 4 * HEAD, depth).transpose(2, 0, 1)
    return triple, merge.reshape(4 * HEAD, depth)


def flip(values, axis, bit):
    return jnp.where(bit == 0, values, jnp.flip(values, axis))


def dot(left, right, left_dim, right_dim):
    return lax.dot_general(
        left, right, (((left_dim,), (right_dim,)), ((), ())), preferred_element_type=f32
    )


def params():
    return pltpu.CompilerParams(vmem_limit_bytes=56 << 20)


def anywhere(arrays):
    return [pl.BlockSpec(memory_space=pl.ANY) for _ in arrays]


def pick(near_ref, far_ref, begin):
    part = slice(begin, begin + HEAD)
    return jnp.concatenate((near_ref[:, part], far_ref[:, part]), 0)


def attend_forward_kernel(q_ref, near_ref, far_ref, qs_ref, ks_ref, out_ref, lse_ref):
    same = ks_ref[...] == qs_ref[...]
    for head in range(2):
        part = slice(head * HEAD, (head + 1) * HEAD)
        keys = pick(near_ref, far_ref, 2 * head * HEAD)
        values = pick(near_ref, far_ref, (2 * head + 1) * HEAD)
        queries = q_ref[:, part] * jnp.asarray(HEAD**-0.5, bf16)
        scores = jnp.where(same, dot(keys, queries, 1, 1), masked_score)
        top = jnp.max(scores, axis=0, keepdims=True)
        weights = jnp.exp(scores - top)
        total = jnp.sum(weights, axis=0, keepdims=True)
        low = (weights * (1.0 / total)).astype(bf16)
        out_ref[part] = dot(values, low, 0, 0).astype(bf16)
        lse_ref[0, head : head + 1] = top + jnp.log(total)


def attend_forward(queries, near, far, query_segment, key_segment):
    tokens, width = queries.shape
    steps = width // (2 * HEAD)
    block = pl.BlockSpec((tokens, 4 * HEAD), lambda i: (0, i))
    return pl.pallas_call(
        attend_forward_kernel,
        grid=(steps,),
        in_specs=[
            pl.BlockSpec((tokens, 2 * HEAD), lambda i: (0, i)),
            block,
            block,
            pl.BlockSpec((1, tokens), lambda i: (0, 0)),
            pl.BlockSpec((2 * tokens, 1), lambda i: (0, 0)),
        ],
        out_specs=[
            pl.BlockSpec((2 * HEAD, tokens), lambda i: (i, 0)),
            pl.BlockSpec((1, 2, tokens), lambda i: (i, 0, 0)),
        ],
        out_shape=[
            jax.ShapeDtypeStruct((width, tokens), bf16),
            jax.ShapeDtypeStruct((steps, 2, tokens), f32),
        ],
        compiler_params=params(),
        cost_estimate=pl.CostEstimate(
            flops=32 * tokens * tokens * width,
            bytes_accessed=4 << 20,
            transcendentals=2 * tokens * tokens * width // HEAD,
        ),
    )(queries, near, far, query_segment, key_segment)


def attend_backward_kernel(
    q_ref, kv_ref, far_kv_ref, g_ref, qs_ref, ks_ref, lse_ref, dq_ref, near_ref, far_ref
):
    same = ks_ref[...] == qs_ref[...]
    scale = HEAD**-0.5
    near = near_ref.shape[0]
    for head in range(2):
        part = slice(head * HEAD, (head + 1) * HEAD)
        key_part = slice(2 * head * HEAD, (2 * head + 1) * HEAD)
        value_part = slice((2 * head + 1) * HEAD, (2 * head + 2) * HEAD)
        keys = pick(kv_ref, far_kv_ref, key_part.start)
        values = pick(kv_ref, far_kv_ref, value_part.start)
        queries = q_ref[:, part] * jnp.asarray(scale, bf16)
        grad = g_ref[:, part]
        scores = jnp.where(same, dot(keys, queries, 1, 1), masked_score)
        weights = jnp.exp(scores - lse_ref[0, head : head + 1])
        grad_weights = dot(values, grad, 1, 1)
        inner = jnp.sum(weights * grad_weights, axis=0, keepdims=True)
        grad_scores = (weights * (grad_weights - inner)).astype(bf16)
        dq_ref[part] = (dot(keys, grad_scores, 0, 0) * scale).astype(bf16)
        grad_keys = dot(grad_scores, queries, 1, 0)
        grad_values = dot(weights.astype(bf16), grad, 1, 0)
        near_ref[:, key_part], far_ref[:, key_part] = grad_keys[:near], grad_keys[near:]
        near_ref[:, value_part], far_ref[:, value_part] = grad_values[:near], grad_values[near:]


def attend_backward(queries, near, far, grad, query_segment, key_segment, lse, begin, steps):
    tokens = queries.shape[0]
    block = pl.BlockSpec((tokens, 4 * HEAD), lambda i: (0, begin + i))
    query_block = pl.BlockSpec((tokens, 2 * HEAD), lambda i: (0, begin + i))
    key_block = pl.BlockSpec((tokens, 4 * HEAD), lambda i: (0, i))
    return pl.pallas_call(
        attend_backward_kernel,
        grid=(steps,),
        in_specs=[
            query_block,
            block,
            block,
            query_block,
            pl.BlockSpec((1, tokens), lambda i: (0, 0)),
            pl.BlockSpec((2 * tokens, 1), lambda i: (0, 0)),
            pl.BlockSpec((1, 2, tokens), lambda i: (begin + i, 0, 0)),
        ],
        out_specs=[pl.BlockSpec((2 * HEAD, tokens), lambda i: (i, 0)), key_block, key_block],
        out_shape=[
            jax.ShapeDtypeStruct((2 * HEAD * steps, tokens), bf16),
            jax.ShapeDtypeStruct((tokens, 4 * HEAD * steps), f32),
            jax.ShapeDtypeStruct((tokens, 4 * HEAD * steps), f32),
        ],
        compiler_params=params(),
        cost_estimate=pl.CostEstimate(
            flops=160 * tokens * tokens * steps * HEAD,
            bytes_accessed=8 << 20,
            transcendentals=4 * tokens * tokens * steps,
        ),
    )(queries, near, far, grad, query_segment, key_segment, lse)


def attend_weights_kernel(
    which_ref, dkv_ref, dq_ref, out_in_ref, x_ref, g_ref, *rest, added, cols
):
    add_ref = rest[0] if added else None
    out_refs = rest[-cols:]

    def put(rows, value):
        value = value.reshape(cols, -1, D)
        for step, out_ref in enumerate(out_refs):
            term = value[step]
            if added:
                term = term + add_ref[0, step, rows].astype(f32)
            out_ref[rows] = term.astype(out_ref.dtype)

    @pl.when(which_ref[0] == 0)
    def _():
        put(slice(0, 2 * HEAD), dot(dkv_ref[...], x_ref[...], 0, 0))

    @pl.when(which_ref[0] == 1)
    def _():
        put(slice(0, HEAD), dot(dq_ref[...], x_ref[...], 1, 0))
        put(slice(HEAD, 2 * HEAD), dot(out_in_ref[...], g_ref[...], 1, 0))


def attend_weights(which, dkv, dq, out_in, x, g, begin, cols, kind, add=None, earlier=()):
    tokens = x.shape[0]
    full = pl.BlockSpec((tokens, D), lambda i, w: (0, 0))
    rows = pl.BlockSpec((cols * HEAD, tokens), lambda i, w: (begin, 0))
    specs = [pl.BlockSpec((tokens, cols * 2 * HEAD), lambda i, w: (0, begin)), rows, rows, full, full]
    given = [dkv, dq, out_in, x, g]
    if add is not None:
        specs.append(pl.BlockSpec((1, cols, 2 * HEAD, D), lambda i, w: (begin, 0, 0, 0)))
        given.append(add)
    return pl.pallas_call(
        functools.partial(attend_weights_kernel, added=add is not None, cols=cols),
        grid_spec=pltpu.PrefetchScalarGridSpec(
            num_scalar_prefetch=1,
            grid=(1,),
            in_specs=specs + anywhere(earlier),
            out_specs=[pl.BlockSpec((2 * HEAD, D), lambda i, w: (0, 0))] * cols,
        ),
        out_shape=[jax.ShapeDtypeStruct((2 * HEAD, D), kind)] * cols,
        compiler_params=params(),
        cost_estimate=pl.CostEstimate(
            flops=4 * tokens * D * cols * HEAD, bytes_accessed=6 << 20, transcendentals=0
        ),
    )(which, *given, *earlier)


def attend_far_kernel(which_ref, dkv_ref, dq_ref, out_in_ref, x_ref, g_ref, *rest):
    out_ref = rest[-1]
    cols = out_ref.shape[1]

    @pl.when(which_ref[0] == 0)
    def _():
        value = dot(dkv_ref[...], x_ref[...], 0, 0)
        out_ref[0] = value.reshape(cols, 2 * HEAD, D).astype(out_ref.dtype)

    @pl.when(which_ref[0] == 1)
    def _():
        for part, value in enumerate(
            (dot(dq_ref[...], x_ref[...], 1, 0), dot(out_in_ref[...], g_ref[...], 1, 0))
        ):
            rows = slice(part * HEAD, (part + 1) * HEAD)
            out_ref[0, :, rows] = value.reshape(cols, HEAD, D).astype(out_ref.dtype)


def attend_far_weights(which, dkv, dq, out_in, x, g, cols, *earlier):
    tokens = x.shape[0]
    full = pl.BlockSpec((tokens, D), lambda i, w: (0, 0))
    rows = pl.BlockSpec((cols * HEAD, tokens), lambda i, w: (i, 0))
    return pl.pallas_call(
        attend_far_kernel,
        grid_spec=pltpu.PrefetchScalarGridSpec(
            num_scalar_prefetch=1,
            grid=(2,),
            in_specs=[
                pl.BlockSpec((tokens, cols * 2 * HEAD), lambda i, w: (0, i)), rows, rows, full, full
            ]
            + anywhere(earlier),
            out_specs=pl.BlockSpec((1, cols, 2 * HEAD, D), lambda i, w: (i, 0, 0, 0)),
        ),
        out_shape=jax.ShapeDtypeStruct((2, cols, 2 * HEAD, D), bf16),
        compiler_params=params(),
        cost_estimate=pl.CostEstimate(
            flops=8 * tokens * D * cols * HEAD, bytes_accessed=6 << 20, transcendentals=0
        ),
    )(which, dkv, dq, out_in, x, g, *earlier)


SPARE = 8


def units_of(weights):
    units = (weights.shape[2] - SPARE) // 2
    expand = weights[:, :, :units].reshape(-1, D)
    shrink = weights[:, :, units : 2 * units].reshape(-1, D)
    return expand, shrink


def finish(total, keep_ref, send_ref):
    @pl.when(pl.program_id(0) == pl.num_programs(0) - 1)
    def _():
        half = total.shape[0] // 2
        keep_ref[...] = total[:half]
        send_ref[...] = total[half:].astype(bf16)


def add_to(total, term):
    @pl.when(pl.program_id(0) == 0)
    def _():
        total[...] = term

    @pl.when(pl.program_id(0) > 0)
    def _():
        total[...] += term


def hidden_forward_kernel(
    x_ref, bias_ref, weights_ref, hidden_ref, slope_ref, keep_ref, send_ref, total
):
    expand, shrink = units_of(weights_ref[0, 0:1])
    u = dot(x_ref[...], expand, 1, 1) + bias_ref[0]
    normal = 0.5 * (1.0 + lax.erf(u * (0.5**0.5)))
    slope_ref[...] = normal + u * (jnp.exp(-0.5 * u * u) * ((0.5 / jnp.pi) ** 0.5))
    hidden = (u * normal).astype(bf16)
    hidden_ref[...] = hidden
    add_to(total, dot(hidden, shrink, 1, 0))
    finish(total, keep_ref, send_ref)


def hidden_specs(tokens, weights):
    outer, core, cols, rows, _ = weights.shape
    units = (rows - SPARE) // 2
    steps, width = outer * core, cols * units
    block = pl.BlockSpec((1, 1, cols, rows, D), lambda i: (i // core, i % core, 0, 0, 0))
    wide = pl.BlockSpec((tokens, width), lambda i: (0, i))
    half = pl.BlockSpec((tokens // 2, D), lambda i: (0, 0))
    half_shapes = [
        jax.ShapeDtypeStruct((tokens // 2, D), f32),
        jax.ShapeDtypeStruct((tokens // 2, D), bf16),
    ]
    full = pl.BlockSpec((tokens, D), lambda i: (0, 0))
    row = pl.BlockSpec((1, 1, width), lambda i: (i, 0, 0))
    cost = pl.CostEstimate(
        flops=4 * tokens * D * steps * width, bytes_accessed=20 << 20, transcendentals=0
    )
    return steps, width, block, wide, half, half_shapes, full, row, cost


def hidden_forward(x, weights, bias):
    tokens = x.shape[0]
    steps, width, block, wide, half, half_shapes, full, row, cost = hidden_specs(tokens, weights)
    shape = (tokens, steps * width)
    return pl.pallas_call(
        hidden_forward_kernel,
        grid=(steps,),
        in_specs=[full, row, block],
        out_specs=[wide, wide, half, half],
        out_shape=[jax.ShapeDtypeStruct(shape, bf16), jax.ShapeDtypeStruct(shape, f32)]
        + half_shapes,
        scratch_shapes=[pltpu.VMEM((tokens, D), f32)],
        compiler_params=params(),
        cost_estimate=cost,
    )(x, bias, weights)


def hidden_backward_kernel(
    g_ref, slope_ref, weights_ref, grad_ref, sum_ref, keep_ref, send_ref, total
):
    expand, shrink = units_of(weights_ref[0, 0:1])
    grad = (dot(g_ref[...], shrink, 1, 1) * slope_ref[...]).astype(bf16)
    grad_ref[...] = grad
    sum_ref[0] = jnp.sum(grad.astype(f32), axis=0, keepdims=True)
    add_to(total, dot(grad, expand, 1, 0))
    finish(total, keep_ref, send_ref)


def hidden_backward(g, weights, slope):
    tokens = g.shape[0]
    steps, width, block, wide, half, half_shapes, full, row, cost = hidden_specs(tokens, weights)
    return pl.pallas_call(
        hidden_backward_kernel,
        grid=(steps,),
        in_specs=[full, wide, block],
        out_specs=[wide, row, half, half],
        out_shape=[
            jax.ShapeDtypeStruct((tokens, steps * width), bf16),
            jax.ShapeDtypeStruct((steps, 1, width), f32),
        ]
        + half_shapes,
        scratch_shapes=[pltpu.VMEM((tokens, D), f32)],
        compiler_params=params(),
        cost_estimate=cost,
    )(g, slope, weights)


def hidden_weights_kernel(grad_ref, hidden_ref, x_ref, g_ref, sum_ref, out_ref):
    cols, rows, _ = out_ref.shape[2:]
    units = (rows - SPARE) // 2
    for part, (left, right) in enumerate(((grad_ref, x_ref), (hidden_ref, g_ref))):
        value = dot(left[...], right[...], 0, 0).reshape(cols, units, D)
        out_ref[0, 0, :, part * units : (part + 1) * units] = value.astype(bf16)
    first = lax.broadcasted_iota(jnp.int32, (cols, SPARE, units), 1) == 0
    sums = jnp.where(first, sum_ref[0][:, None, :], 0.0).astype(bf16)
    out_ref[0, 0, :, 2 * units :] = jnp.zeros((cols, SPARE, D), bf16)
    for begin in (0, D // 2):
        out_ref[0, 0, :, 2 * units :, begin : begin + units] = sums


def hidden_weights(grad, hidden, x, g, sums, shape):
    tokens = x.shape[0]
    outer, core, cols, rows, _ = shape
    width = grad.shape[1] // (outer * core)
    wide = pl.BlockSpec((tokens, width), lambda i: (0, i))
    full = pl.BlockSpec((tokens, D), lambda i: (0, 0))
    return pl.pallas_call(
        hidden_weights_kernel,
        grid=(outer * core,),
        in_specs=[
            wide, wide, full, full, pl.BlockSpec((1, cols, width // cols), lambda i: (i, 0, 0))
        ],
        out_specs=pl.BlockSpec(
            (1, 1, cols, rows, D), lambda i: (i // core, i % core, 0, 0, 0)
        ),
        out_shape=jax.ShapeDtypeStruct(shape, bf16),
        compiler_params=params(),
        cost_estimate=pl.CostEstimate(
            flops=4 * tokens * D * grad.shape[1], bytes_accessed=16 << 20, transcendentals=0
        ),
    )(grad, hidden, x, g, sums)


def layer(
    tokens, segments, triple_weight, pair_bias, merge_weight, merge_bias, first_gain, first_shift,
    expand_weight, expand_bias, shrink_weight, shrink_bias, second_gain, second_shift, cotangent,
):
    cols = size("col")
    count = tokens.shape[0]
    own = count // 2
    heads = D // HEAD // 2
    row, col, core, outer = place("row"), place("col"), place("core"), place("outer")
    row_size, pair_size, hidden_size = merge_bias.shape[0], pair_bias.shape[1], expand_bias.shape[0]

    step_of = lax.optimization_barrier
    groups = three_groups(triple_weight, merge_weight, expand_weight, shrink_weight)
    attend_group = my_quarter(groups[0])
    row_vectors = jnp.stack(
        (merge_bias, first_gain, first_shift, shrink_bias, second_gain, second_shift)
    )
    column = jnp.concatenate(
        [
            lax.dynamic_slice_in_dim(vector, row * (vector.shape[0] // 2), vector.shape[0] // 2)
            for vector in (pair_bias[0], pair_bias[1], expand_bias)
        ]
    )
    moved = swap_sequences(tokens)
    quarter = exchange_rows(attend_group)
    pair_column, hidden_column = column[:pair_size], column[pair_size:].reshape(4, -1)
    pair_column = pair_column.reshape(2, 2, HEAD)
    pair_column = lax.dynamic_index_in_dim(pair_column, outer, 1, keepdims=False)
    pair_column = lax.dynamic_index_in_dim(pair_column, 1 - core, 0)
    moved_cotangent = swap_sequences(cotangent)
    hidden_column = lax.dynamic_index_in_dim(hidden_column, 2 * outer + core, 0)
    v = step_of(
        dict(
            quarter=quarter, moved=moved, other=segments.astype(f32), rows=row_vectors, pairs=pair_column,
            hidden=hidden_column, cot=moved_cotangent,
        )
    )

    def beside(rows, value):
        spare = jnp.pad(value, ((0, SPARE - 1), (0, D - value.shape[1])))
        return jnp.concatenate((rows, spare), 0)

    quarter, moved = beside(v["quarter"], v["pairs"]), v["moved"]
    parts = {0: quarter, 1: shift(quarter, 1), 3: shift(quarter, 3)}
    pairs = {0: pair(quarter, "outer")}
    got_tokens = pair(moved, "row")
    other_group = jnp.concatenate([my_quarter(group) for group in groups[1:]], 1)
    v.update(
        quarter=quarter, parts=parts, pairs=pairs, moved=moved, got=got_tokens, group=other_group
    )
    v = step_of(v)
    parts, pairs, quarter = v["parts"], v["pairs"], v["quarter"]
    parts[2] = shift(quarter, 2)
    pairs[1], pairs[3] = pair(parts[1], "outer"), pair(parts[3], "outer")
    v["inputs"] = own_first(by_place(row, v["moved"], v["got"], 1))
    v["vectors"] = by_place(row, v["rows"], pair(v["rows"], "row"), 1)
    v["other"] = pair(v["other"], "core")
    v["group"] = exchange_rows(v["group"])
    v = step_of(v)
    parts, pairs = v["parts"], v["pairs"]
    pairs[2] = pair(parts[2], "outer")
    mine = beside(v["group"], v["hidden"])
    hidden_all = lax.all_gather(mine, ("outer", "core", "col"), axis=0)
    hidden_all = hidden_all.reshape(2, 2, cols, -1, D)
    v = step_of(v)
    parts, pairs = v["parts"], v["pairs"]
    rows = 2 * HEAD

    def without(group):
        return {step: group[step][:rows] for step in range(cols)}

    attend_own = own_core_half(without(parts), without(pairs))
    v["attend_own"], v["attend_other"] = attend_own, pair(attend_own, "core")
    bias_own = jnp.stack(
        [group[step][rows, :HEAD] for group in (parts, pairs) for step in range(cols)]
    ).astype(f32)
    v["bias_own"], v["bias_other"] = bias_own, pair(bias_own, "core")
    other = v["other"].astype(jnp.int32)
    sequence = lax.dynamic_slice_in_dim(
        jnp.where(col % 2 == core, segments, other), (col // 2) * LEN, LEN
    ).reshape(2, count)
    query_segment = own_first(lax.dynamic_index_in_dim(sequence, core, 0, keepdims=False))
    far_segment = own_first(lax.dynamic_index_in_dim(sequence, 1 - core, 0, keepdims=False))
    key_segment = jnp.concatenate((query_segment, far_segment))
    segment_row, segment_column = query_segment[None], key_segment[:, None]
    vectors = v["vectors"].astype(f32)
    v = step_of(
        dict(
            own=v["attend_own"], other=v["attend_other"], cot=v["cot"], inputs=v["inputs"],
            vectors=vectors, biases=(v["bias_own"], v["bias_other"]),
        )
    )
    attend_own, attend_other, inputs, vectors = v["own"], v["other"], v["inputs"], v["vectors"]
    first = jnp.where(core == 0, attend_own, attend_other)
    second = jnp.where(core == 0, attend_other, attend_own)
    bias_values = jnp.where(core == 0, v["biases"][0], v["biases"][1])
    bias_keys_values = jnp.stack((jnp.zeros_like(bias_values), bias_values), 1).reshape(-1)
    bias_queries = jnp.where(core == 0, v["biases"][1], v["biases"][0]).reshape(-1)
    weight_keys_values = first.reshape(-1, D)
    second = second.reshape(heads, 2, HEAD, D)
    weight_queries, weight_merge = second[:, 0].reshape(-1, D), second[:, 1].reshape(-1, D)

    cut = heads * HEAD // 2
    steps = heads // 4
    keys_values = (nt(inputs, weight_keys_values) + bias_keys_values).astype(bf16)
    v["far"] = pair(keys_values, "core")
    v["queries"] = (nt(inputs, weight_queries) + bias_queries).astype(bf16)
    v["keys_values"] = keys_values
    v["weights"] = (weight_keys_values, weight_queries, weight_merge)
    v = step_of(v)
    queries = v["queries"]
    keys_values, far_keys_values = v["keys_values"], v["far"]
    v["attended"], v["lse"] = attend_forward(
        queries, keys_values, far_keys_values, segment_row, segment_column
    )
    v["upstream"] = to_own_tokens(v["cot"])
    v = step_of(v)
    attended, lse = v["attended"], v["lse"]
    queries, keys_values, far_keys_values = v["queries"], v["keys_values"], v["far"]
    weight_keys_values, weight_queries, weight_merge = v["weights"]
    branch = sum_tokens(tn(attended, weight_merge))
    residual = inputs[:own].astype(f32) + (branch + vectors[0])
    scaled_one, inverse_one, normed_one = norm_forward(residual, vectors[1], vectors[2])
    normed_low = gather_tokens(normed_one.astype(bf16))
    normed_low, normed_one, hidden_all = step_of((normed_low, normed_one, hidden_all))
    units = hidden_size // 8
    bias_hidden = hidden_all[:, :, :, 2 * units, :units].reshape(4, 1, -1).astype(f32)
    upstream = v["upstream"]

    hidden, slope, keep, send = hidden_forward(normed_low, hidden_all, bias_hidden)
    shrunk = keep + pair(send, "row").astype(f32)
    scaled_two, inverse_two, final = norm_forward(
        normed_one + (shrunk + vectors[3]), vectors[4], vectors[5]
    )
    live = (query_segment[:own] != 0).astype(f32)[:, None]
    upstream = upstream.astype(f32) * live
    grad_sum_two, grad_gain_two, grad_shift_two = norm_backward(
        upstream, scaled_two, inverse_two, vectors[4]
    )
    grad_shrunk_own = grad_sum_two.astype(bf16)
    grad_shrunk = gather_tokens(grad_shrunk_own)
    grad_pre, sum_hidden, keep, send = hidden_backward(grad_shrunk, hidden_all, slope)
    cut = heads * HEAD // 2
    steps = heads // 4
    spare = sum_hidden.reshape(4, cols, units)
    v = dict(
        grad_pre=grad_pre, hidden=hidden, normed=normed_low, g=grad_shrunk, inputs=inputs,
        attended=attended, queries=queries, keys_values=keys_values, lse=lse,
        far_keys_values=far_keys_values, keep=keep, send=send, sum_two=grad_sum_two,
        scaled_one=scaled_one, inverse_one=inverse_one, final=final, shrunk_own=grad_shrunk_own,
        sum_two_rows=(grad_gain_two, grad_shift_two), spare=spare, vectors=vectors,
        weight_merge=weight_merge, weight_queries=weight_queries,
        weight_keys_values=weight_keys_values,
    )

    v = step_of(v)
    v["got"] = pair(v["send"], "row")
    hidden_grads = hidden_weights(
        v["grad_pre"], v["hidden"], v["normed"], v["g"], v["spare"], hidden_all.shape
    )
    v["hidden_grads"] = hidden_grads
    v = step_of(v)
    hidden_sums = lax.psum_scatter(
        v["hidden_grads"].reshape(-1, D), ("outer", "core", "col"), scatter_dimension=0, tiled=True
    )
    grad_normed = v["sum_two"] + (v["keep"] + v["got"].astype(f32))
    res, grad_gain_one, grad_shift_one = norm_backward(
        grad_normed, v["scaled_one"], v["inverse_one"], v["vectors"][1]
    )
    branch_own = res.astype(bf16)
    branch_got = pair(branch_own, "row")
    sum_rows = jnp.stack(
        (
            jnp.sum(branch_own, axis=0, dtype=f32),
            grad_gain_one,
            grad_shift_one,
            jnp.sum(v["shrunk_own"], axis=0, dtype=f32),
            *v["sum_two_rows"],
        )
    )
    names = (
        "inputs", "attended", "queries", "keys_values", "far_keys_values", "lse", "final",
        "weight_merge", "weight_queries", "weight_keys_values",
    )
    v = {name: v[name] for name in names}
    v["branch"] = jnp.concatenate((branch_own, branch_got), 0)
    v["grad_attended"] = nt(v["branch"], v["weight_merge"], bf16)
    v["res"], v["sum_rows"] = res, sum_rows
    v["out"] = v["final"].astype(bf16)
    v = step_of(v)
    shared = (
        v["queries"], v["keys_values"], v["far_keys_values"], v["grad_attended"], segment_row,
        segment_column, v["lse"],
    )
    v["second"] = attend_backward(*shared, steps, steps)
    v["out"] = to_own_features(v["out"])
    v = step_of(v)
    shared = (
        v["queries"], v["keys_values"], v["far_keys_values"], v["grad_attended"], segment_row,
        segment_column, v["lse"],
    )
    v["far"] = pair(v["second"][2], "core")
    v["first"] = attend_backward(*shared, 0, steps)
    middle = D // 2
    res_low, res_high = v["res"][:, :middle], v["res"][:, middle:]
    v["res_mine"] = jnp.where(row == 0, res_low, res_high)
    v["res_send"] = halves(jnp.where(row == 0, res_high, res_low))
    v["res_got"] = [pair(v["res_send"][0], "row")]
    v = step_of(v)
    far = pair(v["first"][2], "core")
    dkv_second = (v["second"][1] + v["far"]).astype(bf16)
    v["grad_queries"] = jnp.concatenate((v["first"][0], v["second"][0]), 0)
    v["entry"] = tn(v["grad_queries"], v["weight_queries"])
    dkv_first = (v["first"][1] + far).astype(bf16)
    v["grad_keys_values"] = jnp.concatenate((dkv_first, dkv_second), 1)
    v = step_of(v)
    which = core.reshape(1)
    part = (v["grad_keys_values"], v["grad_queries"], v["attended"], v["inputs"], v["branch"])
    v["far"] = attend_far_weights((1 - core).reshape(1), *part, cols)
    v["res_got"].append(pair(v["res_send"][1], "row"))
    v = step_of(v)
    v["far"] = pair(v["far"], "core")
    entry = v["entry"] + nn(v["grad_keys_values"], v["weight_keys_values"])
    v["res_columns"] = by_place(row, v["res_mine"], jnp.concatenate(v["res_got"], 0), 0)
    v["entry_keep"] = jnp.where(row == 0, entry[:, :middle], entry[:, middle:])
    v["entry_send"] = jnp.where(row == 0, entry[:, middle:], entry[:, :middle]).astype(bf16)
    v = step_of(v)
    part = (v["grad_keys_values"], v["grad_queries"], v["attended"], v["inputs"], v["branch"])
    v["mates"] = attend_weights(which, *part, 1, cols, bf16, v["far"])
    v = step_of(v)
    part = (v["grad_keys_values"], v["grad_queries"], v["attended"], v["inputs"], v["branch"])
    v["got"] = {2: pair(v["mates"][2], "outer")}
    v["entry_got"] = pair(v["entry_send"], "row")
    v["own"] = attend_weights(which, *part, 0, cols, f32, v["far"])
    sum_queries = jnp.sum(v["grad_queries"], axis=1, dtype=f32)
    sum_values = jnp.sum(v["grad_keys_values"], axis=0, dtype=f32).reshape(heads, 2, HEAD)[:, 1]
    sum_pair = jnp.stack((sum_queries, sum_values.reshape(-1))).reshape(2, 2, cols, HEAD)
    sum_pair = flip(sum_pair.transpose(2, 0, 1, 3), 2, outer).reshape(cols, -1)
    length = sum_pair.shape[1]
    sum_pair = jnp.concatenate(
        [
            lax.dynamic_index_in_dim(sum_pair, (col - place_of) % cols, 0, keepdims=False)
            for place_of in range(cols)
        ]
    )
    v["total"] = jnp.concatenate((sum_pair, v["sum_rows"].reshape(-1)))
    v = step_of(v)

    def to_send(sums, got, step):
        return (sums[step] + got.astype(f32)).astype(bf16)

    got = v["got"]
    got[1], got[3] = pair(v["mates"][1], "outer"), pair(v["mates"][3], "outer")
    v["two"] = shift(to_send(v["own"], got[2], 2), -2)
    total = v["total"]
    v["total"] = total + lax.ppermute(total, "col", [(i, i ^ 1) for i in range(cols)])
    entry = jnp.roll(v["entry_got"].astype(f32), own, axis=0)
    v["grad_tokens"] = own_first(v["entry_keep"] + entry) + v["res_columns"]
    v = step_of(v)
    v["one"] = to_send(v["own"], v["got"][1], 1)
    v["three"] = to_send(v["own"], v["got"][3], 3)
    v["hidden_sums"] = hidden_sums
    v = step_of(v)
    v["one"], v["three"] = shift(v["one"], -1), shift(v["three"], -3)
    v["got"][0] = pair(v["mates"][0], "outer")
    total = v["total"]
    v["total"] = total + lax.ppermute(total, "col", [(i, i ^ 2) for i in range(cols)])
    v["block"] = collect_row(v["hidden_sums"])
    v = step_of(v)
    attend_rest = v["own"][0] + v["got"][0].astype(f32)
    for name in ("one", "two", "three"):
        attend_rest = attend_rest + v[name].astype(f32)
    v["attend"] = collect_row(attend_rest)
    v["block_got"] = pair(v["block"], "outer")
    v["total"] = v["total"] + pair(v["total"], "core")
    v["grad_tokens"] = swap_sequences(v["grad_tokens"])
    v = step_of(v)
    v["block"] = by_place(outer, v["block"][:, None], v["block_got"][:, None], 1)
    v = step_of(v)
    v["attend_got"] = pair(v["attend"], "outer")
    v["total_got"] = pair(v["total"], "outer")
    v["block_got"] = pair(v["block"], "core")
    v["out"] = swap_sequences(v["out"])
    v = step_of(v)
    total = v["total"] + v["total_got"]
    layer_out, grad_tokens = v["out"], v["grad_tokens"]
    attend = by_place(outer, v["attend"][:, None], v["attend_got"][:, None], 1)
    attend_got = pair(attend, "core")
    hidden_block = by_place(
        core, v["block"][:, :, None], v["block_got"][:, :, None], 2
    ).astype(f32)
    attend = by_place(core, attend[:, :, None], attend_got[:, :, None], 2).astype(f32)
    grad_triple, grad_merge = ungroup(attend)
    grad_expand = hidden_block[:, :, :, :units].reshape(-1, D // 2).T
    grad_shrink = hidden_block[:, :, :, units : 2 * units].reshape(-1, D // 2)
    grad_expand_bias = hidden_block[:, :, :, 2 * units, :units].reshape(-1)
    mine = lax.dynamic_slice_in_dim(total, col * length, length)
    sum_rows = total[cols * length :].reshape(6, 2, row_size)
    low, high = sum_rows[:, 0].reshape(-1), sum_rows[:, 1].reshape(-1)
    got = pair(jnp.concatenate((mine, jnp.where(row == 0, high, low))), "row")
    totals = (jnp.where(row == 0, low, high) + got[length:]).reshape(6, row_size)
    got = got[:length]
    short = 2 * HEAD
    grad_pair = by_place(
        row, mine[: 2 * short].reshape(2, short), got[: 2 * short].reshape(2, short), 1
    )
    return (
        layer_out, grad_tokens, grad_triple, grad_pair, grad_merge, totals[0], totals[1], totals[2],
        grad_expand, grad_expand_bias, grad_shrink, totals[3], totals[4], totals[5],
    )


def masked(scores, query_segment, key_segment):
    same = query_segment[:, None] == key_segment[None, :]
    return jnp.where(same[None], scores, masked_score)


def attention_forward(queries, keys, values, query_segment, key_segment):
    scores = jnp.einsum("qhd,khd->hqk", queries, keys, preferred_element_type=f32)
    scores = masked(scores * HEAD**-0.5, query_segment, key_segment)
    top = jnp.max(scores, axis=-1, keepdims=True)
    weights = jnp.exp(scores - top)
    total = jnp.sum(weights, axis=-1, keepdims=True)
    low = (weights / total).astype(bf16)
    attended = jnp.einsum("hqk,khd->qhd", low, values, preferred_element_type=f32)
    return attended.astype(bf16), top + jnp.log(total)


def attention_backward(queries, keys, values, query_segment, key_segment, lse, grad):
    scores = jnp.einsum("qhd,khd->hqk", queries, keys, preferred_element_type=f32)
    scores = masked(scores * HEAD**-0.5, query_segment, key_segment)
    weights = jnp.exp(scores - lse)
    grad_weights = jnp.einsum("qhd,khd->hqk", grad, values, preferred_element_type=f32)
    inner = jnp.sum(weights * grad_weights, axis=-1, keepdims=True)
    grad_scores = (weights * (grad_weights - inner)).astype(bf16)
    scale = HEAD**-0.5
    grad_queries = jnp.einsum("hqk,khd->qhd", grad_scores, keys, preferred_element_type=f32) * scale
    grad_keys = jnp.einsum("hqk,qhd->khd", grad_scores, queries, preferred_element_type=f32) * scale
    grad_values = jnp.einsum(
        "hqk,qhd->khd", weights.astype(bf16), grad, preferred_element_type=f32
    )
    return grad_queries.astype(bf16), grad_keys, grad_values


def norm_forward(values, gain, shift):
    center = jnp.mean(values, axis=1, keepdims=True)
    inverse = lax.rsqrt(
        jnp.mean(values * values, axis=1, keepdims=True) - center * center + epsilon
    )
    scaled = (values - center) * inverse
    return scaled, inverse, scaled * gain + shift


def norm_backward(upstream, scaled, inverse, gain):
    through = upstream * gain
    grad = inverse * (
        through
        - jnp.mean(through, axis=1, keepdims=True)
        - scaled * jnp.mean(through * scaled, axis=1, keepdims=True)
    )
    return grad, jnp.sum(upstream * scaled, axis=0), jnp.sum(upstream, axis=0)


def exact_gelu(values):
    return jax.nn.gelu(values, approximate=False)


def layer_anywhere(
    tokens,
    segments,
    triple_weight,
    pair_bias,
    merge_weight,
    merge_bias,
    first_gain,
    first_shift,
    expand_weight,
    expand_bias,
    shrink_weight,
    shrink_bias,
    second_gain,
    second_shift,
    cotangent,
):
    rows, cols = size("row"), size("col")
    count = tokens.shape[0]
    own = count // rows
    heads = D // HEAD // rows
    row, col = place("row"), place("col")

    query_segment = lax.dynamic_slice_in_dim(segments, col * count, count)
    key_segment = query_segment

    row_size, pair_size, hidden_size = merge_bias.shape[0], pair_bias.shape[1], expand_bias.shape[0]
    row_vectors = jnp.stack(
        (merge_bias, first_gain, first_shift, shrink_bias, second_gain, second_shift)
    )
    vectors = lax.all_gather(row_vectors, "row", axis=1, tiled=True)

    def mine_of(full, axis=0):
        share = full.shape[axis] // rows
        return lax.dynamic_slice_in_dim(full, row * share, share, axis)

    bias_pair = mine_of(lax.all_gather(pair_bias, "col", axis=1, tiled=True), 1)
    bias_queries, bias_values = bias_pair[0], bias_pair[1]
    bias_hidden = mine_of(lax.all_gather(expand_bias, "col", axis=0, tiled=True)).astype(f32)
    vectors = vectors.astype(f32)

    triple = lax.all_gather(triple_weight, "col", axis=2, tiled=True)
    triple = lax.all_gather(triple, "row", axis=0, tiled=True).transpose(1, 2, 0)
    merge = lax.all_gather(merge_weight, "col", axis=0, tiled=True)
    merge = lax.all_gather(merge, "row", axis=1, tiled=True)
    expand = lax.all_gather(expand_weight, "col", axis=1, tiled=True)
    expand = lax.all_gather(expand, "row", axis=0, tiled=True).T
    shrink = lax.all_gather(shrink_weight, "col", axis=0, tiled=True)
    shrink = lax.all_gather(shrink, "row", axis=1, tiled=True)

    weight_queries, weight_keys, weight_values = (mine_of(triple[j]) for j in range(3))
    weight_merge, weight_expand, weight_shrink = mine_of(merge), mine_of(expand), mine_of(shrink)

    inputs = gather_features(tokens)
    head_shape = (-1, heads, HEAD)
    queries = (nt(inputs, weight_queries) + bias_queries.astype(f32)).astype(bf16)
    keys = nt(inputs, weight_keys).astype(bf16)
    values = (nt(inputs, weight_values) + bias_values.astype(f32)).astype(bf16)
    all_keys, all_values = keys, values
    queries_heads = queries.reshape(head_shape)
    keys_heads, values_heads = all_keys.reshape(head_shape), all_values.reshape(head_shape)
    attended, lse = attention_forward(
        queries_heads, keys_heads, values_heads, query_segment, key_segment
    )
    attended = attended.reshape(count, -1)
    branch = sum_tokens(nn(attended, weight_merge))
    residual = own_part(inputs).astype(f32) + (branch + vectors[0])
    scaled_one, inverse_one, normed_one = norm_forward(residual, vectors[1], vectors[2])
    normed_low = gather_tokens(normed_one.astype(bf16))
    pre_gelu = nt(normed_low, weight_expand) + bias_hidden
    hidden = exact_gelu(pre_gelu).astype(bf16)
    shrunk = sum_tokens(nn(hidden, weight_shrink))
    scaled_two, inverse_two, final = norm_forward(
        normed_one + (shrunk + vectors[3]), vectors[4], vectors[5]
    )

    live = (own_part(query_segment) != 0).astype(f32)[:, None]
    upstream = to_own_tokens(cotangent).astype(f32) * live
    grad_sum_two, grad_gain_two, grad_shift_two = norm_backward(
        upstream, scaled_two, inverse_two, vectors[4]
    )
    grad_shrunk_own = grad_sum_two.astype(bf16)
    grad_shrunk = gather_tokens(grad_shrunk_own)
    grad_hidden = nt(grad_shrunk, weight_shrink)
    grad_pre = jax.vjp(exact_gelu, pre_gelu)[1](grad_hidden)[0].astype(bf16)
    grad_normed = grad_sum_two + sum_tokens(nn(grad_pre, weight_expand))
    grad_res, grad_gain_one, grad_shift_one = norm_backward(
        grad_normed, scaled_one, inverse_one, vectors[1]
    )
    grad_branch_own = grad_res.astype(bf16)
    grad_branch = gather_tokens(grad_branch_own)
    grad_attended = nt(grad_branch, weight_merge).astype(bf16)
    late_out, late_res, grad_attended = lax.optimization_barrier(
        (final.astype(bf16), grad_res, grad_attended)
    )
    layer_out, grad_res_columns = to_own_features(late_out), to_own_features(late_res)
    grad_queries, grad_keys, grad_values = attention_backward(
        queries_heads,
        keys_heads,
        values_heads,
        query_segment,
        key_segment,
        lse,
        grad_attended.reshape(head_shape),
    )
    grad_queries = grad_queries.reshape(count, -1)
    grad_keys_values = jnp.concatenate(
        (grad_keys.reshape(-1, heads * HEAD), grad_values.reshape(-1, heads * HEAD)), 1
    )
    grad_keys_values = grad_keys_values.astype(bf16)
    grad_keys, grad_values = (
        grad_keys_values[:, : heads * HEAD],
        grad_keys_values[:, heads * HEAD :],
    )
    grad_entry = (
        nn(grad_queries, weight_queries)
        + nn(grad_keys, weight_keys)
        + nn(grad_values, weight_values)
    )
    grad_tokens = sum_features(grad_entry, grad_res_columns)

    def assemble(local, row_axis, col_axis):
        full = jnp.zeros((local.shape[0], local.shape[1] * rows, D), bf16)
        full = lax.dynamic_update_slice(
            full, local.astype(bf16), (0, row * local.shape[1], 0)
        )
        full = lax.psum_scatter(full, "row", scatter_dimension=2, tiled=True)
        full = lax.psum_scatter(full, "col", scatter_dimension=1, tiled=True)
        return lax.psum(full, ("outer", "core")).astype(f32)

    grad_triple = assemble(
        jnp.stack(
            (tn(grad_queries, inputs), tn(grad_keys, inputs), tn(grad_values, inputs))
        ),
        0,
        2,
    ).transpose(2, 0, 1)
    grad_merge = assemble(tn(attended, grad_branch)[None], 1, 0)[0]
    grad_expand = assemble(tn(grad_pre, normed_low)[None], 0, 1)[0].T
    grad_shrink = assemble(tn(hidden, grad_shrunk)[None], 1, 0)[0]

    def column_sums(values):
        return jnp.sum(values, axis=0, dtype=f32)

    sum_hidden = column_sums(grad_pre)
    sum_queries, sum_values = column_sums(grad_queries), column_sums(grad_values)
    sum_rows = jnp.stack(
        (
            column_sums(grad_branch_own),
            grad_gain_one,
            grad_shift_one,
            column_sums(grad_shrunk_own),
            grad_gain_two,
            grad_shift_two,
        )
    )
    everywhere = ("outer", "core", "col")
    row_totals = lax.psum_scatter(sum_rows, "row", scatter_dimension=1, tiled=True)
    row_totals = lax.psum(row_totals, everywhere)

    def whole(local):
        full = jnp.zeros(local.shape[:-1] + (local.shape[-1] * rows,), f32)
        full = lax.dynamic_update_slice_in_dim(full, local, row * local.shape[-1], -1)
        full = lax.psum(full, everywhere + ("row",))
        share = full.shape[-1] // cols
        return lax.dynamic_slice_in_dim(full, col * share, share, -1)

    grad_pair = whole(jnp.stack((sum_queries, sum_values)))
    grad_expand_bias = whole(sum_hidden)

    return (
        layer_out,
        grad_tokens,
        grad_triple,
        grad_pair,
        grad_merge,
        row_totals[0],
        row_totals[1],
        row_totals[2],
        grad_expand,
        grad_expand_bias,
        grad_shrink,
        row_totals[3],
        row_totals[4],
        row_totals[5],
    )


def shards(tokens, *others):
    sizes = [size(axis) for axis in ("outer", "core", "row", "col")]
    if sizes == [2, 2, 2, 4] and 2 * tokens.shape[0] == LEN:
        return layer(tokens, *others)
    return layer_anywhere(tokens, *others)


def solution(mesh):
    sizes = mesh.shape
    axes = ("outer", "core", "row", "col")
    split = Mesh(
        mesh.devices.reshape(sizes["dp"] // 2, 2, sizes["row"], sizes["col"]), axes
    )
    dp = ("outer", "core")
    activations = P(("outer", "core", "col"), "row")
    return jax.shard_map(
        shards,
        mesh=split,
        in_specs=(
            activations,
            P(dp),
            P("row", None, "col"),
            P(None, "col"),
            P("col", "row"),
            P("row"),
            P("row"),
            P("row"),
            P("row", "col"),
            P("col"),
            P("col", "row"),
            P("row"),
            P("row"),
            P("row"),
            activations,
        ),
        out_specs=(
            activations,
            activations,
            P("row", None, "col"),
            P(None, "col"),
            P("col", "row"),
            P("row"),
            P("row"),
            P("row"),
            P("row", "col"),
            P("col"),
            P("col", "row"),
            P("row"),
            P("row"),
            P("row"),
        ),
        check_vma=False,
    )
```

```python
import functools

import jax
import jax.numpy as jnp
from jax import lax
from jax.experimental import pallas as pl
from jax.experimental.pallas import tpu as pltpu
from jax.sharding import Mesh, PartitionSpec as P

D = 1024
HEAD = 64
LEN = 1024
epsilon = 1e-05
masked_score = -1e30
bf16 = jnp.bfloat16
f32 = jnp.float32


def size(axis):
    return lax.axis_size(axis)


def place(axis):
    return lax.axis_index(axis)


def pair(values, axis):
    return lax.ppermute(values, axis, [(0, 1), (1, 0)])


def after(values, *others):
    return lax.optimization_barrier((values,) + others)[0]


def together(*arrays):
    return lax.optimization_barrier(arrays)


def shift(values, step):
    count = size("col")
    return lax.ppermute(values, "col", [(i, (i + step) % count) for i in range(count)])


def across(values, bits):
    return lax.ppermute(values, "col", [(i, i ^ bits) for i in range(size("col"))])


def by_place(bit, own, other, axis):
    return jnp.where(
        bit == 0,
        jnp.concatenate((own, other), axis),
        jnp.concatenate((other, own), axis),
    )


def nt(left, right, kind=f32):
    return lax.dot_general(
        left, right, (((1,), (1,)), ((), ())), preferred_element_type=f32
    ).astype(kind)


def nn(left, right, kind=f32):
    return lax.dot_general(
        left, right, (((1,), (0,)), ((), ())), preferred_element_type=f32
    ).astype(kind)


def tn(left, right, kind=f32):
    return lax.dot_general(
        left, right, (((0,), (0,)), ((), ())), preferred_element_type=f32
    ).astype(kind)


def swap_sequences(values):
    count = size("col")
    perm = []
    for core in range(2):
        for col in range(count):
            half, other = col % 2, col - col % 2
            target = (half, other + core)
            perm.append((core * count + col, target[0] * count + target[1]))
    return lax.ppermute(values, ("core", "col"), perm)


def own_first(values):
    if size("row") != 2:
        return values
    half = values.shape[0] // 2
    return jnp.where(place("row") == 0, values, jnp.roll(values, half, axis=0))


def own_part(values):
    share = values.shape[0] // size("row")
    if size("row") == 2:
        return values[:share]
    return lax.dynamic_slice_in_dim(values, place("row") * share, share)


def gather_features(values):
    if size("row") == 2:
        full = by_place(place("row"), values, pair(values, "row"), 1)
        return own_first(full)
    return lax.all_gather(values, "row", axis=1, tiled=True)


def gather_tokens(values):
    if size("row") == 2:
        return jnp.concatenate((values, pair(values, "row")), 0)
    return lax.all_gather(values, "row", axis=0, tiled=True)


def sum_tokens(partial):
    if size("row") == 2:
        share = partial.shape[0] // 2
        return partial[:share] + pair(partial[share:].astype(bf16), "row").astype(f32)
    return lax.psum_scatter(partial, "row", scatter_dimension=0, tiled=True)


def to_own_tokens(values):
    if size("row") == 2:
        bit = place("row")
        ordered = own_first(values)
        share = values.shape[0] // 2
        return by_place(bit, ordered[:share], pair(ordered[share:], "row"), 1)
    return lax.all_to_all(values, "row", 0, 1, tiled=True)


def to_own_features(values):
    if size("row") == 2:
        bit = place("row")
        half = values.shape[1] // 2
        low, high = values[:, :half], values[:, half:]
        own = jnp.where(bit == 0, low, high)
        other = pair(jnp.where(bit == 0, high, low), "row")
        return by_place(bit, own, other, 0)
    return lax.all_to_all(values, "row", 1, 0, tiled=True)


def sum_features(partial, addend):
    if size("row") == 2:
        half = partial.shape[1] // 2
        low, high = partial[:, :half], partial[:, half:]
        bit = place("row")
        got = pair(jnp.where(bit == 0, high, low).astype(bf16), "row").astype(f32)
        got = jnp.roll(got, partial.shape[0] // 2, axis=0)
        return own_first(jnp.where(bit == 0, low, high) + got) + addend
    return lax.psum_scatter(partial, "row", scatter_dimension=1, tiled=True) + addend


class Held:
    def __init__(self, **arrays):
        vars(self).update(arrays)

    update = __init__


def step_of(held):
    return Held(**lax.optimization_barrier(vars(held)))


def halves(values):
    middle = values.shape[0] // 2
    return values[:middle], values[middle:]


def three_groups(triple, merge, expand, shrink):
    depth = triple.shape[0]
    heads = triple.transpose(1, 2, 0).reshape(3, 2, 2, 1, HEAD, depth)
    out = merge.reshape(1, 2, 2, 1, HEAD, depth)
    keys_values = jnp.concatenate((heads[1], heads[2]), 3 - 1)
    queries_merge = jnp.concatenate((heads[0], out[0]), 3 - 1)
    attend = jnp.stack((keys_values, queries_merge), 2).reshape(2, 2, 2, 2 * HEAD, depth)
    widen = expand.T.reshape(2, 2, 2, -1, depth)
    narrow = shrink.reshape(2, 2, 2, -1, depth)
    return attend, widen, narrow


def my_quarter(group):
    some = lax.dynamic_index_in_dim(group, place("outer"), 1, keepdims=False)
    return lax.dynamic_index_in_dim(some, place("core"), 1, keepdims=False)


def exchange_rows(quarter):
    bit = place("row")
    mine = jnp.where(bit == 0, quarter[0], quarter[1])
    other = pair(jnp.where(bit == 0, quarter[1], quarter[0]), "row")
    return by_place(bit, mine, other, 1)


STEPS = (1, 3, 2)
BACK = (2, 1, 3)


def own_core_half(parts, pairs):
    count = size("col")
    return jnp.stack(
        [jnp.stack([group[step] for step in range(count)]) for group in (parts, pairs)]
    )


def gather_attend(quarter):
    parts = {0: quarter}
    for step in STEPS:
        parts[step] = shift(quarter, step)
    pairs = {step: pair(parts[step], "outer") for step in (0,) + STEPS}
    return own_core_half(parts, pairs), parts[2], pairs[2]


def collect_row(last):
    bit = place("row")
    half = last.shape[1] // 2
    low, high = last[:, :half].astype(bf16), last[:, half:].astype(bf16)
    mine = jnp.where(bit == 0, low, high)
    got = pair(jnp.where(bit == 0, high, low), "row")
    return jnp.stack((jnp.where(bit == 0, mine, got), jnp.where(bit == 0, got, mine)))


def ungroup(attend):
    depth = attend.shape[-1]
    heads = attend.reshape(4, 2, 2, HEAD, depth)
    keys, values = heads[:, 0, 0], heads[:, 0, 1]
    queries, merge = heads[:, 1, 0], heads[:, 1, 1]
    triple = jnp.stack((queries, keys, values)).reshape(3, 4 * HEAD, depth).transpose(2, 0, 1)
    return triple, merge.reshape(4 * HEAD, depth)


def flip(values, axis, bit):
    return jnp.where(bit == 0, values, jnp.flip(values, axis))


def dot(left, right, left_dim, right_dim):
    return lax.dot_general(
        left, right, (((left_dim,), (right_dim,)), ((), ())), preferred_element_type=f32
    )


def params():
    return pltpu.CompilerParams(vmem_limit_bytes=36 << 20)


def anywhere(arrays):
    return [pl.BlockSpec(memory_space=pl.ANY) for _ in arrays]


def pick(near_ref, far_ref, begin):
    part = slice(begin, begin + HEAD)
    return jnp.concatenate((near_ref[:, part], far_ref[:, part]), 0)


def attend_forward_kernel(q_ref, near_ref, far_ref, qs_ref, ks_ref, out_ref, lse_ref):
    same = ks_ref[...] == qs_ref[...]
    for head in range(2):
        part = slice(head * HEAD, (head + 1) * HEAD)
        keys = pick(near_ref, far_ref, 2 * head * HEAD)
        values = pick(near_ref, far_ref, (2 * head + 1) * HEAD)
        queries = q_ref[:, part] * jnp.asarray(HEAD**-0.5, bf16)
        scores = jnp.where(same, dot(keys, queries, 1, 1), masked_score)
        top = jnp.max(scores, axis=0, keepdims=True)
        weights = jnp.exp(scores - top)
        total = jnp.sum(weights, axis=0, keepdims=True)
        low = (weights * (1.0 / total)).astype(bf16)
        out_ref[part] = dot(values, low, 0, 0).astype(bf16)
        lse_ref[0, head : head + 1] = top + jnp.log(total)


def attend_forward(queries, near, far, query_segment, key_segment):
    tokens, width = queries.shape
    steps = width // (2 * HEAD)
    block = pl.BlockSpec((tokens, 4 * HEAD), lambda i: (0, i))
    return pl.pallas_call(
        attend_forward_kernel,
        grid=(steps,),
        in_specs=[
            pl.BlockSpec((tokens, 2 * HEAD), lambda i: (0, i)),
            block,
            block,
            pl.BlockSpec((1, tokens), lambda i: (0, 0)),
            pl.BlockSpec((2 * tokens, 1), lambda i: (0, 0)),
        ],
        out_specs=[
            pl.BlockSpec((2 * HEAD, tokens), lambda i: (i, 0)),
            pl.BlockSpec((1, 2, tokens), lambda i: (i, 0, 0)),
        ],
        out_shape=[
            jax.ShapeDtypeStruct((width, tokens), bf16),
            jax.ShapeDtypeStruct((steps, 2, tokens), f32),
        ],
        compiler_params=params(),
        cost_estimate=pl.CostEstimate(
            flops=32 * tokens * tokens * width,
            bytes_accessed=4 << 20,
            transcendentals=2 * tokens * tokens * width // HEAD,
        ),
    )(queries, near, far, query_segment, key_segment)


def attend_backward_kernel(
    q_ref, kv_ref, far_kv_ref, g_ref, qs_ref, ks_ref, lse_ref, dq_ref, near_ref, far_ref
):
    same = ks_ref[...] == qs_ref[...]
    scale = HEAD**-0.5
    near = near_ref.shape[0]
    for head in range(2):
        part = slice(head * HEAD, (head + 1) * HEAD)
        key_part = slice(2 * head * HEAD, (2 * head + 1) * HEAD)
        value_part = slice((2 * head + 1) * HEAD, (2 * head + 2) * HEAD)
        keys = pick(kv_ref, far_kv_ref, key_part.start)
        values = pick(kv_ref, far_kv_ref, value_part.start)
        queries = q_ref[:, part] * jnp.asarray(scale, bf16)
        grad = g_ref[:, part]
        scores = jnp.where(same, dot(keys, queries, 1, 1), masked_score)
        weights = jnp.exp(scores - lse_ref[0, head : head + 1])
        grad_weights = dot(values, grad, 1, 1)
        inner = jnp.sum(weights * grad_weights, axis=0, keepdims=True)
        grad_scores = (weights * (grad_weights - inner)).astype(bf16)
        dq_ref[part] = (dot(keys, grad_scores, 0, 0) * scale).astype(bf16)
        grad_keys = dot(grad_scores, queries, 1, 0)
        grad_values = dot(weights.astype(bf16), grad, 1, 0)
        near_ref[:, key_part], far_ref[:, key_part] = grad_keys[:near], grad_keys[near:]
        near_ref[:, value_part], far_ref[:, value_part] = grad_values[:near], grad_values[near:]


def attend_backward(queries, near, far, grad, query_segment, key_segment, lse, begin, steps):
    tokens = queries.shape[0]
    block = pl.BlockSpec((tokens, 4 * HEAD), lambda i: (0, begin + i))
    query_block = pl.BlockSpec((tokens, 2 * HEAD), lambda i: (0, begin + i))
    key_block = pl.BlockSpec((tokens, 4 * HEAD), lambda i: (0, i))
    return pl.pallas_call(
        attend_backward_kernel,
        grid=(steps,),
        in_specs=[
            query_block,
            block,
            block,
            query_block,
            pl.BlockSpec((1, tokens), lambda i: (0, 0)),
            pl.BlockSpec((2 * tokens, 1), lambda i: (0, 0)),
            pl.BlockSpec((1, 2, tokens), lambda i: (begin + i, 0, 0)),
        ],
        out_specs=[pl.BlockSpec((2 * HEAD, tokens), lambda i: (i, 0)), key_block, key_block],
        out_shape=[
            jax.ShapeDtypeStruct((2 * HEAD * steps, tokens), bf16),
            jax.ShapeDtypeStruct((tokens, 4 * HEAD * steps), f32),
            jax.ShapeDtypeStruct((tokens, 4 * HEAD * steps), f32),
        ],
        compiler_params=params(),
        cost_estimate=pl.CostEstimate(
            flops=160 * tokens * tokens * steps * HEAD,
            bytes_accessed=8 << 20,
            transcendentals=4 * tokens * tokens * steps,
        ),
    )(queries, near, far, grad, query_segment, key_segment, lse)


def attend_weights_kernel(
    which_ref, dkv_ref, dq_ref, out_in_ref, x_ref, g_ref, *rest, added, cols
):
    add_ref = rest[0] if added else None
    out_refs = rest[-cols:]

    def put(rows, value):
        value = value.reshape(cols, -1, D)
        for step, out_ref in enumerate(out_refs):
            term = value[step]
            if added:
                term = term + add_ref[0, step, rows].astype(f32)
            out_ref[rows] = term.astype(out_ref.dtype)

    @pl.when(which_ref[0] == 0)
    def _():
        put(slice(0, 2 * HEAD), dot(dkv_ref[...], x_ref[...], 0, 0))

    @pl.when(which_ref[0] == 1)
    def _():
        put(slice(0, HEAD), dot(dq_ref[...], x_ref[...], 1, 0))
        put(slice(HEAD, 2 * HEAD), dot(out_in_ref[...], g_ref[...], 1, 0))


def attend_weights(which, dkv, dq, out_in, x, g, begin, cols, kind, add=None, earlier=()):
    tokens = x.shape[0]
    full = pl.BlockSpec((tokens, D), lambda i, w: (0, 0))
    rows = pl.BlockSpec((cols * HEAD, tokens), lambda i, w: (begin, 0))
    specs = [pl.BlockSpec((tokens, cols * 2 * HEAD), lambda i, w: (0, begin)), rows, rows, full, full]
    given = [dkv, dq, out_in, x, g]
    if add is not None:
        specs.append(pl.BlockSpec((1, cols, 2 * HEAD, D), lambda i, w: (begin, 0, 0, 0)))
        given.append(add)
    return pl.pallas_call(
        functools.partial(attend_weights_kernel, added=add is not None, cols=cols),
        grid_spec=pltpu.PrefetchScalarGridSpec(
            num_scalar_prefetch=1,
            grid=(1,),
            in_specs=specs + anywhere(earlier),
            out_specs=[pl.BlockSpec((2 * HEAD, D), lambda i, w: (0, 0))] * cols,
        ),
        out_shape=[jax.ShapeDtypeStruct((2 * HEAD, D), kind)] * cols,
        compiler_params=params(),
        cost_estimate=pl.CostEstimate(
            flops=4 * tokens * D * cols * HEAD, bytes_accessed=6 << 20, transcendentals=0
        ),
    )(which, *given, *earlier)


def attend_far_kernel(which_ref, dkv_ref, dq_ref, out_in_ref, x_ref, g_ref, *rest):
    out_ref = rest[-1]
    cols = out_ref.shape[1]

    @pl.when(which_ref[0] == 0)
    def _():
        value = dot(dkv_ref[...], x_ref[...], 0, 0)
        out_ref[0] = value.reshape(cols, 2 * HEAD, D).astype(out_ref.dtype)

    @pl.when(which_ref[0] == 1)
    def _():
        for part, value in enumerate(
            (dot(dq_ref[...], x_ref[...], 1, 0), dot(out_in_ref[...], g_ref[...], 1, 0))
        ):
            rows = slice(part * HEAD, (part + 1) * HEAD)
            out_ref[0, :, rows] = value.reshape(cols, HEAD, D).astype(out_ref.dtype)


def attend_far_weights(which, dkv, dq, out_in, x, g, cols, *earlier):
    tokens = x.shape[0]
    full = pl.BlockSpec((tokens, D), lambda i, w: (0, 0))
    rows = pl.BlockSpec((cols * HEAD, tokens), lambda i, w: (i, 0))
    return pl.pallas_call(
        attend_far_kernel,
        grid_spec=pltpu.PrefetchScalarGridSpec(
            num_scalar_prefetch=1,
            grid=(2,),
            in_specs=[
                pl.BlockSpec((tokens, cols * 2 * HEAD), lambda i, w: (0, i)), rows, rows, full, full
            ]
            + anywhere(earlier),
            out_specs=pl.BlockSpec((1, cols, 2 * HEAD, D), lambda i, w: (i, 0, 0, 0)),
        ),
        out_shape=jax.ShapeDtypeStruct((2, cols, 2 * HEAD, D), bf16),
        compiler_params=params(),
        cost_estimate=pl.CostEstimate(
            flops=8 * tokens * D * cols * HEAD, bytes_accessed=6 << 20, transcendentals=0
        ),
    )(which, dkv, dq, out_in, x, g, *earlier)


SPARE = 8


def units_of(weights):
    units = (weights.shape[2] - SPARE) // 2
    expand = weights[:, :, :units].reshape(-1, D)
    shrink = weights[:, :, units : 2 * units].reshape(-1, D)
    return expand, shrink


def finish(total, keep_ref, send_ref):
    @pl.when(pl.program_id(0) == pl.num_programs(0) - 1)
    def _():
        half = total.shape[0] // 2
        keep_ref[...] = total[:half]
        send_ref[...] = total[half:].astype(bf16)


def add_to(total, term):
    @pl.when(pl.program_id(0) == 0)
    def _():
        total[...] = term

    @pl.when(pl.program_id(0) > 0)
    def _():
        total[...] += term


def hidden_forward_kernel(
    x_ref, bias_ref, weights_ref, hidden_ref, slope_ref, keep_ref, send_ref, total
):
    expand, shrink = units_of(weights_ref[0, 0:1])
    u = dot(x_ref[...], expand, 1, 1) + bias_ref[0]
    normal = 0.5 * (1.0 + lax.erf(u * (0.5**0.5)))
    slope_ref[...] = normal + u * (jnp.exp(-0.5 * u * u) * ((0.5 / jnp.pi) ** 0.5))
    hidden = (u * normal).astype(bf16)
    hidden_ref[...] = hidden
    add_to(total, dot(hidden, shrink, 1, 0))
    finish(total, keep_ref, send_ref)


def hidden_specs(tokens, weights):
    outer, core, cols, rows, _ = weights.shape
    units = (rows - SPARE) // 2
    steps, width = outer * core, cols * units
    block = pl.BlockSpec((1, 1, cols, rows, D), lambda i: (i // core, i % core, 0, 0, 0))
    wide = pl.BlockSpec((tokens, width), lambda i: (0, i))
    half = pl.BlockSpec((tokens // 2, D), lambda i: (0, 0))
    half_shapes = [
        jax.ShapeDtypeStruct((tokens // 2, D), f32),
        jax.ShapeDtypeStruct((tokens // 2, D), bf16),
    ]
    full = pl.BlockSpec((tokens, D), lambda i: (0, 0))
    row = pl.BlockSpec((1, 1, width), lambda i: (i, 0, 0))
    cost = pl.CostEstimate(
        flops=4 * tokens * D * steps * width, bytes_accessed=20 << 20, transcendentals=0
    )
    return steps, width, block, wide, half, half_shapes, full, row, cost


def hidden_forward(x, weights, bias):
    tokens = x.shape[0]
    steps, width, block, wide, half, half_shapes, full, row, cost = hidden_specs(tokens, weights)
    shape = (tokens, steps * width)
    return pl.pallas_call(
        hidden_forward_kernel,
        grid=(steps,),
        in_specs=[full, row, block],
        out_specs=[wide, wide, half, half],
        out_shape=[jax.ShapeDtypeStruct(shape, bf16), jax.ShapeDtypeStruct(shape, f32)]
        + half_shapes,
        scratch_shapes=[pltpu.VMEM((tokens, D), f32)],
        compiler_params=params(),
        cost_estimate=cost,
    )(x, bias, weights)


def hidden_backward_kernel(
    g_ref, slope_ref, weights_ref, grad_ref, sum_ref, keep_ref, send_ref, total
):
    expand, shrink = units_of(weights_ref[0, 0:1])
    grad = (dot(g_ref[...], shrink, 1, 1) * slope_ref[...]).astype(bf16)
    grad_ref[...] = grad
    sum_ref[0] = jnp.sum(grad.astype(f32), axis=0, keepdims=True)
    add_to(total, dot(grad, expand, 1, 0))
    finish(total, keep_ref, send_ref)


def hidden_backward(g, weights, slope):
    tokens = g.shape[0]
    steps, width, block, wide, half, half_shapes, full, row, cost = hidden_specs(tokens, weights)
    return pl.pallas_call(
        hidden_backward_kernel,
        grid=(steps,),
        in_specs=[full, wide, block],
        out_specs=[wide, row, half, half],
        out_shape=[
            jax.ShapeDtypeStruct((tokens, steps * width), bf16),
            jax.ShapeDtypeStruct((steps, 1, width), f32),
        ]
        + half_shapes,
        scratch_shapes=[pltpu.VMEM((tokens, D), f32)],
        compiler_params=params(),
        cost_estimate=cost,
    )(g, slope, weights)


def hidden_weights_kernel(grad_ref, hidden_ref, x_ref, g_ref, sum_ref, out_ref):
    cols, rows, _ = out_ref.shape[2:]
    units = (rows - SPARE) // 2
    for part, (left, right) in enumerate(((grad_ref, x_ref), (hidden_ref, g_ref))):
        value = dot(left[...], right[...], 0, 0).reshape(cols, units, D)
        out_ref[0, 0, :, part * units : (part + 1) * units] = value.astype(bf16)
    first = lax.broadcasted_iota(jnp.int32, (cols, SPARE, units), 1) == 0
    sums = jnp.where(first, sum_ref[0][:, None, :], 0.0).astype(bf16)
    out_ref[0, 0, :, 2 * units :] = jnp.zeros((cols, SPARE, D), bf16)
    for begin in (0, D // 2):
        out_ref[0, 0, :, 2 * units :, begin : begin + units] = sums


def hidden_weights(grad, hidden, x, g, sums, shape):
    tokens = x.shape[0]
    outer, core, cols, rows, _ = shape
    width = grad.shape[1] // (outer * core)
    wide = pl.BlockSpec((tokens, width), lambda i: (0, i))
    full = pl.BlockSpec((tokens, D), lambda i: (0, 0))
    return pl.pallas_call(
        hidden_weights_kernel,
        grid=(outer * core,),
        in_specs=[
            wide, wide, full, full, pl.BlockSpec((1, cols, width // cols), lambda i: (i, 0, 0))
        ],
        out_specs=pl.BlockSpec(
            (1, 1, cols, rows, D), lambda i: (i // core, i % core, 0, 0, 0)
        ),
        out_shape=jax.ShapeDtypeStruct(shape, bf16),
        compiler_params=params(),
        cost_estimate=pl.CostEstimate(
            flops=4 * tokens * D * grad.shape[1], bytes_accessed=16 << 20, transcendentals=0
        ),
    )(grad, hidden, x, g, sums)


def layer(
    tokens, segments, triple_weight, pair_bias, merge_weight, merge_bias, first_gain, first_shift,
    expand_weight, expand_bias, shrink_weight, shrink_bias, second_gain, second_shift, cotangent,
):
    cols = size("col")
    count = tokens.shape[0]
    own = count // 2
    heads = D // HEAD // 2
    row, col, core, outer = place("row"), place("col"), place("core"), place("outer")
    row_size, pair_size, hidden_size = merge_bias.shape[0], pair_bias.shape[1], expand_bias.shape[0]

    groups = three_groups(triple_weight, merge_weight, expand_weight, shrink_weight)
    attend_group = my_quarter(groups[0])
    row_vectors = jnp.stack(
        (merge_bias, first_gain, first_shift, shrink_bias, second_gain, second_shift)
    )
    column = jnp.concatenate(
        [
            lax.dynamic_slice_in_dim(vector, row * (vector.shape[0] // 2), vector.shape[0] // 2)
            for vector in (pair_bias[0], pair_bias[1], expand_bias)
        ]
    )
    moved = swap_sequences(tokens)
    quarter = exchange_rows(attend_group)
    pair_column, hidden_column = column[:pair_size], column[pair_size:].reshape(4, -1)
    pair_column = pair_column.reshape(2, 2, HEAD)
    pair_column = lax.dynamic_index_in_dim(pair_column, outer, 1, keepdims=False)
    pair_column = lax.dynamic_index_in_dim(pair_column, 1 - core, 0)
    moved_cotangent = swap_sequences(cotangent)
    hidden_column = lax.dynamic_index_in_dim(hidden_column, 2 * outer + core, 0)
    other_group = jnp.concatenate([my_quarter(group) for group in groups[1:]], 1)
    v = step_of(
        Held(
            quarter=quarter, moved=moved, other=segments.astype(f32), group=other_group, rows=row_vectors, pairs=pair_column,
            hidden=hidden_column, cot=moved_cotangent,
        )
    )

    def beside(rows, value):
        spare = jnp.pad(value, ((0, SPARE - 1), (0, D - value.shape[1])))
        return jnp.concatenate((rows, spare), 0)

    quarter, moved = beside(v.quarter, v.pairs), v.moved
    parts = {0: quarter, 1: shift(quarter, 1), 3: shift(quarter, 3)}
    pairs = {0: pair(quarter, "outer")}
    got_tokens = pair(moved, "row")
    v.update(quarter=quarter, parts=parts, pairs=pairs, moved=moved, got=got_tokens)
    v = step_of(v)
    parts, pairs, quarter = v.parts, v.pairs, v.quarter
    parts[2] = shift(quarter, 2)
    pairs[1], pairs[3] = pair(parts[1], "outer"), pair(parts[3], "outer")
    v.vectors = by_place(row, v.rows, pair(v.rows, "row"), 1)
    v.other = pair(v.other, "core")
    v.group = exchange_rows(v.group)
    v = step_of(v)
    parts, pairs = v.parts, v.pairs
    pairs[2] = pair(parts[2], "outer")
    v.inputs = own_first(by_place(row, v.moved, v.got, 1))
    mine = beside(v.group, v.hidden)
    hidden_all = lax.all_gather(mine, ("outer", "core", "col"), axis=0)
    hidden_all = hidden_all.reshape(2, 2, cols, -1, D)
    v = step_of(v)
    parts, pairs = v.parts, v.pairs
    rows = 2 * HEAD

    def without(group):
        return {step: group[step][:rows] for step in range(cols)}

    attend_own = own_core_half(without(parts), without(pairs))
    v.attend_own, v.attend_other = attend_own, pair(attend_own, "core")
    bias_own = jnp.stack(
        [group[step][rows, :HEAD] for group in (parts, pairs) for step in range(cols)]
    ).astype(f32)
    v.bias_own, v.bias_other = bias_own, pair(bias_own, "core")
    other = v.other.astype(jnp.int32)
    sequence = lax.dynamic_slice_in_dim(
        jnp.where(col % 2 == core, segments, other), (col // 2) * LEN, LEN
    ).reshape(2, count)
    query_segment = own_first(lax.dynamic_index_in_dim(sequence, core, 0, keepdims=False))
    far_segment = own_first(lax.dynamic_index_in_dim(sequence, 1 - core, 0, keepdims=False))
    key_segment = jnp.concatenate((query_segment, far_segment))
    segment_row, segment_column = query_segment[None], key_segment[:, None]
    vectors = v.vectors.astype(f32)
    v = step_of(
        Held(
            own=v.attend_own, other=v.attend_other, cot=v.cot, inputs=v.inputs,
            vectors=vectors, biases=(v.bias_own, v.bias_other),
        )
    )
    attend_own, attend_other, inputs, vectors = v.own, v.other, v.inputs, v.vectors
    first = jnp.where(core == 0, attend_own, attend_other)
    second = jnp.where(core == 0, attend_other, attend_own)
    bias_values = jnp.where(core == 0, v.biases[0], v.biases[1])
    bias_keys_values = jnp.stack((jnp.zeros_like(bias_values), bias_values), 1).reshape(-1)
    bias_queries = jnp.where(core == 0, v.biases[1], v.biases[0]).reshape(-1)
    weight_keys_values = first.reshape(-1, D)
    second = second.reshape(heads, 2, HEAD, D)
    weight_queries, weight_merge = second[:, 0].reshape(-1, D), second[:, 1].reshape(-1, D)

    cut = heads * HEAD // 2
    steps = heads // 4
    keys_values = (nt(inputs, weight_keys_values) + bias_keys_values).astype(bf16)
    v.far = pair(keys_values, "core")
    v.queries = (nt(inputs, weight_queries) + bias_queries).astype(bf16)
    v.keys_values = keys_values
    v.weights = (weight_keys_values, weight_queries, weight_merge)
    v = step_of(v)
    queries = v.queries
    keys_values, far_keys_values = v.keys_values, v.far
    v.attended, v.lse = attend_forward(
        queries, keys_values, far_keys_values, segment_row, segment_column
    )
    v.upstream = to_own_tokens(v.cot)
    v = step_of(v)
    attended, lse = v.attended, v.lse
    queries, keys_values, far_keys_values = v.queries, v.keys_values, v.far
    weight_keys_values, weight_queries, weight_merge = v.weights
    branch = sum_tokens(tn(attended, weight_merge))
    residual = inputs[:own].astype(f32) + (branch + vectors[0])
    scaled_one, inverse_one, normed_one = norm_forward(residual, vectors[1], vectors[2])
    normed_low = gather_tokens(normed_one.astype(bf16))
    normed_low, normed_one, hidden_all = lax.optimization_barrier((normed_low, normed_one, hidden_all))
    units = hidden_size // 8
    bias_hidden = hidden_all[:, :, :, 2 * units, :units].reshape(4, 1, -1).astype(f32)
    upstream = v.upstream

    hidden, slope, keep, send = hidden_forward(normed_low, hidden_all, bias_hidden)
    shrunk = keep + pair(send, "row").astype(f32)
    scaled_two, inverse_two, final = norm_forward(
        normed_one + (shrunk + vectors[3]), vectors[4], vectors[5]
    )
    live = (query_segment[:own] != 0).astype(f32)[:, None]
    upstream = upstream.astype(f32) * live
    grad_sum_two, grad_gain_two, grad_shift_two = norm_backward(
        upstream, scaled_two, inverse_two, vectors[4]
    )
    grad_shrunk_own = grad_sum_two.astype(bf16)
    grad_shrunk = gather_tokens(grad_shrunk_own)
    grad_shrunk, out = lax.optimization_barrier((grad_shrunk, final.astype(bf16)))
    grad_pre, sum_hidden, keep, send = hidden_backward(grad_shrunk, hidden_all, slope)
    out = to_own_features(out)
    cut = heads * HEAD // 2
    steps = heads // 4
    spare = sum_hidden.reshape(4, cols, units)
    v = Held(
        grad_pre=grad_pre, hidden=hidden, normed=normed_low, g=grad_shrunk, inputs=inputs,
        attended=attended, queries=queries, keys_values=keys_values, lse=lse,
        far_keys_values=far_keys_values, keep=keep, send=send, sum_two=grad_sum_two,
        scaled_one=scaled_one, inverse_one=inverse_one, out=out, shrunk_own=grad_shrunk_own,
        sum_two_rows=(grad_gain_two, grad_shift_two), spare=spare, vectors=vectors,
        weight_merge=weight_merge, weight_queries=weight_queries,
        weight_keys_values=weight_keys_values,
    )

    v = step_of(v)
    v.got = pair(v.send, "row")
    hidden_grads = hidden_weights(
        v.grad_pre, v.hidden, v.normed, v.g, v.spare, hidden_all.shape
    )
    v.hidden_grads = hidden_grads
    v.out = swap_sequences(v.out)
    v = step_of(v)
    hidden_sums = lax.psum_scatter(
        v.hidden_grads.reshape(-1, D), ("outer", "core", "col"), scatter_dimension=0, tiled=True
    )
    grad_normed = v.sum_two + (v.keep + v.got.astype(f32))
    res, grad_gain_one, grad_shift_one = norm_backward(
        grad_normed, v.scaled_one, v.inverse_one, v.vectors[1]
    )
    branch_own = res.astype(bf16)
    branch_got = pair(branch_own, "row")
    sum_rows = jnp.stack(
        (
            jnp.sum(branch_own, axis=0, dtype=f32),
            grad_gain_one,
            grad_shift_one,
            jnp.sum(v.shrunk_own, axis=0, dtype=f32),
            *v.sum_two_rows,
        )
    )
    v = Held(
        inputs=v.inputs, attended=v.attended, queries=v.queries, out=v.out,
        keys_values=v.keys_values, far_keys_values=v.far_keys_values, lse=v.lse,
        weight_merge=v.weight_merge, weight_queries=v.weight_queries,
        weight_keys_values=v.weight_keys_values,
    )
    v.branch = jnp.concatenate((branch_own, branch_got), 0)
    v.grad_attended = nt(v.branch, v.weight_merge, bf16)
    v.sum_rows = sum_rows
    middle = D // 2
    v.res_mine = jnp.where(row == 0, res[:, :middle], res[:, middle:])
    v.res_send = halves(jnp.where(row == 0, res[:, middle:], res[:, :middle]))
    v = step_of(v)
    shared = (
        v.queries, v.keys_values, v.far_keys_values, v.grad_attended, segment_row,
        segment_column, v.lse,
    )
    v.second = attend_backward(*shared, steps, steps)
    v.res_got = [pair(v.res_send[0], "row")]
    v = step_of(v)
    shared = (
        v.queries, v.keys_values, v.far_keys_values, v.grad_attended, segment_row,
        segment_column, v.lse,
    )
    v.far = pair(v.second[2], "core")
    v.first = attend_backward(*shared, 0, steps)
    v.res_got.append(pair(v.res_send[1], "row"))
    v = step_of(v)
    far = pair(v.first[2], "core")
    dkv_second = (v.second[1] + v.far).astype(bf16)
    v.grad_queries = jnp.concatenate((v.first[0], v.second[0]), 0)
    v.entry = tn(v.grad_queries, v.weight_queries)
    dkv_first = (v.first[1] + far).astype(bf16)
    v.grad_keys_values = jnp.concatenate((dkv_first, dkv_second), 1)
    v = step_of(v)
    which = core.reshape(1)
    part = (v.grad_keys_values, v.grad_queries, v.attended, v.inputs, v.branch)
    v.far = attend_far_weights((1 - core).reshape(1), *part, cols)
    v = step_of(v)
    v.far = pair(v.far, "core")
    entry = v.entry + nn(v.grad_keys_values, v.weight_keys_values)
    v.res_columns = by_place(row, v.res_mine, jnp.concatenate(v.res_got, 0), 0)
    v.entry_keep = jnp.where(row == 0, entry[:, :middle], entry[:, middle:])
    v.entry_send = jnp.where(row == 0, entry[:, middle:], entry[:, :middle]).astype(bf16)
    v = step_of(v)
    part = (v.grad_keys_values, v.grad_queries, v.attended, v.inputs, v.branch)
    v.mates = attend_weights(which, *part, 1, cols, bf16, v.far)
    v = step_of(v)
    part = (v.grad_keys_values, v.grad_queries, v.attended, v.inputs, v.branch)
    v.got = {2: pair(v.mates[2], "outer")}
    v.entry_got = pair(v.entry_send, "row")
    v.own = attend_weights(which, *part, 0, cols, f32, v.far)
    sum_queries = jnp.sum(v.grad_queries, axis=1, dtype=f32)
    sum_values = jnp.sum(v.grad_keys_values, axis=0, dtype=f32).reshape(heads, 2, HEAD)[:, 1]
    sum_pair = jnp.stack((sum_queries, sum_values.reshape(-1))).reshape(2, 2, cols, HEAD)
    sum_pair = flip(sum_pair.transpose(2, 0, 1, 3), 2, outer).reshape(cols, -1)
    length = sum_pair.shape[1]
    sum_pair = jnp.concatenate(
        [
            lax.dynamic_index_in_dim(sum_pair, (col - place_of) % cols, 0, keepdims=False)
            for place_of in range(cols)
        ]
    )
    v.total = jnp.concatenate((sum_pair, v.sum_rows.reshape(-1)))
    v = step_of(v)

    def to_send(sums, got, step):
        return (sums[step] + got.astype(f32)).astype(bf16)

    got = v.got
    got[1], got[3] = pair(v.mates[1], "outer"), pair(v.mates[3], "outer")
    v.two = shift(to_send(v.own, got[2], 2), -2)
    total = v.total
    v.total = total + lax.ppermute(total, "col", [(i, i ^ 1) for i in range(cols)])
    entry = jnp.roll(v.entry_got.astype(f32), own, axis=0)
    v.grad_tokens = own_first(v.entry_keep + entry) + v.res_columns
    v = step_of(v)
    v.one = to_send(v.own, v.got[1], 1)
    v.three = to_send(v.own, v.got[3], 3)
    v.hidden_sums = hidden_sums
    v = step_of(v)
    v.one, v.three = shift(v.one, -1), shift(v.three, -3)
    v.got[0] = pair(v.mates[0], "outer")
    total = v.total
    v.total = total + lax.ppermute(total, "col", [(i, i ^ 2) for i in range(cols)])
    v.block = collect_row(v.hidden_sums)
    v = step_of(v)
    attend_rest = v.own[0] + v.got[0].astype(f32)
    for term in (v.one, v.two, v.three):
        attend_rest = attend_rest + term.astype(f32)
    v.attend = collect_row(attend_rest)
    v.block_got = pair(v.block, "outer")
    v.total = v.total + pair(v.total, "core")
    v.grad_tokens = swap_sequences(v.grad_tokens)
    v = step_of(v)
    v.block = by_place(outer, v.block[:, None], v.block_got[:, None], 1)
    v = step_of(v)
    v.attend_got = pair(v.attend, "outer")
    v.total_got = pair(v.total, "outer")
    v.block_got = pair(v.block, "core")
    v = step_of(v)
    total = v.total + v.total_got
    layer_out, grad_tokens = v.out, v.grad_tokens
    attend = by_place(outer, v.attend[:, None], v.attend_got[:, None], 1)
    attend_got = pair(attend, "core")
    hidden_block = by_place(
        core, v.block[:, :, None], v.block_got[:, :, None], 2
    ).astype(f32)
    attend = by_place(core, attend[:, :, None], attend_got[:, :, None], 2).astype(f32)
    grad_triple, grad_merge = ungroup(attend)
    grad_expand = hidden_block[:, :, :, :units].reshape(-1, D // 2).T
    grad_shrink = hidden_block[:, :, :, units : 2 * units].reshape(-1, D // 2)
    grad_expand_bias = hidden_block[:, :, :, 2 * units, :units].reshape(-1)
    mine = lax.dynamic_slice_in_dim(total, col * length, length)
    sum_rows = total[cols * length :].reshape(6, 2, row_size)
    low, high = sum_rows[:, 0].reshape(-1), sum_rows[:, 1].reshape(-1)
    got = pair(jnp.concatenate((mine, jnp.where(row == 0, high, low))), "row")
    totals = (jnp.where(row == 0, low, high) + got[length:]).reshape(6, row_size)
    got = got[:length]
    short = 2 * HEAD
    grad_pair = by_place(
        row, mine[: 2 * short].reshape(2, short), got[: 2 * short].reshape(2, short), 1
    )
    return (
        layer_out, grad_tokens, grad_triple, grad_pair, grad_merge, totals[0], totals[1], totals[2],
        grad_expand, grad_expand_bias, grad_shrink, totals[3], totals[4], totals[5],
    )


def masked(scores, query_segment, key_segment):
    same = query_segment[:, None] == key_segment[None, :]
    return jnp.where(same[None], scores, masked_score)


def attention_forward(queries, keys, values, query_segment, key_segment):
    scores = jnp.einsum("qhd,khd->hqk", queries, keys, preferred_element_type=f32)
    scores = masked(scores * HEAD**-0.5, query_segment, key_segment)
    top = jnp.max(scores, axis=-1, keepdims=True)
    weights = jnp.exp(scores - top)
    total = jnp.sum(weights, axis=-1, keepdims=True)
    low = (weights / total).astype(bf16)
    attended = jnp.einsum("hqk,khd->qhd", low, values, preferred_element_type=f32)
    return attended.astype(bf16), top + jnp.log(total)


def attention_backward(queries, keys, values, query_segment, key_segment, lse, grad):
    scores = jnp.einsum("qhd,khd->hqk", queries, keys, preferred_element_type=f32)
    scores = masked(scores * HEAD**-0.5, query_segment, key_segment)
    weights = jnp.exp(scores - lse)
    grad_weights = jnp.einsum("qhd,khd->hqk", grad, values, preferred_element_type=f32)
    inner = jnp.sum(weights * grad_weights, axis=-1, keepdims=True)
    grad_scores = (weights * (grad_weights - inner)).astype(bf16)
    scale = HEAD**-0.5
    grad_queries = jnp.einsum("hqk,khd->qhd", grad_scores, keys, preferred_element_type=f32) * scale
    grad_keys = jnp.einsum("hqk,qhd->khd", grad_scores, queries, preferred_element_type=f32) * scale
    grad_values = jnp.einsum(
        "hqk,qhd->khd", weights.astype(bf16), grad, preferred_element_type=f32
    )
    return grad_queries.astype(bf16), grad_keys, grad_values


def norm_forward(values, gain, shift):
    center = jnp.mean(values, axis=1, keepdims=True)
    inverse = lax.rsqrt(
        jnp.mean(values * values, axis=1, keepdims=True) - center * center + epsilon
    )
    scaled = (values - center) * inverse
    return scaled, inverse, scaled * gain + shift


def norm_backward(upstream, scaled, inverse, gain):
    through = upstream * gain
    grad = inverse * (
        through
        - jnp.mean(through, axis=1, keepdims=True)
        - scaled * jnp.mean(through * scaled, axis=1, keepdims=True)
    )
    return grad, jnp.sum(upstream * scaled, axis=0), jnp.sum(upstream, axis=0)


def exact_gelu(values):
    return jax.nn.gelu(values, approximate=False)


def layer_anywhere(
    tokens,
    segments,
    triple_weight,
    pair_bias,
    merge_weight,
    merge_bias,
    first_gain,
    first_shift,
    expand_weight,
    expand_bias,
    shrink_weight,
    shrink_bias,
    second_gain,
    second_shift,
    cotangent,
):
    rows, cols = size("row"), size("col")
    count = tokens.shape[0]
    own = count // rows
    heads = D // HEAD // rows
    row, col = place("row"), place("col")

    query_segment = lax.dynamic_slice_in_dim(segments, col * count, count)
    key_segment = query_segment

    row_size, pair_size, hidden_size = merge_bias.shape[0], pair_bias.shape[1], expand_bias.shape[0]
    row_vectors = jnp.stack(
        (merge_bias, first_gain, first_shift, shrink_bias, second_gain, second_shift)
    )
    vectors = lax.all_gather(row_vectors, "row", axis=1, tiled=True)

    def mine_of(full, axis=0):
        share = full.shape[axis] // rows
        return lax.dynamic_slice_in_dim(full, row * share, share, axis)

    bias_pair = mine_of(lax.all_gather(pair_bias, "col", axis=1, tiled=True), 1)
    bias_queries, bias_values = bias_pair[0], bias_pair[1]
    bias_hidden = mine_of(lax.all_gather(expand_bias, "col", axis=0, tiled=True)).astype(f32)
    vectors = vectors.astype(f32)

    triple = lax.all_gather(triple_weight, "col", axis=2, tiled=True)
    triple = lax.all_gather(triple, "row", axis=0, tiled=True).transpose(1, 2, 0)
    merge = lax.all_gather(merge_weight, "col", axis=0, tiled=True)
    merge = lax.all_gather(merge, "row", axis=1, tiled=True)
    expand = lax.all_gather(expand_weight, "col", axis=1, tiled=True)
    expand = lax.all_gather(expand, "row", axis=0, tiled=True).T
    shrink = lax.all_gather(shrink_weight, "col", axis=0, tiled=True)
    shrink = lax.all_gather(shrink, "row", axis=1, tiled=True)

    weight_queries, weight_keys, weight_values = (mine_of(triple[j]) for j in range(3))
    weight_merge, weight_expand, weight_shrink = mine_of(merge), mine_of(expand), mine_of(shrink)

    inputs = gather_features(tokens)
    head_shape = (-1, heads, HEAD)
    queries = (nt(inputs, weight_queries) + bias_queries.astype(f32)).astype(bf16)
    keys = nt(inputs, weight_keys).astype(bf16)
    values = (nt(inputs, weight_values) + bias_values.astype(f32)).astype(bf16)
    all_keys, all_values = keys, values
    queries_heads = queries.reshape(head_shape)
    keys_heads, values_heads = all_keys.reshape(head_shape), all_values.reshape(head_shape)
    attended, lse = attention_forward(
        queries_heads, keys_heads, values_heads, query_segment, key_segment
    )
    attended = attended.reshape(count, -1)
    branch = sum_tokens(nn(attended, weight_merge))
    residual = own_part(inputs).astype(f32) + (branch + vectors[0])
    scaled_one, inverse_one, normed_one = norm_forward(residual, vectors[1], vectors[2])
    normed_low = gather_tokens(normed_one.astype(bf16))
    pre_gelu = nt(normed_low, weight_expand) + bias_hidden
    hidden = exact_gelu(pre_gelu).astype(bf16)
    shrunk = sum_tokens(nn(hidden, weight_shrink))
    scaled_two, inverse_two, final = norm_forward(
        normed_one + (shrunk + vectors[3]), vectors[4], vectors[5]
    )

    live = (own_part(query_segment) != 0).astype(f32)[:, None]
    upstream = to_own_tokens(cotangent).astype(f32) * live
    grad_sum_two, grad_gain_two, grad_shift_two = norm_backward(
        upstream, scaled_two, inverse_two, vectors[4]
    )
    grad_shrunk_own = grad_sum_two.astype(bf16)
    grad_shrunk = gather_tokens(grad_shrunk_own)
    grad_hidden = nt(grad_shrunk, weight_shrink)
    grad_pre = jax.vjp(exact_gelu, pre_gelu)[1](grad_hidden)[0].astype(bf16)
    grad_normed = grad_sum_two + sum_tokens(nn(grad_pre, weight_expand))
    grad_res, grad_gain_one, grad_shift_one = norm_backward(
        grad_normed, scaled_one, inverse_one, vectors[1]
    )
    grad_branch_own = grad_res.astype(bf16)
    grad_branch = gather_tokens(grad_branch_own)
    grad_attended = nt(grad_branch, weight_merge).astype(bf16)
    late_out, late_res, grad_attended = lax.optimization_barrier(
        (final.astype(bf16), grad_res, grad_attended)
    )
    layer_out, grad_res_columns = to_own_features(late_out), to_own_features(late_res)
    grad_queries, grad_keys, grad_values = attention_backward(
        queries_heads,
        keys_heads,
        values_heads,
        query_segment,
        key_segment,
        lse,
        grad_attended.reshape(head_shape),
    )
    grad_queries = grad_queries.reshape(count, -1)
    grad_keys_values = jnp.concatenate(
        (grad_keys.reshape(-1, heads * HEAD), grad_values.reshape(-1, heads * HEAD)), 1
    )
    grad_keys_values = grad_keys_values.astype(bf16)
    grad_keys, grad_values = (
        grad_keys_values[:, : heads * HEAD],
        grad_keys_values[:, heads * HEAD :],
    )
    grad_entry = (
        nn(grad_queries, weight_queries)
        + nn(grad_keys, weight_keys)
        + nn(grad_values, weight_values)
    )
    grad_tokens = sum_features(grad_entry, grad_res_columns)

    def assemble(local, row_axis, col_axis):
        full = jnp.zeros((local.shape[0], local.shape[1] * rows, D), bf16)
        full = lax.dynamic_update_slice(
            full, local.astype(bf16), (0, row * local.shape[1], 0)
        )
        full = lax.psum_scatter(full, "row", scatter_dimension=2, tiled=True)
        full = lax.psum_scatter(full, "col", scatter_dimension=1, tiled=True)
        return lax.psum(full, ("outer", "core")).astype(f32)

    grad_triple = assemble(
        jnp.stack(
            (tn(grad_queries, inputs), tn(grad_keys, inputs), tn(grad_values, inputs))
        ),
        0,
        2,
    ).transpose(2, 0, 1)
    grad_merge = assemble(tn(attended, grad_branch)[None], 1, 0)[0]
    grad_expand = assemble(tn(grad_pre, normed_low)[None], 0, 1)[0].T
    grad_shrink = assemble(tn(hidden, grad_shrunk)[None], 1, 0)[0]

    def column_sums(values):
        return jnp.sum(values, axis=0, dtype=f32)

    sum_hidden = column_sums(grad_pre)
    sum_queries, sum_values = column_sums(grad_queries), column_sums(grad_values)
    sum_rows = jnp.stack(
        (
            column_sums(grad_branch_own),
            grad_gain_one,
            grad_shift_one,
            column_sums(grad_shrunk_own),
            grad_gain_two,
            grad_shift_two,
        )
    )
    everywhere = ("outer", "core", "col")
    row_totals = lax.psum_scatter(sum_rows, "row", scatter_dimension=1, tiled=True)
    row_totals = lax.psum(row_totals, everywhere)

    def whole(local):
        full = jnp.zeros(local.shape[:-1] + (local.shape[-1] * rows,), f32)
        full = lax.dynamic_update_slice_in_dim(full, local, row * local.shape[-1], -1)
        full = lax.psum(full, everywhere + ("row",))
        share = full.shape[-1] // cols
        return lax.dynamic_slice_in_dim(full, col * share, share, -1)

    grad_pair = whole(jnp.stack((sum_queries, sum_values)))
    grad_expand_bias = whole(sum_hidden)

    return (
        layer_out,
        grad_tokens,
        grad_triple,
        grad_pair,
        grad_merge,
        row_totals[0],
        row_totals[1],
        row_totals[2],
        grad_expand,
        grad_expand_bias,
        grad_shrink,
        row_totals[3],
        row_totals[4],
        row_totals[5],
    )


def shards(tokens, *others):
    sizes = [size(axis) for axis in ("outer", "core", "row", "col")]
    if sizes == [2, 2, 2, 4] and 2 * tokens.shape[0] == LEN:
        return layer(tokens, *others)
    return layer_anywhere(tokens, *others)


def solution(mesh):
    sizes = mesh.shape
    axes = ("outer", "core", "row", "col")
    split = Mesh(
        mesh.devices.reshape(sizes["dp"] // 2, 2, sizes["row"], sizes["col"]), axes
    )
    dp = ("outer", "core")
    activations = P(("outer", "core", "col"), "row")
    return jax.shard_map(
        shards,
        mesh=split,
        in_specs=(
            activations,
            P(dp),
            P("row", None, "col"),
            P(None, "col"),
            P("col", "row"),
            P("row"),
            P("row"),
            P("row"),
            P("row", "col"),
            P("col"),
            P("col", "row"),
            P("row"),
            P("row"),
            P("row"),
            activations,
        ),
        out_specs=(
            activations,
            activations,
            P("row", None, "col"),
            P(None, "col"),
            P("col", "row"),
            P("row"),
            P("row"),
            P("row"),
            P("row", "col"),
            P("col"),
            P("col", "row"),
            P("row"),
            P("row"),
            P("row"),
        ),
        check_vma=False,
    )
```

```python
import functools

import jax
import jax.numpy as jnp
from jax import lax
from jax.experimental import pallas as pl
from jax.experimental.pallas import tpu as pltpu
from jax.sharding import Mesh, PartitionSpec as P

D = 1024
HEAD = 64
LEN = 1024
epsilon = 1e-05
masked_score = -1e30
bf16 = jnp.bfloat16
f32 = jnp.float32


def size(axis):
    return lax.axis_size(axis)


def place(axis):
    return lax.axis_index(axis)


def pair(values, axis):
    return lax.ppermute(values, axis, [(0, 1), (1, 0)])


def after(values, *others):
    return lax.optimization_barrier((values,) + others)[0]


def together(*arrays):
    return lax.optimization_barrier(arrays)


def shift(values, step):
    count = size("col")
    return lax.ppermute(values, "col", [(i, (i + step) % count) for i in range(count)])


def across(values, bits):
    return lax.ppermute(values, "col", [(i, i ^ bits) for i in range(size("col"))])


def by_place(bit, own, other, axis):
    return jnp.where(
        bit == 0,
        jnp.concatenate((own, other), axis),
        jnp.concatenate((other, own), axis),
    )


def nt(left, right, kind=f32):
    return lax.dot_general(
        left, right, (((1,), (1,)), ((), ())), preferred_element_type=f32
    ).astype(kind)


def nn(left, right, kind=f32):
    return lax.dot_general(
        left, right, (((1,), (0,)), ((), ())), preferred_element_type=f32
    ).astype(kind)


def tn(left, right, kind=f32):
    return lax.dot_general(
        left, right, (((0,), (0,)), ((), ())), preferred_element_type=f32
    ).astype(kind)


def swap_sequences(values):
    count = size("col")
    perm = []
    for core in range(2):
        for col in range(count):
            half, other = col % 2, col - col % 2
            target = (half, other + core)
            perm.append((core * count + col, target[0] * count + target[1]))
    return lax.ppermute(values, ("core", "col"), perm)


def own_first(values):
    if size("row") != 2:
        return values
    half = values.shape[0] // 2
    return jnp.where(place("row") == 0, values, jnp.roll(values, half, axis=0))


def own_part(values):
    share = values.shape[0] // size("row")
    if size("row") == 2:
        return values[:share]
    return lax.dynamic_slice_in_dim(values, place("row") * share, share)


def gather_features(values):
    if size("row") == 2:
        full = by_place(place("row"), values, pair(values, "row"), 1)
        return own_first(full)
    return lax.all_gather(values, "row", axis=1, tiled=True)


def gather_tokens(values):
    if size("row") == 2:
        return jnp.concatenate((values, pair(values, "row")), 0)
    return lax.all_gather(values, "row", axis=0, tiled=True)


def sum_tokens(partial):
    if size("row") == 2:
        share = partial.shape[0] // 2
        return partial[:share] + pair(partial[share:].astype(bf16), "row").astype(f32)
    return lax.psum_scatter(partial, "row", scatter_dimension=0, tiled=True)


def to_own_tokens(values):
    if size("row") == 2:
        bit = place("row")
        ordered = own_first(values)
        share = values.shape[0] // 2
        return by_place(bit, ordered[:share], pair(ordered[share:], "row"), 1)
    return lax.all_to_all(values, "row", 0, 1, tiled=True)


def to_own_features(values):
    if size("row") == 2:
        bit = place("row")
        half = values.shape[1] // 2
        low, high = values[:, :half], values[:, half:]
        own = jnp.where(bit == 0, low, high)
        other = pair(jnp.where(bit == 0, high, low), "row")
        return by_place(bit, own, other, 0)
    return lax.all_to_all(values, "row", 1, 0, tiled=True)


def sum_features(partial, addend):
    if size("row") == 2:
        half = partial.shape[1] // 2
        low, high = partial[:, :half], partial[:, half:]
        bit = place("row")
        got = pair(jnp.where(bit == 0, high, low).astype(bf16), "row").astype(f32)
        got = jnp.roll(got, partial.shape[0] // 2, axis=0)
        return own_first(jnp.where(bit == 0, low, high) + got) + addend
    return lax.psum_scatter(partial, "row", scatter_dimension=1, tiled=True) + addend


class Held:
    def __init__(self, **arrays):
        vars(self).update(arrays)

    update = __init__


def step_of(held):
    return Held(**lax.optimization_barrier(vars(held)))


def halves(values):
    middle = values.shape[0] // 2
    return values[:middle], values[middle:]


def three_groups(triple, merge, expand, shrink):
    depth = triple.shape[0]
    heads = triple.transpose(1, 2, 0).reshape(3, 2, 2, 1, HEAD, depth)
    out = merge.reshape(1, 2, 2, 1, HEAD, depth)
    keys_values = jnp.concatenate((heads[1], heads[2]), 3 - 1)
    queries_merge = jnp.concatenate((heads[0], out[0]), 3 - 1)
    attend = jnp.stack((keys_values, queries_merge), 2).reshape(2, 2, 2, 2 * HEAD, depth)
    widen = expand.T.reshape(2, 2, 2, -1, depth)
    narrow = shrink.reshape(2, 2, 2, -1, depth)
    return attend, widen, narrow


def my_quarter(group):
    some = lax.dynamic_index_in_dim(group, place("outer"), 1, keepdims=False)
    return lax.dynamic_index_in_dim(some, place("core"), 1, keepdims=False)


def exchange_rows(quarter):
    bit = place("row")
    mine = jnp.where(bit == 0, quarter[0], quarter[1])
    other = pair(jnp.where(bit == 0, quarter[1], quarter[0]), "row")
    return by_place(bit, mine, other, 1)


STEPS = (1, 3, 2)
BACK = (2, 1, 3)


def own_core_half(parts, pairs):
    count = size("col")
    return jnp.stack(
        [jnp.stack([group[step] for step in range(count)]) for group in (parts, pairs)]
    )


def gather_attend(quarter):
    parts = {0: quarter}
    for step in STEPS:
        parts[step] = shift(quarter, step)
    pairs = {step: pair(parts[step], "outer") for step in (0,) + STEPS}
    return own_core_half(parts, pairs), parts[2], pairs[2]


def collect_row(last):
    bit = place("row")
    half = last.shape[1] // 2
    low, high = last[:, :half].astype(bf16), last[:, half:].astype(bf16)
    mine = jnp.where(bit == 0, low, high)
    got = pair(jnp.where(bit == 0, high, low), "row")
    return jnp.stack((jnp.where(bit == 0, mine, got), jnp.where(bit == 0, got, mine)))


def ungroup(attend):
    depth = attend.shape[-1]
    heads = attend.reshape(4, 2, 2, HEAD, depth)
    keys, values = heads[:, 0, 0], heads[:, 0, 1]
    queries, merge = heads[:, 1, 0], heads[:, 1, 1]
    triple = jnp.stack((queries, keys, values)).reshape(3, 4 * HEAD, depth).transpose(2, 0, 1)
    return triple, merge.reshape(4 * HEAD, depth)


def flip(values, axis, bit):
    return jnp.where(bit == 0, values, jnp.flip(values, axis))


def dot(left, right, left_dim, right_dim):
    return lax.dot_general(
        left, right, (((left_dim,), (right_dim,)), ((), ())), preferred_element_type=f32
    )


def params():
    return pltpu.CompilerParams(vmem_limit_bytes=36 << 20)


def anywhere(arrays):
    return [pl.BlockSpec(memory_space=pl.ANY) for _ in arrays]


def pick(near_ref, far_ref, begin):
    part = slice(begin, begin + HEAD)
    return jnp.concatenate((near_ref[:, part], far_ref[:, part]), 0)


def attend_forward_kernel(q_ref, near_ref, far_ref, qs_ref, ks_ref, out_ref, lse_ref):
    same = ks_ref[...] == qs_ref[...]
    for head in range(2):
        part = slice(head * HEAD, (head + 1) * HEAD)
        keys = pick(near_ref, far_ref, 2 * head * HEAD)
        values = pick(near_ref, far_ref, (2 * head + 1) * HEAD)
        queries = q_ref[:, part] * jnp.asarray(HEAD**-0.5, bf16)
        scores = jnp.where(same, dot(keys, queries, 1, 1), masked_score)
        top = jnp.max(scores, axis=0, keepdims=True)
        weights = jnp.exp(scores - top)
        total = jnp.sum(weights, axis=0, keepdims=True)
        low = (weights * (1.0 / total)).astype(bf16)
        out_ref[part] = dot(values, low, 0, 0).astype(bf16)
        lse_ref[0, head : head + 1] = top + jnp.log(total)


def attend_forward(queries, near, far, query_segment, key_segment):
    tokens, width = queries.shape
    steps = width // (2 * HEAD)
    block = pl.BlockSpec((tokens, 4 * HEAD), lambda i: (0, i))
    return pl.pallas_call(
        attend_forward_kernel,
        grid=(steps,),
        in_specs=[
            pl.BlockSpec((tokens, 2 * HEAD), lambda i: (0, i)),
            block,
            block,
            pl.BlockSpec((1, tokens), lambda i: (0, 0)),
            pl.BlockSpec((2 * tokens, 1), lambda i: (0, 0)),
        ],
        out_specs=[
            pl.BlockSpec((2 * HEAD, tokens), lambda i: (i, 0)),
            pl.BlockSpec((1, 2, tokens), lambda i: (i, 0, 0)),
        ],
        out_shape=[
            jax.ShapeDtypeStruct((width, tokens), bf16),
            jax.ShapeDtypeStruct((steps, 2, tokens), f32),
        ],
        compiler_params=params(),
        cost_estimate=pl.CostEstimate(
            flops=32 * tokens * tokens * width,
            bytes_accessed=4 << 20,
            transcendentals=2 * tokens * tokens * width // HEAD,
        ),
    )(queries, near, far, query_segment, key_segment)


def attend_backward_kernel(
    q_ref, kv_ref, far_kv_ref, g_ref, qs_ref, ks_ref, lse_ref, dq_ref, near_ref, far_ref
):
    same = ks_ref[...] == qs_ref[...]
    scale = HEAD**-0.5
    near = near_ref.shape[0]
    for head in range(2):
        part = slice(head * HEAD, (head + 1) * HEAD)
        key_part = slice(2 * head * HEAD, (2 * head + 1) * HEAD)
        value_part = slice((2 * head + 1) * HEAD, (2 * head + 2) * HEAD)
        keys = pick(kv_ref, far_kv_ref, key_part.start)
        values = pick(kv_ref, far_kv_ref, value_part.start)
        queries = q_ref[:, part] * jnp.asarray(scale, bf16)
        grad = g_ref[:, part]
        scores = jnp.where(same, dot(keys, queries, 1, 1), masked_score)
        weights = jnp.exp(scores - lse_ref[0, head : head + 1])
        grad_weights = dot(values, grad, 1, 1)
        inner = jnp.sum(weights * grad_weights, axis=0, keepdims=True)
        grad_scores = (weights * (grad_weights - inner)).astype(bf16)
        dq_ref[part] = (dot(keys, grad_scores, 0, 0) * scale).astype(bf16)
        grad_keys = dot(grad_scores, queries, 1, 0)
        grad_values = dot(weights.astype(bf16), grad, 1, 0)
        near_ref[:, key_part], far_ref[:, key_part] = grad_keys[:near], grad_keys[near:]
        near_ref[:, value_part], far_ref[:, value_part] = grad_values[:near], grad_values[near:]


def attend_backward(queries, near, far, grad, query_segment, key_segment, lse, begin, steps):
    tokens = queries.shape[0]
    block = pl.BlockSpec((tokens, 4 * HEAD), lambda i: (0, begin + i))
    query_block = pl.BlockSpec((tokens, 2 * HEAD), lambda i: (0, begin + i))
    key_block = pl.BlockSpec((tokens, 4 * HEAD), lambda i: (0, i))
    return pl.pallas_call(
        attend_backward_kernel,
        grid=(steps,),
        in_specs=[
            query_block,
            block,
            block,
            query_block,
            pl.BlockSpec((1, tokens), lambda i: (0, 0)),
            pl.BlockSpec((2 * tokens, 1), lambda i: (0, 0)),
            pl.BlockSpec((1, 2, tokens), lambda i: (begin + i, 0, 0)),
        ],
        out_specs=[pl.BlockSpec((2 * HEAD, tokens), lambda i: (i, 0)), key_block, key_block],
        out_shape=[
            jax.ShapeDtypeStruct((2 * HEAD * steps, tokens), bf16),
            jax.ShapeDtypeStruct((tokens, 4 * HEAD * steps), f32),
            jax.ShapeDtypeStruct((tokens, 4 * HEAD * steps), f32),
        ],
        compiler_params=params(),
        cost_estimate=pl.CostEstimate(
            flops=160 * tokens * tokens * steps * HEAD,
            bytes_accessed=8 << 20,
            transcendentals=4 * tokens * tokens * steps,
        ),
    )(queries, near, far, grad, query_segment, key_segment, lse)


def attend_weights_kernel(
    which_ref, dkv_ref, dq_ref, out_in_ref, x_ref, g_ref, *rest, added, cols
):
    add_ref = rest[0] if added else None
    out_refs = rest[-cols:]

    def put(rows, value):
        value = value.reshape(cols, -1, D)
        for step, out_ref in enumerate(out_refs):
            term = value[step]
            if added:
                term = term + add_ref[0, step, rows].astype(f32)
            out_ref[rows] = term.astype(out_ref.dtype)

    @pl.when(which_ref[0] == 0)
    def _():
        put(slice(0, 2 * HEAD), dot(dkv_ref[...], x_ref[...], 0, 0))

    @pl.when(which_ref[0] == 1)
    def _():
        put(slice(0, HEAD), dot(dq_ref[...], x_ref[...], 1, 0))
        put(slice(HEAD, 2 * HEAD), dot(out_in_ref[...], g_ref[...], 1, 0))


def attend_weights(which, dkv, dq, out_in, x, g, begin, cols, kind, add=None, earlier=()):
    tokens = x.shape[0]
    full = pl.BlockSpec((tokens, D), lambda i, w: (0, 0))
    rows = pl.BlockSpec((cols * HEAD, tokens), lambda i, w: (begin, 0))
    specs = [pl.BlockSpec((tokens, cols * 2 * HEAD), lambda i, w: (0, begin)), rows, rows, full, full]
    given = [dkv, dq, out_in, x, g]
    if add is not None:
        specs.append(pl.BlockSpec((1, cols, 2 * HEAD, D), lambda i, w: (begin, 0, 0, 0)))
        given.append(add)
    return pl.pallas_call(
        functools.partial(attend_weights_kernel, added=add is not None, cols=cols),
        grid_spec=pltpu.PrefetchScalarGridSpec(
            num_scalar_prefetch=1,
            grid=(1,),
            in_specs=specs + anywhere(earlier),
            out_specs=[pl.BlockSpec((2 * HEAD, D), lambda i, w: (0, 0))] * cols,
        ),
        out_shape=[jax.ShapeDtypeStruct((2 * HEAD, D), kind)] * cols,
        compiler_params=params(),
        cost_estimate=pl.CostEstimate(
            flops=4 * tokens * D * cols * HEAD, bytes_accessed=6 << 20, transcendentals=0
        ),
    )(which, *given, *earlier)


def attend_far_kernel(which_ref, dkv_ref, dq_ref, out_in_ref, x_ref, g_ref, *rest):
    out_ref = rest[-1]
    cols = out_ref.shape[1]

    @pl.when(which_ref[0] == 0)
    def _():
        value = dot(dkv_ref[...], x_ref[...], 0, 0)
        out_ref[0] = value.reshape(cols, 2 * HEAD, D).astype(out_ref.dtype)

    @pl.when(which_ref[0] == 1)
    def _():
        for part, value in enumerate(
            (dot(dq_ref[...], x_ref[...], 1, 0), dot(out_in_ref[...], g_ref[...], 1, 0))
        ):
            rows = slice(part * HEAD, (part + 1) * HEAD)
            out_ref[0, :, rows] = value.reshape(cols, HEAD, D).astype(out_ref.dtype)


def attend_far_weights(which, dkv, dq, out_in, x, g, cols, *earlier):
    tokens = x.shape[0]
    full = pl.BlockSpec((tokens, D), lambda i, w: (0, 0))
    rows = pl.BlockSpec((cols * HEAD, tokens), lambda i, w: (i, 0))
    return pl.pallas_call(
        attend_far_kernel,
        grid_spec=pltpu.PrefetchScalarGridSpec(
            num_scalar_prefetch=1,
            grid=(2,),
            in_specs=[
                pl.BlockSpec((tokens, cols * 2 * HEAD), lambda i, w: (0, i)), rows, rows, full, full
            ]
            + anywhere(earlier),
            out_specs=pl.BlockSpec((1, cols, 2 * HEAD, D), lambda i, w: (i, 0, 0, 0)),
        ),
        out_shape=jax.ShapeDtypeStruct((2, cols, 2 * HEAD, D), bf16),
        compiler_params=params(),
        cost_estimate=pl.CostEstimate(
            flops=8 * tokens * D * cols * HEAD, bytes_accessed=6 << 20, transcendentals=0
        ),
    )(which, dkv, dq, out_in, x, g, *earlier)


SPARE = 8


def units_of(weights):
    units = (weights.shape[2] - SPARE) // 2
    expand = weights[:, :, :units].reshape(-1, D)
    shrink = weights[:, :, units : 2 * units].reshape(-1, D)
    return expand, shrink


def finish(total, keep_ref, send_ref):
    @pl.when(pl.program_id(0) == pl.num_programs(0) - 1)
    def _():
        half = total.shape[0] // 2
        keep_ref[...] = total[:half]
        send_ref[...] = total[half:].astype(bf16)


def add_to(total, term):
    @pl.when(pl.program_id(0) == 0)
    def _():
        total[...] = term

    @pl.when(pl.program_id(0) > 0)
    def _():
        total[...] += term


def hidden_forward_kernel(
    x_ref, bias_ref, weights_ref, hidden_ref, slope_ref, keep_ref, send_ref, total
):
    expand, shrink = units_of(weights_ref[0, 0:1])
    u = dot(x_ref[...], expand, 1, 1) + bias_ref[0]
    normal = 0.5 * (1.0 + lax.erf(u * (0.5**0.5)))
    slope_ref[...] = normal + u * (jnp.exp(-0.5 * u * u) * ((0.5 / jnp.pi) ** 0.5))
    hidden = (u * normal).astype(bf16)
    hidden_ref[...] = hidden
    add_to(total, dot(hidden, shrink, 1, 0))
    finish(total, keep_ref, send_ref)


def hidden_specs(tokens, weights):
    outer, core, cols, rows, _ = weights.shape
    units = (rows - SPARE) // 2
    steps, width = outer * core, cols * units
    block = pl.BlockSpec((1, 1, cols, rows, D), lambda i: (i // core, i % core, 0, 0, 0))
    wide = pl.BlockSpec((tokens, width), lambda i: (0, i))
    half = pl.BlockSpec((tokens // 2, D), lambda i: (0, 0))
    half_shapes = [
        jax.ShapeDtypeStruct((tokens // 2, D), f32),
        jax.ShapeDtypeStruct((tokens // 2, D), bf16),
    ]
    full = pl.BlockSpec((tokens, D), lambda i: (0, 0))
    row = pl.BlockSpec((1, 1, width), lambda i: (i, 0, 0))
    cost = pl.CostEstimate(
        flops=4 * tokens * D * steps * width, bytes_accessed=20 << 20, transcendentals=0
    )
    return steps, width, block, wide, half, half_shapes, full, row, cost


def hidden_forward(x, weights, bias):
    tokens = x.shape[0]
    steps, width, block, wide, half, half_shapes, full, row, cost = hidden_specs(tokens, weights)
    shape = (tokens, steps * width)
    return pl.pallas_call(
        hidden_forward_kernel,
        grid=(steps,),
        in_specs=[full, row, block],
        out_specs=[wide, wide, half, half],
        out_shape=[jax.ShapeDtypeStruct(shape, bf16), jax.ShapeDtypeStruct(shape, f32)]
        + half_shapes,
        scratch_shapes=[pltpu.VMEM((tokens, D), f32)],
        compiler_params=params(),
        cost_estimate=cost,
    )(x, bias, weights)


def hidden_backward_kernel(
    g_ref, slope_ref, weights_ref, grad_ref, sum_ref, keep_ref, send_ref, total
):
    expand, shrink = units_of(weights_ref[0, 0:1])
    grad = (dot(g_ref[...], shrink, 1, 1) * slope_ref[...]).astype(bf16)
    grad_ref[...] = grad
    sum_ref[0] = jnp.sum(grad.astype(f32), axis=0, keepdims=True)
    add_to(total, dot(grad, expand, 1, 0))
    finish(total, keep_ref, send_ref)


def hidden_backward(g, weights, slope):
    tokens = g.shape[0]
    steps, width, block, wide, half, half_shapes, full, row, cost = hidden_specs(tokens, weights)
    return pl.pallas_call(
        hidden_backward_kernel,
        grid=(steps,),
        in_specs=[full, wide, block],
        out_specs=[wide, row, half, half],
        out_shape=[
            jax.ShapeDtypeStruct((tokens, steps * width), bf16),
            jax.ShapeDtypeStruct((steps, 1, width), f32),
        ]
        + half_shapes,
        scratch_shapes=[pltpu.VMEM((tokens, D), f32)],
        compiler_params=params(),
        cost_estimate=cost,
    )(g, slope, weights)


def hidden_weights_kernel(grad_ref, hidden_ref, x_ref, g_ref, sum_ref, out_ref):
    cols, rows, _ = out_ref.shape[2:]
    units = (rows - SPARE) // 2
    for part, (left, right) in enumerate(((grad_ref, x_ref), (hidden_ref, g_ref))):
        value = dot(left[...], right[...], 0, 0).reshape(cols, units, D)
        out_ref[0, 0, :, part * units : (part + 1) * units] = value.astype(bf16)
    first = lax.broadcasted_iota(jnp.int32, (cols, SPARE, units), 1) == 0
    sums = jnp.where(first, sum_ref[0][:, None, :], 0.0).astype(bf16)
    out_ref[0, 0, :, 2 * units :] = jnp.zeros((cols, SPARE, D), bf16)
    for begin in (0, D // 2):
        out_ref[0, 0, :, 2 * units :, begin : begin + units] = sums


def hidden_weights(grad, hidden, x, g, sums, shape):
    tokens = x.shape[0]
    outer, core, cols, rows, _ = shape
    width = grad.shape[1] // (outer * core)
    wide = pl.BlockSpec((tokens, width), lambda i: (0, i))
    full = pl.BlockSpec((tokens, D), lambda i: (0, 0))
    return pl.pallas_call(
        hidden_weights_kernel,
        grid=(outer * core,),
        in_specs=[
            wide, wide, full, full, pl.BlockSpec((1, cols, width // cols), lambda i: (i, 0, 0))
        ],
        out_specs=pl.BlockSpec(
            (1, 1, cols, rows, D), lambda i: (i // core, i % core, 0, 0, 0)
        ),
        out_shape=jax.ShapeDtypeStruct(shape, bf16),
        compiler_params=params(),
        cost_estimate=pl.CostEstimate(
            flops=4 * tokens * D * grad.shape[1], bytes_accessed=16 << 20, transcendentals=0
        ),
    )(grad, hidden, x, g, sums)


def hidden_gradients_kernel(core_ref, own_ref, got_ref, expand_ref, shrink_ref, bias_ref):
    units = shrink_ref.shape[0]

    def put(ref):
        expand_ref[...] = ref[0, 0, :units].astype(f32).T
        shrink_ref[...] = ref[0, 0, units : 2 * units].astype(f32)
        bias_ref[0] = ref[0, 0, 2 * units :, :units].astype(f32)

    mine = pl.program_id(0) % 2 == core_ref[0]
    pl.when(mine)(lambda: put(own_ref))
    pl.when(jnp.logical_not(mine))(lambda: put(got_ref))


def hidden_gradients(core, own, got):
    rows, depth = own.shape[2:]
    units = (rows - SPARE) // 2
    piece = pl.BlockSpec((1, 1, rows, depth), lambda i, w: (i // 4, i // 2 % 2, 0, 0))
    expand, shrink, bias = pl.pallas_call(
        hidden_gradients_kernel,
        grid_spec=pltpu.PrefetchScalarGridSpec(
            num_scalar_prefetch=1,
            grid=(8,),
            in_specs=[piece, piece],
            out_specs=[
                pl.BlockSpec((depth, units), lambda i, w: (0, i)),
                pl.BlockSpec((units, depth), lambda i, w: (i, 0)),
                pl.BlockSpec((1, SPARE, units), lambda i, w: (i, 0, 0)),
            ],
        ),
        out_shape=[
            jax.ShapeDtypeStruct((depth, 8 * units), f32),
            jax.ShapeDtypeStruct((8 * units, depth), f32),
            jax.ShapeDtypeStruct((8, SPARE, units), f32),
        ],
        compiler_params=params(),
        cost_estimate=pl.CostEstimate(flops=1 << 20, bytes_accessed=6 << 20, transcendentals=0),
    )(core, own, got)
    return expand, shrink, bias[:, 0].reshape(-1)


def layer(
    tokens, segments, triple_weight, pair_bias, merge_weight, merge_bias, first_gain, first_shift,
    expand_weight, expand_bias, shrink_weight, shrink_bias, second_gain, second_shift, cotangent,
):
    cols = size("col")
    count = tokens.shape[0]
    own = count // 2
    heads = D // HEAD // 2
    row, col, core, outer = place("row"), place("col"), place("core"), place("outer")
    row_size, pair_size, hidden_size = merge_bias.shape[0], pair_bias.shape[1], expand_bias.shape[0]

    groups = three_groups(triple_weight, merge_weight, expand_weight, shrink_weight)
    attend_group = my_quarter(groups[0])
    row_vectors = jnp.stack(
        (merge_bias, first_gain, first_shift, shrink_bias, second_gain, second_shift)
    )
    column = jnp.concatenate(
        [
            lax.dynamic_slice_in_dim(vector, row * (vector.shape[0] // 2), vector.shape[0] // 2)
            for vector in (pair_bias[0], pair_bias[1], expand_bias)
        ]
    )
    moved = swap_sequences(tokens)
    quarter = exchange_rows(attend_group)
    pair_column, hidden_column = column[:pair_size], column[pair_size:].reshape(4, -1)
    pair_column = pair_column.reshape(2, 2, HEAD)
    pair_column = lax.dynamic_index_in_dim(pair_column, outer, 1, keepdims=False)
    pair_column = lax.dynamic_index_in_dim(pair_column, 1 - core, 0)
    hidden_column = lax.dynamic_index_in_dim(hidden_column, 2 * outer + core, 0)
    other_group = exchange_rows(
        jnp.concatenate([my_quarter(group) for group in groups[1:]], 1)
    )
    v = step_of(
        Held(
            quarter=quarter, moved=moved, other=segments.astype(f32), group=other_group, rows=row_vectors, pairs=pair_column,
            hidden=hidden_column, cot=cotangent,
        )
    )

    def beside(rows, value):
        spare = jnp.pad(value, ((0, SPARE - 1), (0, D - value.shape[1])))
        return jnp.concatenate((rows, spare), 0)

    quarter, moved = beside(v.quarter, v.pairs), v.moved
    parts = {0: quarter, 1: shift(quarter, 1), 3: shift(quarter, 3)}
    pairs = {0: pair(quarter, "outer")}
    got_tokens = pair(moved, "row")
    v.update(quarter=quarter, parts=parts, pairs=pairs, moved=moved, got=got_tokens)
    v = step_of(v)
    parts, pairs, quarter = v.parts, v.pairs, v.quarter
    parts[2] = shift(quarter, 2)
    pairs[1], pairs[3] = pair(parts[1], "outer"), pair(parts[3], "outer")
    mine = beside(v.group, v.hidden)
    hidden_all = lax.all_gather(mine, ("outer", "core", "col"), axis=0)
    hidden_all = hidden_all.reshape(2, 2, cols, -1, D)
    v.vectors = by_place(row, v.rows, pair(v.rows, "row"), 1)
    v.other = pair(v.other, "core")
    v = step_of(v)
    parts, pairs = v.parts, v.pairs
    pairs[2] = pair(parts[2], "outer")
    v.inputs = own_first(by_place(row, v.moved, v.got, 1))
    v = step_of(v)
    parts, pairs = v.parts, v.pairs
    rows = 2 * HEAD

    def without(group):
        return {step: group[step][:rows] for step in range(cols)}

    attend_own = own_core_half(without(parts), without(pairs))
    v.attend_own, v.attend_other = attend_own, pair(attend_own, "core")
    bias_own = jnp.stack(
        [group[step][rows, :HEAD] for group in (parts, pairs) for step in range(cols)]
    ).astype(f32)
    v.bias_own, v.bias_other = bias_own, pair(bias_own, "core")
    other = v.other.astype(jnp.int32)
    sequence = lax.dynamic_slice_in_dim(
        jnp.where(col % 2 == core, segments, other), (col // 2) * LEN, LEN
    ).reshape(2, count)
    query_segment = own_first(lax.dynamic_index_in_dim(sequence, core, 0, keepdims=False))
    far_segment = own_first(lax.dynamic_index_in_dim(sequence, 1 - core, 0, keepdims=False))
    key_segment = jnp.concatenate((query_segment, far_segment))
    segment_row, segment_column = query_segment[None], key_segment[:, None]
    vectors = v.vectors.astype(f32)
    v = step_of(
        Held(
            own=v.attend_own, other=v.attend_other, cot=v.cot, inputs=v.inputs,
            vectors=vectors, biases=(v.bias_own, v.bias_other),
        )
    )
    attend_own, attend_other, inputs, vectors = v.own, v.other, v.inputs, v.vectors
    first = jnp.where(core == 0, attend_own, attend_other)
    second = jnp.where(core == 0, attend_other, attend_own)
    bias_values = jnp.where(core == 0, v.biases[0], v.biases[1])
    bias_keys_values = jnp.stack((jnp.zeros_like(bias_values), bias_values), 1).reshape(-1)
    bias_queries = jnp.where(core == 0, v.biases[1], v.biases[0]).reshape(-1)
    weight_keys_values = first.reshape(-1, D)
    second = second.reshape(heads, 2, HEAD, D)
    weight_queries, weight_merge = second[:, 0].reshape(-1, D), second[:, 1].reshape(-1, D)

    cut = heads * HEAD // 2
    steps = heads // 4
    keys_values = (nt(inputs, weight_keys_values) + bias_keys_values).astype(bf16)
    v.far = pair(keys_values, "core")
    v.queries = (nt(inputs, weight_queries) + bias_queries).astype(bf16)
    v.keys_values = keys_values
    v.weights = (weight_keys_values, weight_queries, weight_merge)
    v = step_of(v)
    queries = v.queries
    keys_values, far_keys_values = v.keys_values, v.far
    v.attended, v.lse = attend_forward(
        queries, keys_values, far_keys_values, segment_row, segment_column
    )
    v = step_of(v)
    attended, lse = v.attended, v.lse
    queries, keys_values, far_keys_values = v.queries, v.keys_values, v.far
    weight_keys_values, weight_queries, weight_merge = v.weights
    branch = sum_tokens(tn(attended, weight_merge))
    residual = inputs[:own].astype(f32) + (branch + vectors[0])
    scaled_one, inverse_one, normed_one = norm_forward(residual, vectors[1], vectors[2])
    normed_low = gather_tokens(normed_one.astype(bf16))
    cotangent = swap_sequences(v.cot)
    normed_low, normed_one, hidden_all, cotangent = lax.optimization_barrier(
        (normed_low, normed_one, hidden_all, cotangent)
    )
    units = hidden_size // 8
    bias_hidden = hidden_all[:, :, :, 2 * units, :units].reshape(4, 1, -1).astype(f32)
    hidden, slope, keep, send = hidden_forward(normed_low, hidden_all, bias_hidden)
    upstream = to_own_tokens(cotangent)
    keep, send, upstream = lax.optimization_barrier((keep, send, upstream))
    shrunk = keep + pair(send, "row").astype(f32)
    scaled_two, inverse_two, final = norm_forward(
        normed_one + (shrunk + vectors[3]), vectors[4], vectors[5]
    )
    live = (query_segment[:own] != 0).astype(f32)[:, None]
    upstream = upstream.astype(f32) * live
    grad_sum_two, grad_gain_two, grad_shift_two = norm_backward(
        upstream, scaled_two, inverse_two, vectors[4]
    )
    grad_shrunk_own = grad_sum_two.astype(bf16)
    grad_shrunk = gather_tokens(grad_shrunk_own)
    grad_shrunk, out = lax.optimization_barrier((grad_shrunk, final.astype(bf16)))
    grad_pre, sum_hidden, keep, send = hidden_backward(grad_shrunk, hidden_all, slope)
    out = to_own_features(out)
    cut = heads * HEAD // 2
    steps = heads // 4
    spare = sum_hidden.reshape(4, cols, units)
    v = Held(
        grad_pre=grad_pre, hidden=hidden, normed=normed_low, g=grad_shrunk, inputs=inputs,
        attended=attended, queries=queries, keys_values=keys_values, lse=lse,
        far_keys_values=far_keys_values, keep=keep, send=send, sum_two=grad_sum_two,
        scaled_one=scaled_one, inverse_one=inverse_one, out=out, shrunk_own=grad_shrunk_own,
        sum_two_rows=(grad_gain_two, grad_shift_two), spare=spare, vectors=vectors,
        weight_merge=weight_merge, weight_queries=weight_queries,
        weight_keys_values=weight_keys_values,
    )

    v = step_of(v)
    v.got = pair(v.send, "row")
    hidden_grads = hidden_weights(
        v.grad_pre, v.hidden, v.normed, v.g, v.spare, hidden_all.shape
    )
    hidden_sums = lax.psum_scatter(
        hidden_grads.reshape(-1, D), ("outer", "core", "col"), scatter_dimension=0, tiled=True
    )
    v = step_of(v)
    grad_normed = v.sum_two + (v.keep + v.got.astype(f32))
    res, grad_gain_one, grad_shift_one = norm_backward(
        grad_normed, v.scaled_one, v.inverse_one, v.vectors[1]
    )
    branch_own = res.astype(bf16)
    branch_got = pair(branch_own, "row")
    sum_rows = jnp.stack(
        (
            jnp.sum(branch_own, axis=0, dtype=f32),
            grad_gain_one,
            grad_shift_one,
            jnp.sum(v.shrunk_own, axis=0, dtype=f32),
            *v.sum_two_rows,
        )
    )
    v = Held(
        inputs=v.inputs, attended=v.attended, queries=v.queries, out=v.out,
        keys_values=v.keys_values, far_keys_values=v.far_keys_values, lse=v.lse,
        weight_merge=v.weight_merge, weight_queries=v.weight_queries,
        weight_keys_values=v.weight_keys_values,
    )
    v.branch = jnp.concatenate((branch_own, branch_got), 0)
    v.grad_attended = nt(v.branch, v.weight_merge, bf16)
    v.sum_rows = sum_rows
    middle = D // 2
    v.res_mine = jnp.where(row == 0, res[:, :middle], res[:, middle:])
    v.res_send = halves(jnp.where(row == 0, res[:, middle:], res[:, :middle]))
    v = step_of(v)
    shared = (
        v.queries, v.keys_values, v.far_keys_values, v.grad_attended, segment_row,
        segment_column, v.lse,
    )
    v.second = attend_backward(*shared, steps, steps)
    v.res_got = [pair(v.res_send[0], "row")]
    v = step_of(v)
    shared = (
        v.queries, v.keys_values, v.far_keys_values, v.grad_attended, segment_row,
        segment_column, v.lse,
    )
    v.far = pair(v.second[2], "core")
    v.first = attend_backward(*shared, 0, steps)
    v.res_got.append(pair(v.res_send[1], "row"))
    v = step_of(v)
    far = pair(v.first[2], "core")
    dkv_second = (v.second[1] + v.far).astype(bf16)
    v.grad_queries = jnp.concatenate((v.first[0], v.second[0]), 0)
    v.entry = tn(v.grad_queries, v.weight_queries)
    dkv_first = (v.first[1] + far).astype(bf16)
    v.grad_keys_values = jnp.concatenate((dkv_first, dkv_second), 1)
    v = step_of(v)
    which = core.reshape(1)
    part = (v.grad_keys_values, v.grad_queries, v.attended, v.inputs, v.branch)
    v.far = attend_far_weights((1 - core).reshape(1), *part, cols)
    v = step_of(v)
    v.far = pair(v.far, "core")
    entry = v.entry + nn(v.grad_keys_values, v.weight_keys_values)
    v.res_columns = by_place(row, v.res_mine, jnp.concatenate(v.res_got, 0), 0)
    v.entry_keep = jnp.where(row == 0, entry[:, :middle], entry[:, middle:])
    v.entry_send = jnp.where(row == 0, entry[:, middle:], entry[:, :middle]).astype(bf16)
    v = step_of(v)
    part = (v.grad_keys_values, v.grad_queries, v.attended, v.inputs, v.branch)
    v.mates = attend_weights(which, *part, 1, cols, bf16, v.far)
    v = step_of(v)
    part = (v.grad_keys_values, v.grad_queries, v.attended, v.inputs, v.branch)
    v.got = {2: pair(v.mates[2], "outer")}
    v.entry_got = pair(v.entry_send, "row")
    v.own = attend_weights(which, *part, 0, cols, f32, v.far)
    sum_queries = jnp.sum(v.grad_queries, axis=1, dtype=f32)
    sum_values = jnp.sum(v.grad_keys_values, axis=0, dtype=f32).reshape(heads, 2, HEAD)[:, 1]
    sum_pair = jnp.stack((sum_queries, sum_values.reshape(-1))).reshape(2, 2, cols, HEAD)
    sum_pair = flip(sum_pair.transpose(2, 0, 1, 3), 2, outer).reshape(cols, -1)
    length = sum_pair.shape[1]
    sum_pair = jnp.concatenate(
        [
            lax.dynamic_index_in_dim(sum_pair, (col - place_of) % cols, 0, keepdims=False)
            for place_of in range(cols)
        ]
    )
    v.total = jnp.concatenate((sum_pair, v.sum_rows.reshape(-1)))
    v = step_of(v)

    def to_send(sums, got, step):
        return (sums[step] + got.astype(f32)).astype(bf16)

    got = v.got
    got[1], got[3] = pair(v.mates[1], "outer"), pair(v.mates[3], "outer")
    v.two = shift(to_send(v.own, got[2], 2), -2)
    total = v.total
    v.total = total + lax.ppermute(total, "col", [(i, i ^ 1) for i in range(cols)])
    entry = jnp.roll(v.entry_got.astype(f32), own, axis=0)
    v.grad_tokens = own_first(v.entry_keep + entry) + v.res_columns
    v = step_of(v)
    v.one = to_send(v.own, v.got[1], 1)
    v.three = to_send(v.own, v.got[3], 3)
    v = step_of(v)
    v.one, v.three = shift(v.one, -1), shift(v.three, -3)
    v.got[0] = pair(v.mates[0], "outer")
    total = v.total
    v.total = total + lax.ppermute(total, "col", [(i, i ^ 2) for i in range(cols)])
    v = step_of(v)
    attend_rest = v.own[0] + v.got[0].astype(f32)
    for term in (v.one, v.two, v.three):
        attend_rest = attend_rest + term.astype(f32)
    v = step_of(
        Held(
            rest=attend_rest, hidden=hidden_sums, total=v.total, out=v.out,
            grad_tokens=v.grad_tokens,
        )
    )
    v.out = swap_sequences(v.out)
    v.block = collect_row(v.hidden)
    v.total = v.total + pair(v.total, "core")
    v = step_of(v)
    v.block_got = pair(v.block, "outer")
    v.grad_tokens = swap_sequences(v.grad_tokens)
    v.attend = collect_row(v.rest)
    v = step_of(v)
    v.block = by_place(outer, v.block[:, None], v.block_got[:, None], 1)
    v = step_of(v)
    v.attend_got = pair(v.attend, "outer")
    v.total_got = pair(v.total, "outer")
    v.block_got = pair(v.block, "core")
    v = step_of(v)
    total = v.total + v.total_got
    layer_out, grad_tokens = v.out, v.grad_tokens
    attend = by_place(outer, v.attend[:, None], v.attend_got[:, None], 1)
    attend_got = pair(attend, "core")
    grad_expand, grad_shrink, grad_expand_bias = hidden_gradients(which, v.block, v.block_got)
    attend = by_place(core, attend[:, :, None], attend_got[:, :, None], 2).astype(f32)
    grad_triple, grad_merge = ungroup(attend)
    mine = lax.dynamic_slice_in_dim(total, col * length, length)
    sum_rows = total[cols * length :].reshape(6, 2, row_size)
    low, high = sum_rows[:, 0].reshape(-1), sum_rows[:, 1].reshape(-1)
    got = pair(jnp.concatenate((mine, jnp.where(row == 0, high, low))), "row")
    totals = (jnp.where(row == 0, low, high) + got[length:]).reshape(6, row_size)
    got = got[:length]
    short = 2 * HEAD
    grad_pair = by_place(
        row, mine[: 2 * short].reshape(2, short), got[: 2 * short].reshape(2, short), 1
    )
    return (
        layer_out, grad_tokens, grad_triple, grad_pair, grad_merge, totals[0], totals[1], totals[2],
        grad_expand, grad_expand_bias, grad_shrink, totals[3], totals[4], totals[5],
    )


def masked(scores, query_segment, key_segment):
    same = query_segment[:, None] == key_segment[None, :]
    return jnp.where(same[None], scores, masked_score)


def attention_forward(queries, keys, values, query_segment, key_segment):
    scores = jnp.einsum("qhd,khd->hqk", queries, keys, preferred_element_type=f32)
    scores = masked(scores * HEAD**-0.5, query_segment, key_segment)
    top = jnp.max(scores, axis=-1, keepdims=True)
    weights = jnp.exp(scores - top)
    total = jnp.sum(weights, axis=-1, keepdims=True)
    low = (weights / total).astype(bf16)
    attended = jnp.einsum("hqk,khd->qhd", low, values, preferred_element_type=f32)
    return attended.astype(bf16), top + jnp.log(total)


def attention_backward(queries, keys, values, query_segment, key_segment, lse, grad):
    scores = jnp.einsum("qhd,khd->hqk", queries, keys, preferred_element_type=f32)
    scores = masked(scores * HEAD**-0.5, query_segment, key_segment)
    weights = jnp.exp(scores - lse)
    grad_weights = jnp.einsum("qhd,khd->hqk", grad, values, preferred_element_type=f32)
    inner = jnp.sum(weights * grad_weights, axis=-1, keepdims=True)
    grad_scores = (weights * (grad_weights - inner)).astype(bf16)
    scale = HEAD**-0.5
    grad_queries = jnp.einsum("hqk,khd->qhd", grad_scores, keys, preferred_element_type=f32) * scale
    grad_keys = jnp.einsum("hqk,qhd->khd", grad_scores, queries, preferred_element_type=f32) * scale
    grad_values = jnp.einsum(
        "hqk,qhd->khd", weights.astype(bf16), grad, preferred_element_type=f32
    )
    return grad_queries.astype(bf16), grad_keys, grad_values


def norm_forward(values, gain, shift):
    center = jnp.mean(values, axis=1, keepdims=True)
    inverse = lax.rsqrt(
        jnp.mean(values * values, axis=1, keepdims=True) - center * center + epsilon
    )
    scaled = (values - center) * inverse
    return scaled, inverse, scaled * gain + shift


def norm_backward(upstream, scaled, inverse, gain):
    through = upstream * gain
    grad = inverse * (
        through
        - jnp.mean(through, axis=1, keepdims=True)
        - scaled * jnp.mean(through * scaled, axis=1, keepdims=True)
    )
    return grad, jnp.sum(upstream * scaled, axis=0), jnp.sum(upstream, axis=0)


def exact_gelu(values):
    return jax.nn.gelu(values, approximate=False)


def layer_anywhere(
    tokens,
    segments,
    triple_weight,
    pair_bias,
    merge_weight,
    merge_bias,
    first_gain,
    first_shift,
    expand_weight,
    expand_bias,
    shrink_weight,
    shrink_bias,
    second_gain,
    second_shift,
    cotangent,
):
    rows, cols = size("row"), size("col")
    count = tokens.shape[0]
    own = count // rows
    heads = D // HEAD // rows
    row, col = place("row"), place("col")

    query_segment = lax.dynamic_slice_in_dim(segments, col * count, count)
    key_segment = query_segment

    row_size, pair_size, hidden_size = merge_bias.shape[0], pair_bias.shape[1], expand_bias.shape[0]
    row_vectors = jnp.stack(
        (merge_bias, first_gain, first_shift, shrink_bias, second_gain, second_shift)
    )
    vectors = lax.all_gather(row_vectors, "row", axis=1, tiled=True)

    def mine_of(full, axis=0):
        share = full.shape[axis] // rows
        return lax.dynamic_slice_in_dim(full, row * share, share, axis)

    bias_pair = mine_of(lax.all_gather(pair_bias, "col", axis=1, tiled=True), 1)
    bias_queries, bias_values = bias_pair[0], bias_pair[1]
    bias_hidden = mine_of(lax.all_gather(expand_bias, "col", axis=0, tiled=True)).astype(f32)
    vectors = vectors.astype(f32)

    triple = lax.all_gather(triple_weight, "col", axis=2, tiled=True)
    triple = lax.all_gather(triple, "row", axis=0, tiled=True).transpose(1, 2, 0)
    merge = lax.all_gather(merge_weight, "col", axis=0, tiled=True)
    merge = lax.all_gather(merge, "row", axis=1, tiled=True)
    expand = lax.all_gather(expand_weight, "col", axis=1, tiled=True)
    expand = lax.all_gather(expand, "row", axis=0, tiled=True).T
    shrink = lax.all_gather(shrink_weight, "col", axis=0, tiled=True)
    shrink = lax.all_gather(shrink, "row", axis=1, tiled=True)

    weight_queries, weight_keys, weight_values = (mine_of(triple[j]) for j in range(3))
    weight_merge, weight_expand, weight_shrink = mine_of(merge), mine_of(expand), mine_of(shrink)

    inputs = gather_features(tokens)
    head_shape = (-1, heads, HEAD)
    queries = (nt(inputs, weight_queries) + bias_queries.astype(f32)).astype(bf16)
    keys = nt(inputs, weight_keys).astype(bf16)
    values = (nt(inputs, weight_values) + bias_values.astype(f32)).astype(bf16)
    all_keys, all_values = keys, values
    queries_heads = queries.reshape(head_shape)
    keys_heads, values_heads = all_keys.reshape(head_shape), all_values.reshape(head_shape)
    attended, lse = attention_forward(
        queries_heads, keys_heads, values_heads, query_segment, key_segment
    )
    attended = attended.reshape(count, -1)
    branch = sum_tokens(nn(attended, weight_merge))
    residual = own_part(inputs).astype(f32) + (branch + vectors[0])
    scaled_one, inverse_one, normed_one = norm_forward(residual, vectors[1], vectors[2])
    normed_low = gather_tokens(normed_one.astype(bf16))
    pre_gelu = nt(normed_low, weight_expand) + bias_hidden
    hidden = exact_gelu(pre_gelu).astype(bf16)
    shrunk = sum_tokens(nn(hidden, weight_shrink))
    scaled_two, inverse_two, final = norm_forward(
        normed_one + (shrunk + vectors[3]), vectors[4], vectors[5]
    )

    live = (own_part(query_segment) != 0).astype(f32)[:, None]
    upstream = to_own_tokens(cotangent).astype(f32) * live
    grad_sum_two, grad_gain_two, grad_shift_two = norm_backward(
        upstream, scaled_two, inverse_two, vectors[4]
    )
    grad_shrunk_own = grad_sum_two.astype(bf16)
    grad_shrunk = gather_tokens(grad_shrunk_own)
    grad_hidden = nt(grad_shrunk, weight_shrink)
    grad_pre = jax.vjp(exact_gelu, pre_gelu)[1](grad_hidden)[0].astype(bf16)
    grad_normed = grad_sum_two + sum_tokens(nn(grad_pre, weight_expand))
    grad_res, grad_gain_one, grad_shift_one = norm_backward(
        grad_normed, scaled_one, inverse_one, vectors[1]
    )
    grad_branch_own = grad_res.astype(bf16)
    grad_branch = gather_tokens(grad_branch_own)
    grad_attended = nt(grad_branch, weight_merge).astype(bf16)
    late_out, late_res, grad_attended = lax.optimization_barrier(
        (final.astype(bf16), grad_res, grad_attended)
    )
    layer_out, grad_res_columns = to_own_features(late_out), to_own_features(late_res)
    grad_queries, grad_keys, grad_values = attention_backward(
        queries_heads,
        keys_heads,
        values_heads,
        query_segment,
        key_segment,
        lse,
        grad_attended.reshape(head_shape),
    )
    grad_queries = grad_queries.reshape(count, -1)
    grad_keys_values = jnp.concatenate(
        (grad_keys.reshape(-1, heads * HEAD), grad_values.reshape(-1, heads * HEAD)), 1
    )
    grad_keys_values = grad_keys_values.astype(bf16)
    grad_keys, grad_values = (
        grad_keys_values[:, : heads * HEAD],
        grad_keys_values[:, heads * HEAD :],
    )
    grad_entry = (
        nn(grad_queries, weight_queries)
        + nn(grad_keys, weight_keys)
        + nn(grad_values, weight_values)
    )
    grad_tokens = sum_features(grad_entry, grad_res_columns)

    def assemble(local, row_axis, col_axis):
        full = jnp.zeros((local.shape[0], local.shape[1] * rows, D), bf16)
        full = lax.dynamic_update_slice(
            full, local.astype(bf16), (0, row * local.shape[1], 0)
        )
        full = lax.psum_scatter(full, "row", scatter_dimension=2, tiled=True)
        full = lax.psum_scatter(full, "col", scatter_dimension=1, tiled=True)
        return lax.psum(full, ("outer", "core")).astype(f32)

    grad_triple = assemble(
        jnp.stack(
            (tn(grad_queries, inputs), tn(grad_keys, inputs), tn(grad_values, inputs))
        ),
        0,
        2,
    ).transpose(2, 0, 1)
    grad_merge = assemble(tn(attended, grad_branch)[None], 1, 0)[0]
    grad_expand = assemble(tn(grad_pre, normed_low)[None], 0, 1)[0].T
    grad_shrink = assemble(tn(hidden, grad_shrunk)[None], 1, 0)[0]

    def column_sums(values):
        return jnp.sum(values, axis=0, dtype=f32)

    sum_hidden = column_sums(grad_pre)
    sum_queries, sum_values = column_sums(grad_queries), column_sums(grad_values)
    sum_rows = jnp.stack(
        (
            column_sums(grad_branch_own),
            grad_gain_one,
            grad_shift_one,
            column_sums(grad_shrunk_own),
            grad_gain_two,
            grad_shift_two,
        )
    )
    everywhere = ("outer", "core", "col")
    row_totals = lax.psum_scatter(sum_rows, "row", scatter_dimension=1, tiled=True)
    row_totals = lax.psum(row_totals, everywhere)

    def whole(local):
        full = jnp.zeros(local.shape[:-1] + (local.shape[-1] * rows,), f32)
        full = lax.dynamic_update_slice_in_dim(full, local, row * local.shape[-1], -1)
        full = lax.psum(full, everywhere + ("row",))
        share = full.shape[-1] // cols
        return lax.dynamic_slice_in_dim(full, col * share, share, -1)

    grad_pair = whole(jnp.stack((sum_queries, sum_values)))
    grad_expand_bias = whole(sum_hidden)

    return (
        layer_out,
        grad_tokens,
        grad_triple,
        grad_pair,
        grad_merge,
        row_totals[0],
        row_totals[1],
        row_totals[2],
        grad_expand,
        grad_expand_bias,
        grad_shrink,
        row_totals[3],
        row_totals[4],
        row_totals[5],
    )


def shards(tokens, *others):
    sizes = [size(axis) for axis in ("outer", "core", "row", "col")]
    if sizes == [2, 2, 2, 4] and 2 * tokens.shape[0] == LEN:
        return layer(tokens, *others)
    return layer_anywhere(tokens, *others)


def solution(mesh):
    sizes = mesh.shape
    axes = ("outer", "core", "row", "col")
    split = Mesh(
        mesh.devices.reshape(sizes["dp"] // 2, 2, sizes["row"], sizes["col"]), axes
    )
    dp = ("outer", "core")
    activations = P(("outer", "core", "col"), "row")
    return jax.shard_map(
        shards,
        mesh=split,
        in_specs=(
            activations,
            P(dp),
            P("row", None, "col"),
            P(None, "col"),
            P("col", "row"),
            P("row"),
            P("row"),
            P("row"),
            P("row", "col"),
            P("col"),
            P("col", "row"),
            P("row"),
            P("row"),
            P("row"),
            activations,
        ),
        out_specs=(
            activations,
            activations,
            P("row", None, "col"),
            P(None, "col"),
            P("col", "row"),
            P("row"),
            P("row"),
            P("row"),
            P("row", "col"),
            P("col"),
            P("col", "row"),
            P("row"),
            P("row"),
            P("row"),
        ),
        check_vma=False,
    )
```

```python
import functools

import jax
import jax.numpy as jnp
from jax import lax
from jax.experimental import pallas as pl
from jax.experimental.pallas import tpu as pltpu
from jax.sharding import Mesh, PartitionSpec as P

D = 1024
HEAD = 64
LEN = 1024
epsilon = 1e-05
masked_score = -1e30
bf16 = jnp.bfloat16
f32 = jnp.float32


def size(axis):
    return lax.axis_size(axis)


def place(axis):
    return lax.axis_index(axis)


def pair(values, axis):
    return lax.ppermute(values, axis, [(0, 1), (1, 0)])


def after(values, *others):
    return lax.optimization_barrier((values,) + others)[0]


def together(*arrays):
    return lax.optimization_barrier(arrays)


def shift(values, step):
    count = size("col")
    return lax.ppermute(values, "col", [(i, (i + step) % count) for i in range(count)])


def across(values, bits):
    return lax.ppermute(values, "col", [(i, i ^ bits) for i in range(size("col"))])


def by_place(bit, own, other, axis):
    return jnp.where(
        bit == 0,
        jnp.concatenate((own, other), axis),
        jnp.concatenate((other, own), axis),
    )


def nt(left, right, kind=f32):
    return lax.dot_general(
        left, right, (((1,), (1,)), ((), ())), preferred_element_type=f32
    ).astype(kind)


def nn(left, right, kind=f32):
    return lax.dot_general(
        left, right, (((1,), (0,)), ((), ())), preferred_element_type=f32
    ).astype(kind)


def tn(left, right, kind=f32):
    return lax.dot_general(
        left, right, (((0,), (0,)), ((), ())), preferred_element_type=f32
    ).astype(kind)


def swap_sequences(values):
    count = size("col")
    perm = []
    for core in range(2):
        for col in range(count):
            half, other = col % 2, col - col % 2
            target = (half, other + core)
            perm.append((core * count + col, target[0] * count + target[1]))
    return lax.ppermute(values, ("core", "col"), perm)


def own_first(values):
    if size("row") != 2:
        return values
    half = values.shape[0] // 2
    return jnp.where(place("row") == 0, values, jnp.roll(values, half, axis=0))


def own_part(values):
    share = values.shape[0] // size("row")
    if size("row") == 2:
        return values[:share]
    return lax.dynamic_slice_in_dim(values, place("row") * share, share)


def gather_features(values):
    if size("row") == 2:
        full = by_place(place("row"), values, pair(values, "row"), 1)
        return own_first(full)
    return lax.all_gather(values, "row", axis=1, tiled=True)


def gather_tokens(values):
    if size("row") == 2:
        return jnp.concatenate((values, pair(values, "row")), 0)
    return lax.all_gather(values, "row", axis=0, tiled=True)


def sum_tokens(partial):
    if size("row") == 2:
        share = partial.shape[0] // 2
        return partial[:share] + pair(partial[share:].astype(bf16), "row").astype(f32)
    return lax.psum_scatter(partial, "row", scatter_dimension=0, tiled=True)


def to_own_tokens(values):
    if size("row") == 2:
        bit = place("row")
        ordered = own_first(values)
        share = values.shape[0] // 2
        return by_place(bit, ordered[:share], pair(ordered[share:], "row"), 1)
    return lax.all_to_all(values, "row", 0, 1, tiled=True)


def to_own_features(values):
    if size("row") == 2:
        bit = place("row")
        half = values.shape[1] // 2
        low, high = values[:, :half], values[:, half:]
        own = jnp.where(bit == 0, low, high)
        other = pair(jnp.where(bit == 0, high, low), "row")
        return by_place(bit, own, other, 0)
    return lax.all_to_all(values, "row", 1, 0, tiled=True)


def sum_features(partial, addend):
    if size("row") == 2:
        half = partial.shape[1] // 2
        low, high = partial[:, :half], partial[:, half:]
        bit = place("row")
        got = pair(jnp.where(bit == 0, high, low).astype(bf16), "row").astype(f32)
        got = jnp.roll(got, partial.shape[0] // 2, axis=0)
        return own_first(jnp.where(bit == 0, low, high) + got) + addend
    return lax.psum_scatter(partial, "row", scatter_dimension=1, tiled=True) + addend


class Held:
    def __init__(self, **arrays):
        vars(self).update(arrays)

    update = __init__


def step_of(held):
    return Held(**lax.optimization_barrier(vars(held)))


def halves(values):
    middle = values.shape[0] // 2
    return values[:middle], values[middle:]


def three_groups(triple, merge, expand, shrink):
    depth = triple.shape[0]
    heads = triple.transpose(1, 2, 0).reshape(3, 2, 2, 1, HEAD, depth)
    out = merge.reshape(1, 2, 2, 1, HEAD, depth)
    keys_values = jnp.concatenate((heads[1], heads[2]), 3 - 1)
    queries_merge = jnp.concatenate((heads[0], out[0]), 3 - 1)
    attend = jnp.stack((keys_values, queries_merge), 2).reshape(2, 2, 2, 2 * HEAD, depth)
    widen = expand.T.reshape(2, 2, 2, -1, depth)
    narrow = shrink.reshape(2, 2, 2, -1, depth)
    return attend, widen, narrow


def my_quarter(group):
    some = lax.dynamic_index_in_dim(group, place("outer"), 1, keepdims=False)
    return lax.dynamic_index_in_dim(some, place("core"), 1, keepdims=False)


def exchange_rows(quarter):
    bit = place("row")
    mine = jnp.where(bit == 0, quarter[0], quarter[1])
    other = pair(jnp.where(bit == 0, quarter[1], quarter[0]), "row")
    return by_place(bit, mine, other, 1)


STEPS = (1, 3, 2)
BACK = (2, 1, 3)


def own_core_half(parts, pairs):
    count = size("col")
    return jnp.stack(
        [jnp.stack([group[step] for step in range(count)]) for group in (parts, pairs)]
    )


def gather_attend(quarter):
    parts = {0: quarter}
    for step in STEPS:
        parts[step] = shift(quarter, step)
    pairs = {step: pair(parts[step], "outer") for step in (0,) + STEPS}
    return own_core_half(parts, pairs), parts[2], pairs[2]


def collect_row(last):
    bit = place("row")
    half = last.shape[1] // 2
    low, high = last[:, :half].astype(bf16), last[:, half:].astype(bf16)
    mine = jnp.where(bit == 0, low, high)
    got = pair(jnp.where(bit == 0, high, low), "row")
    return jnp.stack((jnp.where(bit == 0, mine, got), jnp.where(bit == 0, got, mine)))


def ungroup(attend):
    depth = attend.shape[-1]
    heads = attend.reshape(4, 2, 2, HEAD, depth)
    keys, values = heads[:, 0, 0], heads[:, 0, 1]
    queries, merge = heads[:, 1, 0], heads[:, 1, 1]
    triple = jnp.stack((queries, keys, values)).reshape(3, 4 * HEAD, depth).transpose(2, 0, 1)
    return triple, merge.reshape(4 * HEAD, depth)


def flip(values, axis, bit):
    return jnp.where(bit == 0, values, jnp.flip(values, axis))


def dot(left, right, left_dim, right_dim):
    return lax.dot_general(
        left, right, (((left_dim,), (right_dim,)), ((), ())), preferred_element_type=f32
    )


def params():
    return pltpu.CompilerParams(vmem_limit_bytes=36 << 20)


def anywhere(arrays):
    return [pl.BlockSpec(memory_space=pl.ANY) for _ in arrays]


def pick(near_ref, far_ref, begin):
    part = slice(begin, begin + HEAD)
    return jnp.concatenate((near_ref[:, part], far_ref[:, part]), 0)


def attend_forward_kernel(q_ref, near_ref, far_ref, qs_ref, ks_ref, out_ref, lse_ref):
    same = ks_ref[...] == qs_ref[...]
    for head in range(2):
        part = slice(head * HEAD, (head + 1) * HEAD)
        keys = pick(near_ref, far_ref, 2 * head * HEAD)
        values = pick(near_ref, far_ref, (2 * head + 1) * HEAD)
        queries = q_ref[:, part] * jnp.asarray(HEAD**-0.5, bf16)
        scores = jnp.where(same, dot(keys, queries, 1, 1), masked_score)
        top = jnp.max(scores, axis=0, keepdims=True)
        weights = jnp.exp(scores - top)
        total = jnp.sum(weights, axis=0, keepdims=True)
        low = (weights * (1.0 / total)).astype(bf16)
        out_ref[part] = dot(values, low, 0, 0).astype(bf16)
        lse_ref[0, head : head + 1] = top + jnp.log(total)


def attend_forward(queries, near, far, query_segment, key_segment):
    tokens, width = queries.shape
    steps = width // (2 * HEAD)
    block = pl.BlockSpec((tokens, 4 * HEAD), lambda i: (0, i))
    return pl.pallas_call(
        attend_forward_kernel,
        grid=(steps,),
        in_specs=[
            pl.BlockSpec((tokens, 2 * HEAD), lambda i: (0, i)),
            block,
            block,
            pl.BlockSpec((1, tokens), lambda i: (0, 0)),
            pl.BlockSpec((2 * tokens, 1), lambda i: (0, 0)),
        ],
        out_specs=[
            pl.BlockSpec((2 * HEAD, tokens), lambda i: (i, 0)),
            pl.BlockSpec((1, 2, tokens), lambda i: (i, 0, 0)),
        ],
        out_shape=[
            jax.ShapeDtypeStruct((width, tokens), bf16),
            jax.ShapeDtypeStruct((steps, 2, tokens), f32),
        ],
        compiler_params=params(),
        cost_estimate=pl.CostEstimate(
            flops=32 * tokens * tokens * width,
            bytes_accessed=4 << 20,
            transcendentals=2 * tokens * tokens * width // HEAD,
        ),
    )(queries, near, far, query_segment, key_segment)


def attend_backward_kernel(
    q_ref, kv_ref, far_kv_ref, g_ref, qs_ref, ks_ref, lse_ref, dq_ref, near_ref, far_ref
):
    same = ks_ref[...] == qs_ref[...]
    scale = HEAD**-0.5
    near = near_ref.shape[0]
    for head in range(2):
        part = slice(head * HEAD, (head + 1) * HEAD)
        key_part = slice(2 * head * HEAD, (2 * head + 1) * HEAD)
        value_part = slice((2 * head + 1) * HEAD, (2 * head + 2) * HEAD)
        keys = pick(kv_ref, far_kv_ref, key_part.start)
        values = pick(kv_ref, far_kv_ref, value_part.start)
        queries = q_ref[:, part] * jnp.asarray(scale, bf16)
        grad = g_ref[:, part]
        scores = jnp.where(same, dot(keys, queries, 1, 1), masked_score)
        weights = jnp.exp(scores - lse_ref[0, head : head + 1])
        grad_weights = dot(values, grad, 1, 1)
        inner = jnp.sum(weights * grad_weights, axis=0, keepdims=True)
        grad_scores = (weights * (grad_weights - inner)).astype(bf16)
        dq_ref[part] = (dot(keys, grad_scores, 0, 0) * scale).astype(bf16)
        grad_keys = dot(grad_scores, queries, 1, 0)
        grad_values = dot(weights.astype(bf16), grad, 1, 0)
        near_ref[:, key_part], far_ref[:, key_part] = grad_keys[:near], grad_keys[near:]
        near_ref[:, value_part], far_ref[:, value_part] = grad_values[:near], grad_values[near:]


def attend_backward(queries, near, far, grad, query_segment, key_segment, lse, begin, steps):
    tokens = queries.shape[0]
    block = pl.BlockSpec((tokens, 4 * HEAD), lambda i: (0, begin + i))
    query_block = pl.BlockSpec((tokens, 2 * HEAD), lambda i: (0, begin + i))
    key_block = pl.BlockSpec((tokens, 4 * HEAD), lambda i: (0, i))
    return pl.pallas_call(
        attend_backward_kernel,
        grid=(steps,),
        in_specs=[
            query_block,
            block,
            block,
            query_block,
            pl.BlockSpec((1, tokens), lambda i: (0, 0)),
            pl.BlockSpec((2 * tokens, 1), lambda i: (0, 0)),
            pl.BlockSpec((1, 2, tokens), lambda i: (begin + i, 0, 0)),
        ],
        out_specs=[pl.BlockSpec((2 * HEAD, tokens), lambda i: (i, 0)), key_block, key_block],
        out_shape=[
            jax.ShapeDtypeStruct((2 * HEAD * steps, tokens), bf16),
            jax.ShapeDtypeStruct((tokens, 4 * HEAD * steps), f32),
            jax.ShapeDtypeStruct((tokens, 4 * HEAD * steps), f32),
        ],
        compiler_params=params(),
        cost_estimate=pl.CostEstimate(
            flops=160 * tokens * tokens * steps * HEAD,
            bytes_accessed=8 << 20,
            transcendentals=4 * tokens * tokens * steps,
        ),
    )(queries, near, far, grad, query_segment, key_segment, lse)


def attend_weights_kernel(
    which_ref, dkv_ref, dq_ref, out_in_ref, x_ref, g_ref, *rest, added, cols
):
    add_ref = rest[0] if added else None
    out_refs = rest[-cols:]

    def put(rows, value):
        value = value.reshape(cols, -1, D)
        for step, out_ref in enumerate(out_refs):
            term = value[step]
            if added:
                term = term + add_ref[0, step, rows].astype(f32)
            out_ref[rows] = term.astype(out_ref.dtype)

    @pl.when(which_ref[0] == 0)
    def _():
        put(slice(0, 2 * HEAD), dot(dkv_ref[...], x_ref[...], 0, 0))

    @pl.when(which_ref[0] == 1)
    def _():
        put(slice(0, HEAD), dot(dq_ref[...], x_ref[...], 1, 0))
        put(slice(HEAD, 2 * HEAD), dot(out_in_ref[...], g_ref[...], 1, 0))


def attend_weights(which, dkv, dq, out_in, x, g, begin, cols, kind, add=None, earlier=()):
    tokens = x.shape[0]
    full = pl.BlockSpec((tokens, D), lambda i, w: (0, 0))
    rows = pl.BlockSpec((cols * HEAD, tokens), lambda i, w: (begin, 0))
    specs = [pl.BlockSpec((tokens, cols * 2 * HEAD), lambda i, w: (0, begin)), rows, rows, full, full]
    given = [dkv, dq, out_in, x, g]
    if add is not None:
        specs.append(pl.BlockSpec((1, cols, 2 * HEAD, D), lambda i, w: (begin, 0, 0, 0)))
        given.append(add)
    return pl.pallas_call(
        functools.partial(attend_weights_kernel, added=add is not None, cols=cols),
        grid_spec=pltpu.PrefetchScalarGridSpec(
            num_scalar_prefetch=1,
            grid=(1,),
            in_specs=specs + anywhere(earlier),
            out_specs=[pl.BlockSpec((2 * HEAD, D), lambda i, w: (0, 0))] * cols,
        ),
        out_shape=[jax.ShapeDtypeStruct((2 * HEAD, D), kind)] * cols,
        compiler_params=params(),
        cost_estimate=pl.CostEstimate(
            flops=4 * tokens * D * cols * HEAD, bytes_accessed=6 << 20, transcendentals=0
        ),
    )(which, *given, *earlier)


def attend_far_kernel(which_ref, dkv_ref, dq_ref, out_in_ref, x_ref, g_ref, *rest):
    out_ref = rest[-1]
    cols = out_ref.shape[1]

    @pl.when(which_ref[0] == 0)
    def _():
        value = dot(dkv_ref[...], x_ref[...], 0, 0)
        out_ref[0] = value.reshape(cols, 2 * HEAD, D).astype(out_ref.dtype)

    @pl.when(which_ref[0] == 1)
    def _():
        for part, value in enumerate(
            (dot(dq_ref[...], x_ref[...], 1, 0), dot(out_in_ref[...], g_ref[...], 1, 0))
        ):
            rows = slice(part * HEAD, (part + 1) * HEAD)
            out_ref[0, :, rows] = value.reshape(cols, HEAD, D).astype(out_ref.dtype)


def attend_far_weights(which, dkv, dq, out_in, x, g, cols, *earlier):
    tokens = x.shape[0]
    full = pl.BlockSpec((tokens, D), lambda i, w: (0, 0))
    rows = pl.BlockSpec((cols * HEAD, tokens), lambda i, w: (i, 0))
    return pl.pallas_call(
        attend_far_kernel,
        grid_spec=pltpu.PrefetchScalarGridSpec(
            num_scalar_prefetch=1,
            grid=(2,),
            in_specs=[
                pl.BlockSpec((tokens, cols * 2 * HEAD), lambda i, w: (0, i)), rows, rows, full, full
            ]
            + anywhere(earlier),
            out_specs=pl.BlockSpec((1, cols, 2 * HEAD, D), lambda i, w: (i, 0, 0, 0)),
        ),
        out_shape=jax.ShapeDtypeStruct((2, cols, 2 * HEAD, D), bf16),
        compiler_params=params(),
        cost_estimate=pl.CostEstimate(
            flops=8 * tokens * D * cols * HEAD, bytes_accessed=6 << 20, transcendentals=0
        ),
    )(which, dkv, dq, out_in, x, g, *earlier)


SPARE = 8


def units_of(weights):
    units = (weights.shape[2] - SPARE) // 2
    expand = weights[:, :, :units].reshape(-1, D)
    shrink = weights[:, :, units : 2 * units].reshape(-1, D)
    return expand, shrink


def finish(total, keep_ref, send_ref):
    @pl.when(pl.program_id(0) == pl.num_programs(0) - 1)
    def _():
        half = total.shape[0] // 2
        keep_ref[...] = total[:half]
        send_ref[...] = total[half:].astype(bf16)


def add_to(total, term):
    @pl.when(pl.program_id(0) == 0)
    def _():
        total[...] = term

    @pl.when(pl.program_id(0) > 0)
    def _():
        total[...] += term


def hidden_forward_kernel(
    x_ref, bias_ref, weights_ref, hidden_ref, slope_ref, keep_ref, send_ref, total
):
    expand, shrink = units_of(weights_ref[0, 0:1])
    u = dot(x_ref[...], expand, 1, 1) + bias_ref[0]
    normal = 0.5 * (1.0 + lax.erf(u * (0.5**0.5)))
    slope_ref[...] = normal + u * (jnp.exp(-0.5 * u * u) * ((0.5 / jnp.pi) ** 0.5))
    hidden = (u * normal).astype(bf16)
    hidden_ref[...] = hidden
    add_to(total, dot(hidden, shrink, 1, 0))
    finish(total, keep_ref, send_ref)


def hidden_specs(tokens, weights):
    outer, core, cols, rows, _ = weights.shape
    units = (rows - SPARE) // 2
    steps, width = outer * core, cols * units
    block = pl.BlockSpec((1, 1, cols, rows, D), lambda i: (i // core, i % core, 0, 0, 0))
    wide = pl.BlockSpec((tokens, width), lambda i: (0, i))
    half = pl.BlockSpec((tokens // 2, D), lambda i: (0, 0))
    half_shapes = [
        jax.ShapeDtypeStruct((tokens // 2, D), f32),
        jax.ShapeDtypeStruct((tokens // 2, D), bf16),
    ]
    full = pl.BlockSpec((tokens, D), lambda i: (0, 0))
    row = pl.BlockSpec((1, 1, width), lambda i: (i, 0, 0))
    cost = pl.CostEstimate(
        flops=4 * tokens * D * steps * width, bytes_accessed=20 << 20, transcendentals=0
    )
    return steps, width, block, wide, half, half_shapes, full, row, cost


def hidden_forward(x, weights, bias):
    tokens = x.shape[0]
    steps, width, block, wide, half, half_shapes, full, row, cost = hidden_specs(tokens, weights)
    shape = (tokens, steps * width)
    return pl.pallas_call(
        hidden_forward_kernel,
        grid=(steps,),
        in_specs=[full, row, block],
        out_specs=[wide, wide, half, half],
        out_shape=[jax.ShapeDtypeStruct(shape, bf16), jax.ShapeDtypeStruct(shape, f32)]
        + half_shapes,
        scratch_shapes=[pltpu.VMEM((tokens, D), f32)],
        compiler_params=params(),
        cost_estimate=cost,
    )(x, bias, weights)


def hidden_backward_kernel(
    g_ref, slope_ref, weights_ref, grad_ref, sum_ref, keep_ref, send_ref, total
):
    expand, shrink = units_of(weights_ref[0, 0:1])
    grad = (dot(g_ref[...], shrink, 1, 1) * slope_ref[...]).astype(bf16)
    grad_ref[...] = grad
    sum_ref[0] = jnp.sum(grad.astype(f32), axis=0, keepdims=True)
    add_to(total, dot(grad, expand, 1, 0))
    finish(total, keep_ref, send_ref)


def hidden_backward(g, weights, slope):
    tokens = g.shape[0]
    steps, width, block, wide, half, half_shapes, full, row, cost = hidden_specs(tokens, weights)
    return pl.pallas_call(
        hidden_backward_kernel,
        grid=(steps,),
        in_specs=[full, wide, block],
        out_specs=[wide, row, half, half],
        out_shape=[
            jax.ShapeDtypeStruct((tokens, steps * width), bf16),
            jax.ShapeDtypeStruct((steps, 1, width), f32),
        ]
        + half_shapes,
        scratch_shapes=[pltpu.VMEM((tokens, D), f32)],
        compiler_params=params(),
        cost_estimate=cost,
    )(g, slope, weights)


def hidden_weights_kernel(grad_ref, hidden_ref, x_ref, g_ref, sum_ref, out_ref):
    cols, rows, _ = out_ref.shape[2:]
    units = (rows - SPARE) // 2
    for part, (left, right) in enumerate(((grad_ref, x_ref), (hidden_ref, g_ref))):
        value = dot(left[...], right[...], 0, 0).reshape(cols, units, D)
        out_ref[0, 0, :, part * units : (part + 1) * units] = value.astype(bf16)
    first = lax.broadcasted_iota(jnp.int32, (cols, SPARE, units), 1) == 0
    sums = jnp.where(first, sum_ref[0][:, None, :], 0.0).astype(bf16)
    out_ref[0, 0, :, 2 * units :] = jnp.zeros((cols, SPARE, D), bf16)
    for begin in (0, D // 2):
        out_ref[0, 0, :, 2 * units :, begin : begin + units] = sums


def hidden_weights(grad, hidden, x, g, sums, shape):
    tokens = x.shape[0]
    outer, core, cols, rows, _ = shape
    width = grad.shape[1] // (outer * core)
    wide = pl.BlockSpec((tokens, width), lambda i: (0, i))
    full = pl.BlockSpec((tokens, D), lambda i: (0, 0))
    return pl.pallas_call(
        hidden_weights_kernel,
        grid=(outer * core,),
        in_specs=[
            wide, wide, full, full, pl.BlockSpec((1, cols, width // cols), lambda i: (i, 0, 0))
        ],
        out_specs=pl.BlockSpec(
            (1, 1, cols, rows, D), lambda i: (i // core, i % core, 0, 0, 0)
        ),
        out_shape=jax.ShapeDtypeStruct(shape, bf16),
        compiler_params=params(),
        cost_estimate=pl.CostEstimate(
            flops=4 * tokens * D * grad.shape[1], bytes_accessed=16 << 20, transcendentals=0
        ),
    )(grad, hidden, x, g, sums)


def hidden_gradients_kernel(core_ref, own_ref, got_ref, expand_ref, shrink_ref, bias_ref):
    units = shrink_ref.shape[0]

    def put(ref):
        expand_ref[...] = ref[0, 0, :units].astype(f32).T
        shrink_ref[...] = ref[0, 0, units : 2 * units].astype(f32)
        bias_ref[0] = ref[0, 0, 2 * units :, :units].astype(f32)

    mine = pl.program_id(0) % 2 == core_ref[0]
    pl.when(mine)(lambda: put(own_ref))
    pl.when(jnp.logical_not(mine))(lambda: put(got_ref))


def hidden_gradients(core, own, got):
    rows, depth = own.shape[2:]
    units = (rows - SPARE) // 2
    piece = pl.BlockSpec((1, 1, rows, depth), lambda i, w: (i // 4, i // 2 % 2, 0, 0))
    expand, shrink, bias = pl.pallas_call(
        hidden_gradients_kernel,
        grid_spec=pltpu.PrefetchScalarGridSpec(
            num_scalar_prefetch=1,
            grid=(8,),
            in_specs=[piece, piece],
            out_specs=[
                pl.BlockSpec((depth, units), lambda i, w: (0, i)),
                pl.BlockSpec((units, depth), lambda i, w: (i, 0)),
                pl.BlockSpec((1, SPARE, units), lambda i, w: (i, 0, 0)),
            ],
        ),
        out_shape=[
            jax.ShapeDtypeStruct((depth, 8 * units), f32),
            jax.ShapeDtypeStruct((8 * units, depth), f32),
            jax.ShapeDtypeStruct((8, SPARE, units), f32),
        ],
        compiler_params=params(),
        cost_estimate=pl.CostEstimate(flops=1 << 20, bytes_accessed=6 << 20, transcendentals=0),
    )(core, own, got)
    return expand, shrink, bias[:, 0].reshape(-1)


def layer(
    tokens, segments, triple_weight, pair_bias, merge_weight, merge_bias, first_gain, first_shift,
    expand_weight, expand_bias, shrink_weight, shrink_bias, second_gain, second_shift, cotangent,
):
    cols = size("col")
    count = tokens.shape[0]
    own = count // 2
    heads = D // HEAD // 2
    row, col, core, outer = place("row"), place("col"), place("core"), place("outer")
    row_size, pair_size, hidden_size = merge_bias.shape[0], pair_bias.shape[1], expand_bias.shape[0]

    groups = three_groups(triple_weight, merge_weight, expand_weight, shrink_weight)
    attend_group = my_quarter(groups[0])
    row_vectors = jnp.stack(
        (merge_bias, first_gain, first_shift, shrink_bias, second_gain, second_shift)
    )
    column = jnp.concatenate(
        [
            lax.dynamic_slice_in_dim(vector, row * (vector.shape[0] // 2), vector.shape[0] // 2)
            for vector in (pair_bias[0], pair_bias[1], expand_bias)
        ]
    )
    moved = swap_sequences(tokens)
    quarter = exchange_rows(attend_group)
    pair_column, hidden_column = column[:pair_size], column[pair_size:].reshape(4, -1)
    pair_column = pair_column.reshape(2, 2, HEAD)
    pair_column = lax.dynamic_index_in_dim(pair_column, outer, 1, keepdims=False)
    pair_column = lax.dynamic_index_in_dim(pair_column, 1 - core, 0)
    hidden_column = lax.dynamic_index_in_dim(hidden_column, 2 * outer + core, 0)
    other_group = exchange_rows(
        jnp.concatenate([my_quarter(group) for group in groups[1:]], 1)
    )
    v = step_of(
        Held(
            quarter=quarter, moved=moved, other=segments.astype(f32), group=other_group, rows=row_vectors, pairs=pair_column,
            hidden=hidden_column, cot=cotangent,
        )
    )

    def beside(rows, value):
        spare = jnp.pad(value, ((0, SPARE - 1), (0, D - value.shape[1])))
        return jnp.concatenate((rows, spare), 0)

    quarter, moved = beside(v.quarter, v.pairs), v.moved
    parts = {0: quarter, 1: shift(quarter, 1), 3: shift(quarter, 3)}
    pairs = {0: pair(quarter, "outer")}
    got_tokens = pair(moved, "row")
    v.update(quarter=quarter, parts=parts, pairs=pairs, moved=moved, got=got_tokens)
    v = step_of(v)
    parts, pairs, quarter = v.parts, v.pairs, v.quarter
    parts[2] = shift(quarter, 2)
    pairs[1], pairs[3] = pair(parts[1], "outer"), pair(parts[3], "outer")
    mine = beside(v.group, v.hidden)
    hidden_all = lax.all_gather(mine, ("outer", "core", "col"), axis=0)
    hidden_all = hidden_all.reshape(2, 2, cols, -1, D)
    v.vectors = by_place(row, v.rows, pair(v.rows, "row"), 1)
    v.other = pair(v.other, "core")
    v = step_of(v)
    parts, pairs = v.parts, v.pairs
    pairs[2] = pair(parts[2], "outer")
    v.inputs = own_first(by_place(row, v.moved, v.got, 1))
    v = step_of(v)
    parts, pairs = v.parts, v.pairs
    rows = 2 * HEAD

    def without(group):
        return {step: group[step][:rows] for step in range(cols)}

    attend_own = own_core_half(without(parts), without(pairs))
    v.attend_own, v.attend_other = attend_own, pair(attend_own, "core")
    bias_own = jnp.stack(
        [group[step][rows, :HEAD] for group in (parts, pairs) for step in range(cols)]
    ).astype(f32)
    v.bias_own, v.bias_other = bias_own, pair(bias_own, "core")
    other = v.other.astype(jnp.int32)
    sequence = lax.dynamic_slice_in_dim(
        jnp.where(col % 2 == core, segments, other), (col // 2) * LEN, LEN
    ).reshape(2, count)
    query_segment = own_first(lax.dynamic_index_in_dim(sequence, core, 0, keepdims=False))
    far_segment = own_first(lax.dynamic_index_in_dim(sequence, 1 - core, 0, keepdims=False))
    key_segment = jnp.concatenate((query_segment, far_segment))
    segment_row, segment_column = query_segment[None], key_segment[:, None]
    vectors = v.vectors.astype(f32)
    v = step_of(
        Held(
            own=v.attend_own, other=v.attend_other, cot=v.cot, inputs=v.inputs,
            vectors=vectors, biases=(v.bias_own, v.bias_other),
        )
    )
    attend_own, attend_other, inputs, vectors = v.own, v.other, v.inputs, v.vectors
    first = jnp.where(core == 0, attend_own, attend_other)
    second = jnp.where(core == 0, attend_other, attend_own)
    bias_values = jnp.where(core == 0, v.biases[0], v.biases[1])
    bias_keys_values = jnp.stack((jnp.zeros_like(bias_values), bias_values), 1).reshape(-1)
    bias_queries = jnp.where(core == 0, v.biases[1], v.biases[0]).reshape(-1)
    weight_keys_values = first.reshape(-1, D)
    second = second.reshape(heads, 2, HEAD, D)
    weight_queries, weight_merge = second[:, 0].reshape(-1, D), second[:, 1].reshape(-1, D)

    cut = heads * HEAD // 2
    steps = heads // 4
    keys_values = (nt(inputs, weight_keys_values) + bias_keys_values).astype(bf16)
    v.far = pair(keys_values, "core")
    v.queries = (nt(inputs, weight_queries) + bias_queries).astype(bf16)
    v.keys_values = keys_values
    v.weights = (weight_keys_values, weight_queries, weight_merge)
    v = step_of(v)
    queries = v.queries
    keys_values, far_keys_values = v.keys_values, v.far
    v.attended, v.lse = attend_forward(
        queries, keys_values, far_keys_values, segment_row, segment_column
    )
    v = step_of(v)
    attended, lse = v.attended, v.lse
    queries, keys_values, far_keys_values = v.queries, v.keys_values, v.far
    weight_keys_values, weight_queries, weight_merge = v.weights
    branch = sum_tokens(tn(attended, weight_merge))
    residual = inputs[:own].astype(f32) + (branch + vectors[0])
    scaled_one, inverse_one, normed_one = norm_forward(residual, vectors[1], vectors[2])
    normed_low = gather_tokens(normed_one.astype(bf16))
    cotangent = swap_sequences(v.cot)
    normed_low, normed_one, hidden_all, cotangent = lax.optimization_barrier(
        (normed_low, normed_one, hidden_all, cotangent)
    )
    units = hidden_size // 8
    bias_hidden = hidden_all[:, :, :, 2 * units, :units].reshape(4, 1, -1).astype(f32)
    hidden, slope, keep, send = hidden_forward(normed_low, hidden_all, bias_hidden)
    upstream = to_own_tokens(cotangent)
    keep, send, upstream = lax.optimization_barrier((keep, send, upstream))
    shrunk = keep + pair(send, "row").astype(f32)
    scaled_two, inverse_two, final = norm_forward(
        normed_one + (shrunk + vectors[3]), vectors[4], vectors[5]
    )
    live = (query_segment[:own] != 0).astype(f32)[:, None]
    upstream = upstream.astype(f32) * live
    grad_sum_two, grad_gain_two, grad_shift_two = norm_backward(
        upstream, scaled_two, inverse_two, vectors[4]
    )
    grad_shrunk_own = grad_sum_two.astype(bf16)
    grad_shrunk = gather_tokens(grad_shrunk_own)
    grad_shrunk, out = lax.optimization_barrier((grad_shrunk, final.astype(bf16)))
    grad_pre, sum_hidden, keep, send = hidden_backward(grad_shrunk, hidden_all, slope)
    out = to_own_features(out)
    cut = heads * HEAD // 2
    steps = heads // 4
    spare = sum_hidden.reshape(4, cols, units)
    v = Held(
        grad_pre=grad_pre, hidden=hidden, normed=normed_low, g=grad_shrunk, inputs=inputs,
        attended=attended, queries=queries, keys_values=keys_values, lse=lse,
        far_keys_values=far_keys_values, keep=keep, send=send, sum_two=grad_sum_two,
        scaled_one=scaled_one, inverse_one=inverse_one, out=out, shrunk_own=grad_shrunk_own,
        sum_two_rows=(grad_gain_two, grad_shift_two), spare=spare, vectors=vectors,
        weight_merge=weight_merge, weight_queries=weight_queries,
        weight_keys_values=weight_keys_values,
    )

    v = step_of(v)
    v.got = pair(v.send, "row")
    hidden_grads = hidden_weights(
        v.grad_pre, v.hidden, v.normed, v.g, v.spare, hidden_all.shape
    )
    hidden_sums = lax.psum_scatter(
        hidden_grads.reshape(-1, D), ("outer", "core", "col"), scatter_dimension=0, tiled=True
    )
    v = step_of(v)
    grad_normed = v.sum_two + (v.keep + v.got.astype(f32))
    res, grad_gain_one, grad_shift_one = norm_backward(
        grad_normed, v.scaled_one, v.inverse_one, v.vectors[1]
    )
    branch_own = res.astype(bf16)
    branch_got = pair(branch_own, "row")
    sum_rows = jnp.stack(
        (
            jnp.sum(branch_own, axis=0, dtype=f32),
            grad_gain_one,
            grad_shift_one,
            jnp.sum(v.shrunk_own, axis=0, dtype=f32),
            *v.sum_two_rows,
        )
    )
    v = Held(
        inputs=v.inputs, attended=v.attended, queries=v.queries, out=v.out,
        keys_values=v.keys_values, far_keys_values=v.far_keys_values, lse=v.lse,
        weight_merge=v.weight_merge, weight_queries=v.weight_queries,
        weight_keys_values=v.weight_keys_values,
    )
    v.branch = jnp.concatenate((branch_own, branch_got), 0)
    v.grad_attended = nt(v.branch, v.weight_merge, bf16)
    v.sum_rows = sum_rows
    middle = D // 2
    v.res_mine = jnp.where(row == 0, res[:, :middle], res[:, middle:])
    v.res_send = halves(jnp.where(row == 0, res[:, middle:], res[:, :middle]))
    v = step_of(v)
    shared = (
        v.queries, v.keys_values, v.far_keys_values, v.grad_attended, segment_row,
        segment_column, v.lse,
    )
    v.second = attend_backward(*shared, steps, steps)
    v.res_got = [pair(v.res_send[0], "row")]
    v = step_of(v)
    shared = (
        v.queries, v.keys_values, v.far_keys_values, v.grad_attended, segment_row,
        segment_column, v.lse,
    )
    v.far = pair(v.second[2], "core")
    v.first = attend_backward(*shared, 0, steps)
    v.res_got.append(pair(v.res_send[1], "row"))
    v = step_of(v)
    far = pair(v.first[2], "core")
    dkv_second = (v.second[1] + v.far).astype(bf16)
    v.grad_queries = jnp.concatenate((v.first[0], v.second[0]), 0)
    v.entry = tn(v.grad_queries, v.weight_queries)
    dkv_first = (v.first[1] + far).astype(bf16)
    v.grad_keys_values = jnp.concatenate((dkv_first, dkv_second), 1)
    v = step_of(v)
    which = core.reshape(1)
    part = (v.grad_keys_values, v.grad_queries, v.attended, v.inputs, v.branch)
    v.far = attend_far_weights((1 - core).reshape(1), *part, cols)
    v = step_of(v)
    v.far = pair(v.far, "core")
    entry = v.entry + nn(v.grad_keys_values, v.weight_keys_values)
    v.res_columns = by_place(row, v.res_mine, jnp.concatenate(v.res_got, 0), 0)
    v.entry_keep = jnp.where(row == 0, entry[:, :middle], entry[:, middle:])
    v.entry_send = jnp.where(row == 0, entry[:, middle:], entry[:, :middle]).astype(bf16)
    v = step_of(v)
    part = (v.grad_keys_values, v.grad_queries, v.attended, v.inputs, v.branch)
    v.mates = attend_weights(which, *part, 1, cols, bf16, v.far)
    v = step_of(v)
    part = (v.grad_keys_values, v.grad_queries, v.attended, v.inputs, v.branch)
    v.got = {2: pair(v.mates[2], "outer")}
    v.entry_got = pair(v.entry_send, "row")
    v.own = attend_weights(which, *part, 0, cols, f32, v.far)
    sum_queries = jnp.sum(v.grad_queries, axis=1, dtype=f32)
    sum_values = jnp.sum(v.grad_keys_values, axis=0, dtype=f32).reshape(heads, 2, HEAD)[:, 1]
    sum_pair = jnp.stack((sum_queries, sum_values.reshape(-1))).reshape(2, 2, cols, HEAD)
    sum_pair = flip(sum_pair.transpose(2, 0, 1, 3), 2, outer).reshape(cols, -1)
    length = sum_pair.shape[1]
    sum_pair = jnp.concatenate(
        [
            lax.dynamic_index_in_dim(sum_pair, (col - place_of) % cols, 0, keepdims=False)
            for place_of in range(cols)
        ]
    )
    v.total = jnp.concatenate((sum_pair, v.sum_rows.reshape(-1)))
    v = step_of(v)

    def to_send(sums, got, step):
        return (sums[step] + got.astype(f32)).astype(bf16)

    got = v.got
    got[1], got[3] = pair(v.mates[1], "outer"), pair(v.mates[3], "outer")
    v.two = shift(to_send(v.own, got[2], 2), -2)
    total = v.total
    v.total = total + lax.ppermute(total, "col", [(i, i ^ 1) for i in range(cols)])
    entry = jnp.roll(v.entry_got.astype(f32), own, axis=0)
    v.grad_tokens = own_first(v.entry_keep + entry) + v.res_columns
    v = step_of(v)
    v.one = to_send(v.own, v.got[1], 1)
    v.three = to_send(v.own, v.got[3], 3)
    v = step_of(v)
    v.one, v.three = shift(v.one, -1), shift(v.three, -3)
    v.got[0] = pair(v.mates[0], "outer")
    total = v.total
    v.total = total + lax.ppermute(total, "col", [(i, i ^ 2) for i in range(cols)])
    v = step_of(v)
    attend_rest = v.own[0] + v.got[0].astype(f32)
    for term in (v.one, v.two, v.three):
        attend_rest = attend_rest + term.astype(f32)
    v = step_of(
        Held(
            rest=attend_rest, hidden=hidden_sums, total=v.total, out=v.out,
            grad_tokens=halves(v.grad_tokens),
        )
    )
    v.tokens_low = swap_sequences(v.grad_tokens[0])
    v.block = collect_row(v.hidden)
    v.total = v.total + pair(v.total, "core")
    v = step_of(v)
    v.block_got = pair(v.block, "outer")
    v.tokens_high = swap_sequences(v.grad_tokens[1])
    v.attend = collect_row(v.rest)
    v.total = v.total + pair(v.total, "outer")
    v = step_of(v)
    v.block = by_place(outer, v.block[:, None], v.block_got[:, None], 1)
    v.block_got = pair(v.block, "core")
    v = step_of(v)
    v.attend_got = pair(v.attend, "outer")
    v.out = swap_sequences(v.out)
    grad_expand, grad_shrink, grad_expand_bias = hidden_gradients(which, v.block, v.block_got)
    v = step_of(
        Held(
            expand=grad_expand, shrink=grad_shrink, bias=grad_expand_bias, attend=v.attend,
            attend_got=v.attend_got, total=v.total, out=v.out,
            grad_tokens=jnp.concatenate((v.tokens_low, v.tokens_high), 0),
        )
    )
    total = v.total
    layer_out, grad_tokens = v.out, v.grad_tokens
    grad_expand, grad_shrink, grad_expand_bias = v.expand, v.shrink, v.bias
    attend = by_place(outer, v.attend[:, None], v.attend_got[:, None], 1)
    attend_got = pair(attend, "core")
    attend = by_place(core, attend[:, :, None], attend_got[:, :, None], 2).astype(f32)
    grad_triple, grad_merge = ungroup(attend)
    mine = lax.dynamic_slice_in_dim(total, col * length, length)
    sum_rows = total[cols * length :].reshape(6, 2, row_size)
    low, high = sum_rows[:, 0].reshape(-1), sum_rows[:, 1].reshape(-1)
    got = pair(jnp.concatenate((mine, jnp.where(row == 0, high, low))), "row")
    totals = (jnp.where(row == 0, low, high) + got[length:]).reshape(6, row_size)
    got = got[:length]
    short = 2 * HEAD
    grad_pair = by_place(
        row, mine[: 2 * short].reshape(2, short), got[: 2 * short].reshape(2, short), 1
    )
    return (
        layer_out, grad_tokens, grad_triple, grad_pair, grad_merge, totals[0], totals[1], totals[2],
        grad_expand, grad_expand_bias, grad_shrink, totals[3], totals[4], totals[5],
    )


def masked(scores, query_segment, key_segment):
    same = query_segment[:, None] == key_segment[None, :]
    return jnp.where(same[None], scores, masked_score)


def attention_forward(queries, keys, values, query_segment, key_segment):
    scores = jnp.einsum("qhd,khd->hqk", queries, keys, preferred_element_type=f32)
    scores = masked(scores * HEAD**-0.5, query_segment, key_segment)
    top = jnp.max(scores, axis=-1, keepdims=True)
    weights = jnp.exp(scores - top)
    total = jnp.sum(weights, axis=-1, keepdims=True)
    low = (weights / total).astype(bf16)
    attended = jnp.einsum("hqk,khd->qhd", low, values, preferred_element_type=f32)
    return attended.astype(bf16), top + jnp.log(total)


def attention_backward(queries, keys, values, query_segment, key_segment, lse, grad):
    scores = jnp.einsum("qhd,khd->hqk", queries, keys, preferred_element_type=f32)
    scores = masked(scores * HEAD**-0.5, query_segment, key_segment)
    weights = jnp.exp(scores - lse)
    grad_weights = jnp.einsum("qhd,khd->hqk", grad, values, preferred_element_type=f32)
    inner = jnp.sum(weights * grad_weights, axis=-1, keepdims=True)
    grad_scores = (weights * (grad_weights - inner)).astype(bf16)
    scale = HEAD**-0.5
    grad_queries = jnp.einsum("hqk,khd->qhd", grad_scores, keys, preferred_element_type=f32) * scale
    grad_keys = jnp.einsum("hqk,qhd->khd", grad_scores, queries, preferred_element_type=f32) * scale
    grad_values = jnp.einsum(
        "hqk,qhd->khd", weights.astype(bf16), grad, preferred_element_type=f32
    )
    return grad_queries.astype(bf16), grad_keys, grad_values


def norm_forward(values, gain, shift):
    center = jnp.mean(values, axis=1, keepdims=True)
    inverse = lax.rsqrt(
        jnp.mean(values * values, axis=1, keepdims=True) - center * center + epsilon
    )
    scaled = (values - center) * inverse
    return scaled, inverse, scaled * gain + shift


def norm_backward(upstream, scaled, inverse, gain):
    through = upstream * gain
    grad = inverse * (
        through
        - jnp.mean(through, axis=1, keepdims=True)
        - scaled * jnp.mean(through * scaled, axis=1, keepdims=True)
    )
    return grad, jnp.sum(upstream * scaled, axis=0), jnp.sum(upstream, axis=0)


def exact_gelu(values):
    return jax.nn.gelu(values, approximate=False)


def layer_anywhere(
    tokens,
    segments,
    triple_weight,
    pair_bias,
    merge_weight,
    merge_bias,
    first_gain,
    first_shift,
    expand_weight,
    expand_bias,
    shrink_weight,
    shrink_bias,
    second_gain,
    second_shift,
    cotangent,
):
    rows, cols = size("row"), size("col")
    count = tokens.shape[0]
    own = count // rows
    heads = D // HEAD // rows
    row, col = place("row"), place("col")

    query_segment = lax.dynamic_slice_in_dim(segments, col * count, count)
    key_segment = query_segment

    row_size, pair_size, hidden_size = merge_bias.shape[0], pair_bias.shape[1], expand_bias.shape[0]
    row_vectors = jnp.stack(
        (merge_bias, first_gain, first_shift, shrink_bias, second_gain, second_shift)
    )
    vectors = lax.all_gather(row_vectors, "row", axis=1, tiled=True)

    def mine_of(full, axis=0):
        share = full.shape[axis] // rows
        return lax.dynamic_slice_in_dim(full, row * share, share, axis)

    bias_pair = mine_of(lax.all_gather(pair_bias, "col", axis=1, tiled=True), 1)
    bias_queries, bias_values = bias_pair[0], bias_pair[1]
    bias_hidden = mine_of(lax.all_gather(expand_bias, "col", axis=0, tiled=True)).astype(f32)
    vectors = vectors.astype(f32)

    triple = lax.all_gather(triple_weight, "col", axis=2, tiled=True)
    triple = lax.all_gather(triple, "row", axis=0, tiled=True).transpose(1, 2, 0)
    merge = lax.all_gather(merge_weight, "col", axis=0, tiled=True)
    merge = lax.all_gather(merge, "row", axis=1, tiled=True)
    expand = lax.all_gather(expand_weight, "col", axis=1, tiled=True)
    expand = lax.all_gather(expand, "row", axis=0, tiled=True).T
    shrink = lax.all_gather(shrink_weight, "col", axis=0, tiled=True)
    shrink = lax.all_gather(shrink, "row", axis=1, tiled=True)

    weight_queries, weight_keys, weight_values = (mine_of(triple[j]) for j in range(3))
    weight_merge, weight_expand, weight_shrink = mine_of(merge), mine_of(expand), mine_of(shrink)

    inputs = gather_features(tokens)
    head_shape = (-1, heads, HEAD)
    queries = (nt(inputs, weight_queries) + bias_queries.astype(f32)).astype(bf16)
    keys = nt(inputs, weight_keys).astype(bf16)
    values = (nt(inputs, weight_values) + bias_values.astype(f32)).astype(bf16)
    all_keys, all_values = keys, values
    queries_heads = queries.reshape(head_shape)
    keys_heads, values_heads = all_keys.reshape(head_shape), all_values.reshape(head_shape)
    attended, lse = attention_forward(
        queries_heads, keys_heads, values_heads, query_segment, key_segment
    )
    attended = attended.reshape(count, -1)
    branch = sum_tokens(nn(attended, weight_merge))
    residual = own_part(inputs).astype(f32) + (branch + vectors[0])
    scaled_one, inverse_one, normed_one = norm_forward(residual, vectors[1], vectors[2])
    normed_low = gather_tokens(normed_one.astype(bf16))
    pre_gelu = nt(normed_low, weight_expand) + bias_hidden
    hidden = exact_gelu(pre_gelu).astype(bf16)
    shrunk = sum_tokens(nn(hidden, weight_shrink))
    scaled_two, inverse_two, final = norm_forward(
        normed_one + (shrunk + vectors[3]), vectors[4], vectors[5]
    )

    live = (own_part(query_segment) != 0).astype(f32)[:, None]
    upstream = to_own_tokens(cotangent).astype(f32) * live
    grad_sum_two, grad_gain_two, grad_shift_two = norm_backward(
        upstream, scaled_two, inverse_two, vectors[4]
    )
    grad_shrunk_own = grad_sum_two.astype(bf16)
    grad_shrunk = gather_tokens(grad_shrunk_own)
    grad_hidden = nt(grad_shrunk, weight_shrink)
    grad_pre = jax.vjp(exact_gelu, pre_gelu)[1](grad_hidden)[0].astype(bf16)
    grad_normed = grad_sum_two + sum_tokens(nn(grad_pre, weight_expand))
    grad_res, grad_gain_one, grad_shift_one = norm_backward(
        grad_normed, scaled_one, inverse_one, vectors[1]
    )
    grad_branch_own = grad_res.astype(bf16)
    grad_branch = gather_tokens(grad_branch_own)
    grad_attended = nt(grad_branch, weight_merge).astype(bf16)
    late_out, late_res, grad_attended = lax.optimization_barrier(
        (final.astype(bf16), grad_res, grad_attended)
    )
    layer_out, grad_res_columns = to_own_features(late_out), to_own_features(late_res)
    grad_queries, grad_keys, grad_values = attention_backward(
        queries_heads,
        keys_heads,
        values_heads,
        query_segment,
        key_segment,
        lse,
        grad_attended.reshape(head_shape),
    )
    grad_queries = grad_queries.reshape(count, -1)
    grad_keys_values = jnp.concatenate(
        (grad_keys.reshape(-1, heads * HEAD), grad_values.reshape(-1, heads * HEAD)), 1
    )
    grad_keys_values = grad_keys_values.astype(bf16)
    grad_keys, grad_values = (
        grad_keys_values[:, : heads * HEAD],
        grad_keys_values[:, heads * HEAD :],
    )
    grad_entry = (
        nn(grad_queries, weight_queries)
        + nn(grad_keys, weight_keys)
        + nn(grad_values, weight_values)
    )
    grad_tokens = sum_features(grad_entry, grad_res_columns)

    def assemble(local, row_axis, col_axis):
        full = jnp.zeros((local.shape[0], local.shape[1] * rows, D), bf16)
        full = lax.dynamic_update_slice(
            full, local.astype(bf16), (0, row * local.shape[1], 0)
        )
        full = lax.psum_scatter(full, "row", scatter_dimension=2, tiled=True)
        full = lax.psum_scatter(full, "col", scatter_dimension=1, tiled=True)
        return lax.psum(full, ("outer", "core")).astype(f32)

    grad_triple = assemble(
        jnp.stack(
            (tn(grad_queries, inputs), tn(grad_keys, inputs), tn(grad_values, inputs))
        ),
        0,
        2,
    ).transpose(2, 0, 1)
    grad_merge = assemble(tn(attended, grad_branch)[None], 1, 0)[0]
    grad_expand = assemble(tn(grad_pre, normed_low)[None], 0, 1)[0].T
    grad_shrink = assemble(tn(hidden, grad_shrunk)[None], 1, 0)[0]

    def column_sums(values):
        return jnp.sum(values, axis=0, dtype=f32)

    sum_hidden = column_sums(grad_pre)
    sum_queries, sum_values = column_sums(grad_queries), column_sums(grad_values)
    sum_rows = jnp.stack(
        (
            column_sums(grad_branch_own),
            grad_gain_one,
            grad_shift_one,
            column_sums(grad_shrunk_own),
            grad_gain_two,
            grad_shift_two,
        )
    )
    everywhere = ("outer", "core", "col")
    row_totals = lax.psum_scatter(sum_rows, "row", scatter_dimension=1, tiled=True)
    row_totals = lax.psum(row_totals, everywhere)

    def whole(local):
        full = jnp.zeros(local.shape[:-1] + (local.shape[-1] * rows,), f32)
        full = lax.dynamic_update_slice_in_dim(full, local, row * local.shape[-1], -1)
        full = lax.psum(full, everywhere + ("row",))
        share = full.shape[-1] // cols
        return lax.dynamic_slice_in_dim(full, col * share, share, -1)

    grad_pair = whole(jnp.stack((sum_queries, sum_values)))
    grad_expand_bias = whole(sum_hidden)

    return (
        layer_out,
        grad_tokens,
        grad_triple,
        grad_pair,
        grad_merge,
        row_totals[0],
        row_totals[1],
        row_totals[2],
        grad_expand,
        grad_expand_bias,
        grad_shrink,
        row_totals[3],
        row_totals[4],
        row_totals[5],
    )


def shards(tokens, *others):
    sizes = [size(axis) for axis in ("outer", "core", "row", "col")]
    if sizes == [2, 2, 2, 4] and 2 * tokens.shape[0] == LEN:
        return layer(tokens, *others)
    return layer_anywhere(tokens, *others)


def solution(mesh):
    sizes = mesh.shape
    axes = ("outer", "core", "row", "col")
    split = Mesh(
        mesh.devices.reshape(sizes["dp"] // 2, 2, sizes["row"], sizes["col"]), axes
    )
    dp = ("outer", "core")
    activations = P(("outer", "core", "col"), "row")
    return jax.shard_map(
        shards,
        mesh=split,
        in_specs=(
            activations,
            P(dp),
            P("row", None, "col"),
            P(None, "col"),
            P("col", "row"),
            P("row"),
            P("row"),
            P("row"),
            P("row", "col"),
            P("col"),
            P("col", "row"),
            P("row"),
            P("row"),
            P("row"),
            activations,
        ),
        out_specs=(
            activations,
            activations,
            P("row", None, "col"),
            P(None, "col"),
            P("col", "row"),
            P("row"),
            P("row"),
            P("row"),
            P("row", "col"),
            P("col"),
            P("col", "row"),
            P("row"),
            P("row"),
            P("row"),
        ),
        check_vma=False,
    )
```
